32 devices in a mesh: dp: 16 (over z, y, core), mp: 2 (over x).
Axes of the slice: x: 2, y: 2, z: 4, core: 2. Of those that a mesh axis runs over, the one named last changes fastest.
Arguments:
- tokens: bfloat16 [16384, 1024], P(('dp', 'mp')), may hold values from -6 to 6
- doc_lengths: int32 [16, 6], P('dp'), may hold values from 1 to 512, 1024 in all within a row
- cotangent: bfloat16 [16384, 1024], P(('dp', 'mp')), may hold values from -6 to 6
- query_weight: bfloat16 [1024, 1024], P(None, 'mp'), may hold values from -0.1875 to 0.1875
- query_bias: bfloat16 [1024], P('mp'), may hold values from -3 to 3
- key_weight: bfloat16 [1024, 1024], P(None, 'mp'), may hold values from -0.1875 to 0.1875
- value_weight: bfloat16 [1024, 1024], P(None, 'mp'), may hold values from -0.1875 to 0.1875
- value_bias: bfloat16 [1024], P('mp'), may hold values from -3 to 3
- out_weight: bfloat16 [1024, 1024], P('mp'), may hold values from -1 to 1
- out_bias: bfloat16 [1024], replicated, may hold values from -3 to 3
- first_gain: bfloat16 [1024], replicated, may hold values from 0.5 to 1.5
- first_shift: bfloat16 [1024], replicated, may hold values from -2 to 2
- up_weight: bfloat16 [1024, 4096], P(None, 'mp'), may hold values from -0.1875 to 0.1875
- up_bias: bfloat16 [4096], P('mp'), may hold values from -3 to 3
- down_weight: bfloat16 [4096, 1024], P('mp'), may hold values from -0.09375 to 0.09375
- down_bias: bfloat16 [1024], replicated, may hold values from -3 to 3
- second_gain: bfloat16 [1024], replicated, may hold values from 0.5 to 1.5
- second_shift: bfloat16 [1024], replicated, may hold values from -2 to 2
Outputs:
- output: bfloat16 [16384, 1024], P(('dp', 'mp'))
- input_grad: float32 [16384, 1024], P(('dp', 'mp'))
- grad_query_weight: float32 [1024, 1024], P(None, 'mp')
- grad_query_bias: float32 [1024], P('mp')
- grad_key_weight: float32 [1024, 1024], P(None, 'mp')
- grad_value_weight: float32 [1024, 1024], P(None, 'mp')
- grad_value_bias: float32 [1024], P('mp')
- grad_out_weight: float32 [1024, 1024], P('mp')
- grad_out_bias: float32 [1024], replicated
- grad_first_gain: float32 [1024], replicated
- grad_first_shift: float32 [1024], replicated
- grad_up_weight: float32 [1024, 4096], P(None, 'mp')
- grad_up_bias: float32 [4096], P('mp')
- grad_down_weight: float32 [4096, 1024], P('mp')
- grad_down_bias: float32 [1024], replicated
- grad_second_gain: float32 [1024], replicated
- grad_second_shift: float32 [1024], replicated
The draws below stay inside these ranges and needn't reach their ends.
Inputs may be any that keep to these rules, and one draw needn't show every extreme that they name: `doc_lengths`: each row lists 6 - 1 document lengths and then the padding's length; a row sums to 1024, and its largest entry is 512.
All inputs are finite; a program needn't handle non-finite values.
Results may differ from the reference program's by a relative error of at most 0.023.
Values may be sent and summed in bfloat16 or wider, within the bound.
No kernel may reach another device: no remote copies, remote signals or barrier semaphores. Data moves between devices by JAX's collectives and lax.ppermute only.
A program may use at most 192 MiB of HBM per device.

```python
import math
import jax
import jax.numpy as jnp
import numpy as np
from jax import lax

D = 1024
FF = 4096
HEAD = 64
HEADS = 16
LEN = 1024
DOCS = 6
SEQS = 16
TOKENS = 16384


def block_levels(own_key, dims, split, least, top_value):
    def one(axis_at, blocks):
        draws = jax.random.uniform(jax.random.fold_in(jax.random.fold_in(own_key, 6), axis_at), (blocks,), jnp.float32, least / len(split), top_value / len(split))
        return jnp.repeat(jnp.exp(draws), dims[axis_at] // blocks).reshape((-1,) + (1,) * (len(dims) - axis_at - 1))

    loudness = one(*split[0])
    for cut in split[1:]:
        loudness = loudness * one(*cut)
    return loudness


def profile(number_of, total, most, skew):
    portions = [(1 << 20) // math.isqrt(rank ** skew) + 1 for rank in range(2, number_of + 1)]
    surplus, counts = total - most - (number_of - 1), [1] * (number_of - 1)
    while surplus > 0:
        movable = [i for i in range(number_of - 1) if counts[i] < most]
        mass, remaining = sum([portions[i] for i in movable]), surplus
        for i in movable:
            addition = min(most - counts[i], max(1, remaining * portions[i] // mass), surplus)
            counts[i] = counts[i] + addition
            surplus = surplus - addition
    return np.array([most] + counts)


def ragged(rng, number_of, total, limit, slope):
    if number_of == 2:
        one = jax.random.randint(rng, (), max(1, total - limit), min(limit, total - 1) + 1)
        return jnp.stack([one, total - one])
    sizes = jnp.asarray(profile(number_of, total, limit, slope), jnp.int32)
    pairs = (number_of - 1) // 2
    source_of, receiver = sizes[1:1 + 2 * pairs:2], sizes[2:2 + 2 * pairs:2]
    slack = jnp.minimum(source_of - 1, limit - receiver)
    moved = jax.random.randint(jax.random.fold_in(rng, 1), (pairs,), 0, 1 << 20) % (slack + 1)
    sizes = sizes.at[1:1 + 2 * pairs:2].set(source_of - moved).at[2:2 + 2 * pairs:2].set(receiver + moved)
    return sizes[jax.random.permutation(jax.random.fold_in(rng, 2), number_of)]


def bell_draw(own_key, extent, scale, most, cuts=(), kind=jnp.bfloat16):
    drawn = scale * jax.random.normal(own_key, extent, jnp.float32)
    if cuts:
        drawn = drawn * block_levels(own_key, extent, cuts, -0.22, 0.18)
    return jnp.clip(drawn, -most, most).astype(kind)


def setup_inputs(seed: int = 0) -> dict:
    key_of = jax.random.split(jax.random.key(seed), 19)
    tokens = bell_draw(key_of[0], (TOKENS, D), 1.0, 6.0, ((0, 32),))
    doc_lengths = jax.vmap(lambda own: ragged(own, DOCS, LEN, LEN // 2, 2))(jax.random.split(key_of[1], SEQS)).reshape((SEQS, DOCS)).astype(jnp.int32)
    cotangent = bell_draw(key_of[2], (TOKENS, D), 1.0, 6.0, ((0, 32),))
    query_weight = bell_draw(key_of[3], (D, D), D ** -0.5, 0.1875, ((1, 2),))
    query_bias = bell_draw(key_of[4], (D,), 0.5, 3.0, ((0, 2),))
    key_weight = bell_draw(key_of[5], (D, D), D ** -0.5, 0.1875, ((1, 2),))
    value_weight = bell_draw(key_of[6], (D, D), D ** -0.5, 0.1875, ((1, 2),))
    value_bias = bell_draw(key_of[7], (D,), 0.5, 3.0, ((0, 2),))
    out_weight = bell_draw(key_of[8], (D, D), (D // 32) ** -0.5, 1.0, ((0, 2),))
    out_bias = bell_draw(key_of[9], (D,), 0.5, 3.0)
    first_gain = jnp.clip(1.0 + 0.1 * jax.random.normal(key_of[10], (D,), jnp.float32), 0.5, 1.5).astype(jnp.bfloat16)
    first_shift = bell_draw(key_of[11], (D,), 0.3, 2.0)
    up_weight = bell_draw(key_of[12], (D, FF), D ** -0.5, 0.1875, ((1, 2),))
    up_bias = bell_draw(key_of[13], (FF,), 0.5, 3.0, ((0, 2),))
    down_weight = bell_draw(key_of[14], (FF, D), FF ** -0.5, 0.09375, ((0, 2),))
    down_bias = bell_draw(key_of[15], (D,), 0.5, 3.0)
    second_gain = jnp.clip(1.0 + 0.1 * jax.random.normal(key_of[16], (D,), jnp.float32), 0.5, 1.5).astype(jnp.bfloat16)
    second_shift = bell_draw(key_of[17], (D,), 0.3, 2.0)
    return {"tokens": tokens, "doc_lengths": doc_lengths, "cotangent": cotangent, "query_weight": query_weight, "query_bias": query_bias, "key_weight": key_weight, "value_weight": value_weight, "value_bias": value_bias, "out_weight": out_weight, "out_bias": out_bias, "first_gain": first_gain, "first_shift": first_shift, "up_weight": up_weight, "up_bias": up_bias, "down_weight": down_weight, "down_bias": down_bias, "second_gain": second_gain, "second_shift": second_shift}


@jax.custom_vjp
def low(v):
    return lax.optimization_barrier(v.astype(jnp.bfloat16)).astype(jnp.float32)

@jax.custom_vjp
def low_back(v):
    return v

def low_keep(v):
    return (low(v), None)

def low_pass(kept, grad):
    return (grad,)

def back_keep(v):
    return (v, None)

def back_low(kept, grad):
    return (low(grad),)
low.defvjp(low_keep, low_pass)
low_back.defvjp(back_keep, back_low)
epsilon = 1e-05
masked_score = -1000000000.0
highest = lax.Precision.HIGHEST

def matmul(left, right):
    return jnp.dot(left, right, preferred_element_type=jnp.float32, precision=highest)

def layer_norm(inputs, gain, shift):
    center = inputs - lax.optimization_barrier(jnp.mean(inputs, axis=-1, keepdims=True))
    spread = lax.optimization_barrier(jnp.mean(center * center, axis=-1, keepdims=True))
    return center * lax.rsqrt(spread + epsilon) * gain + shift

def segment_ids(lengths):
    ends = jnp.cumsum(lengths, axis=-1)
    places = jnp.arange(LEN, dtype=jnp.int32)
    return lax.optimization_barrier(jnp.sum((places[None, :] >= ends[:, None]).astype(jnp.int32), axis=0))

def attend_block(q_block, s_block, key_rows, values, segment):
    raw = jnp.einsum('qhd,khd->hqk', q_block, key_rows, precision=highest) * HEAD ** (-0.5)
    scores = low_back(raw)
    same = s_block[:, None] == segment[None, :]
    scores = jnp.where(same[None], scores, masked_score)
    row_max = lax.optimization_barrier(jnp.max(scores, axis=-1, keepdims=True))
    exponent = jnp.exp(scores - row_max)
    attn_probs = exponent / lax.optimization_barrier(jnp.sum(exponent, axis=-1, keepdims=True))
    return jnp.einsum('hqk,khd->qhd', low(attn_probs), values, precision=highest)

def one_sequence(params, members):
    inputs, lengths = members
    query_weight, query_bias, key_weight, value_weight, value_bias, out_weight, out_bias, first_gain, first_shift, up_weight, up_bias, down_weight, down_bias, second_gain, second_shift = params
    segment = segment_ids(lengths)
    queries = low(low_back(matmul(inputs, query_weight) + query_bias)).reshape(LEN, HEADS, HEAD)
    key_rows = low(low_back(matmul(inputs, key_weight))).reshape(LEN, HEADS, HEAD)
    values = low(low_back(matmul(inputs, value_weight) + value_bias)).reshape(LEN, HEADS, HEAD)
    block_rows = min(512, LEN)
    block_count = LEN // block_rows

    def one_block(pieces):
        return attend_block(pieces[0], pieces[1], key_rows, values, segment)
    context = lax.map(jax.checkpoint(one_block), (queries.reshape(block_count, block_rows, HEADS, HEAD), segment.reshape(block_count, block_rows)))
    context = low(low_back(context.reshape(LEN, D)))
    middle = low_back(matmul(context, out_weight)) + out_bias + inputs
    hidden = layer_norm(middle, first_gain, first_shift)
    pre = low_back(matmul(low(hidden), up_weight) + up_bias)
    act = low(jax.nn.gelu(pre, approximate=False))
    final = low_back(matmul(act, down_weight)) + down_bias + hidden
    return layer_norm(final, second_gain, second_shift)

def reference(tokens, doc_lengths, cotangent, query_weight, query_bias, key_weight, value_weight, value_bias, out_weight, out_bias, first_gain, first_shift, up_weight, up_bias, down_weight, down_bias, second_gain, second_shift):
    params = tuple((item.astype(jnp.float32) for item in (query_weight, query_bias, key_weight, value_weight, value_bias, out_weight, out_bias, first_gain, first_shift, up_weight, up_bias, down_weight, down_bias, second_gain, second_shift)))
    inputs = tokens.astype(jnp.float32).reshape(SEQS, LEN, D)

    def forward(weights, activations):
        stepper = jax.checkpoint(one_sequence)
        return lax.map(lambda members: stepper(weights, members), (activations, doc_lengths))
    output, pullback = jax.vjp(forward, params, inputs)
    segment = jax.vmap(segment_ids)(doc_lengths)
    valid_rows = (segment < DOCS - 1).astype(jnp.float32)
    upstream = cotangent.astype(jnp.float32).reshape(SEQS, LEN, D) * valid_rows[..., None]
    grads, input_grad = pullback(upstream)
    return (output.reshape(TOKENS, D).astype(jnp.bfloat16), input_grad.reshape(TOKENS, D), grads[0], grads[1], grads[2], grads[3], grads[4], grads[5], grads[6], grads[7], grads[8], grads[9], grads[10], grads[11], grads[12], grads[13], grads[14])
```

```python
import functools
import jax
import jax.numpy as jnp
from jax import lax
from jax.experimental import pallas as pl
from jax.experimental.pallas import tpu as pltpu
from jax.sharding import PartitionSpec as P

HEAD = 64
LANES = 128


epsilon = 1e-05
masked_score = -1000000000.0


def dot_nn(left, right):
    return lax.dot_general(left, right, (((1,), (0,)), ((), ())), preferred_element_type=jnp.float32)


def dot_nt(left, right):
    return lax.dot_general(left, right, (((1,), (1,)), ((), ())), preferred_element_type=jnp.float32)


def dot_tn(left, right):
    return lax.dot_general(left, right, (((0,), (0,)), ((), ())), preferred_element_type=jnp.float32)


def forward_kernel(pairs, q_ref, k_ref, v_ref, row_ref, col_ref, ctx_ref, lse_ref, bias_ref):
    bias_ref[...] = jnp.where(col_ref[...] == row_ref[...], 0.0, masked_score)
    rows = q_ref.shape[0]
    lane = lax.broadcasted_iota(jnp.int32, (rows, LANES), 1)
    stats = jnp.zeros((rows, LANES), jnp.float32)
    for pair in range(pairs):
        cols = slice(pair * LANES, (pair + 1) * LANES)
        q_pair = q_ref[:, cols] * jnp.bfloat16(HEAD ** (-0.5))
        k_pair = k_ref[:, cols]
        v_pair = v_ref[:, cols]
        halves = []
        for half in range(2):
            keep = (lane >= HEAD) == (half == 1)
            q_half = jnp.where(keep, q_pair, jnp.bfloat16(0))
            scores = dot_nt(q_half, k_pair) + bias_ref[...]
            row_max = jnp.max(scores, axis=-1, keepdims=True)
            exponent = jnp.exp(scores - row_max)
            row_sum = jnp.sum(exponent, axis=-1, keepdims=True)
            blended = dot_nn(exponent.astype(jnp.bfloat16), v_pair)
            halves.append(blended * (1.0 / row_sum))
            stats = jnp.where(lane == 2 * pair + half, row_max + jnp.log(row_sum), stats)
        ctx_ref[:, cols] = jnp.where(lane >= HEAD, halves[1], halves[0]).astype(ctx_ref.dtype)
    lse_ref[...] = jnp.transpose(stats)[: lse_ref.shape[0], :]


def attention_forward(queries, key_rows, values, segment, block=256):
    length, width = queries.shape
    pairs = width // LANES
    heads = width // HEAD
    whole = lambda shape: pl.BlockSpec(shape, lambda i: (0, 0))
    return pl.pallas_call(
        functools.partial(forward_kernel, pairs),
        grid=(length // block,),
        in_specs=[
            pl.BlockSpec((block, width), lambda i: (i, 0)),
            whole((length, width)),
            whole((length, width)),
            whole((1, length)),
            pl.BlockSpec((block, 1), lambda i: (i, 0)),
        ],
        out_specs=[
            pl.BlockSpec((block, width), lambda i: (i, 0)),
            pl.BlockSpec((heads, block), lambda i: (0, i)),
        ],
        out_shape=[
            jax.ShapeDtypeStruct((length, width), jnp.bfloat16),
            jax.ShapeDtypeStruct((heads, length), jnp.float32),
        ],
        scratch_shapes=[pltpu.VMEM((block, length), jnp.float32)],
        compiler_params=pltpu.CompilerParams(vmem_limit_bytes=48 * 1024 * 1024),
        name="attention_forward",
    )(queries, key_rows, values, segment.reshape(1, length), segment.reshape(length, 1))


def backward_kernel(
    pairs, q_ref, k_ref, v_ref, g_ref, c_ref, lse_ref, row_ref, col_ref,
    dq_ref, dk_ref, dv_ref, bias_ref, dk_sum, dv_sum,
):
    step = pl.program_id(0)
    bias_ref[...] = jnp.where(col_ref[...] == row_ref[...], 0.0, masked_score)
    rows = q_ref.shape[0]
    lane = lax.broadcasted_iota(jnp.int32, (rows, LANES), 1)
    key_lane = lax.broadcasted_iota(jnp.int32, (k_ref.shape[0], LANES), 1)
    inner = jnp.zeros((rows, LANES), jnp.float32)
    for pair in range(pairs):
        cols = slice(pair * LANES, (pair + 1) * LANES)
        both = g_ref[:, cols].astype(jnp.float32) * c_ref[:, cols].astype(jnp.float32)
        low = jnp.sum(jnp.where(lane < HEAD, both, 0.0), axis=-1, keepdims=True)
        high = jnp.sum(jnp.where(lane < HEAD, 0.0, both), axis=-1, keepdims=True)
        inner = jnp.where(lane == 2 * pair, low, jnp.where(lane == 2 * pair + 1, high, inner))
    inner = jnp.transpose(inner)

    @pl.when(step == 0)
    def _():
        dk_sum[...] = jnp.zeros_like(dk_sum)
        dv_sum[...] = jnp.zeros_like(dv_sum)

    for pair in range(pairs):
        cols = slice(pair * LANES, (pair + 1) * LANES)
        q_pair = q_ref[:, cols] * jnp.bfloat16(HEAD ** (-0.5))
        k_pair = k_ref[:, cols]
        v_pair = v_ref[:, cols]
        g_pair = g_ref[:, cols]
        dq = None
        for half in range(2):
            head = 2 * pair + half
            keep = (lane >= HEAD) == (half == 1)
            q_half = jnp.where(keep, q_pair, jnp.bfloat16(0))
            g_half = jnp.where(keep, g_pair, jnp.bfloat16(0))
            k_half = jnp.where((key_lane >= HEAD) == (half == 1), k_pair, jnp.bfloat16(0))
            probs = jnp.exp(dot_nt(k_pair, q_half) + bias_ref[...] - lse_ref[head : head + 1, :])
            d_probs = dot_nt(v_pair, g_half)
            d_scores = (probs * (d_probs - inner[head : head + 1, :])).astype(jnp.bfloat16)
            dv_sum[:, cols] += dot_nn(probs.astype(jnp.bfloat16), g_half)
            dk_sum[:, cols] += dot_nn(d_scores, q_half)
            part = dot_tn(d_scores, k_half)
            dq = part if dq is None else dq + part
        dq_ref[:, cols] = (dq * HEAD ** (-0.5)).astype(dq_ref.dtype)

    @pl.when(step == pl.num_programs(0) - 1)
    def _():
        dk_ref[...] = dk_sum[...].astype(dk_ref.dtype)
        dv_ref[...] = dv_sum[...].astype(dv_ref.dtype)


def attention_backward(queries, key_rows, values, d_context, context, lse, segment, block=256):
    length, width = queries.shape
    pairs = width // LANES
    heads = width // HEAD
    whole = lambda shape: pl.BlockSpec(shape, lambda i: (0, 0))
    part = pl.BlockSpec((block, width), lambda i: (i, 0))
    return pl.pallas_call(
        functools.partial(backward_kernel, pairs),
        grid=(length // block,),
        in_specs=[
            part,
            whole((length, width)),
            whole((length, width)),
            part,
            part,
            pl.BlockSpec((heads, block), lambda i: (0, i)),
            pl.BlockSpec((1, block), lambda i: (0, i)),
            whole((length, 1)),
        ],
        out_specs=[part, whole((length, width)), whole((length, width))],
        out_shape=[jax.ShapeDtypeStruct((length, width), jnp.bfloat16)] * 3,
        scratch_shapes=[
            pltpu.VMEM((length, block), jnp.float32),
            pltpu.VMEM((length, width), jnp.float32),
            pltpu.VMEM((length, width), jnp.float32),
        ],
        compiler_params=pltpu.CompilerParams(vmem_limit_bytes=48 * 1024 * 1024),
        name="attention_backward",
    )(queries, key_rows, values, d_context, context, lse,
      segment.reshape(1, length), segment.reshape(length, 1))


def matmul(left, right):
    return jnp.dot(left, right, preferred_element_type=jnp.float32)


def matmul_tn(left, right):
    return lax.dot_general(
        left, right, (((0,), (0,)), ((), ())), preferred_element_type=jnp.float32
    )


def matmul_nt(left, right):
    return lax.dot_general(
        left, right, (((1,), (1,)), ((), ())), preferred_element_type=jnp.float32
    )


def layer_norm(inputs, gain, shift):
    center = inputs - jnp.mean(inputs, axis=-1, keepdims=True)
    spread = jnp.mean(center * center, axis=-1, keepdims=True)
    return center * lax.rsqrt(spread + epsilon) * gain + shift


def segment_ids(lengths, length):
    ends = jnp.cumsum(lengths, axis=-1)
    places = jnp.arange(length, dtype=jnp.int32)
    return jnp.sum((places[None, None, :] >= ends[:, :, None]).astype(jnp.int32), axis=1)


def score_block(q_block, s_block, key_rows, segment):
    raw = jnp.einsum(
        "qhd,khd->hqk", q_block, key_rows, preferred_element_type=jnp.float32
    ) * HEAD ** (-0.5)
    same = s_block[:, None] == segment[None, :]
    return jnp.where(same[None], raw, masked_score)


def body_general(
    tokens,
    doc_lengths,
    cotangent,
    query_weight,
    query_bias,
    key_weight,
    value_weight,
    value_bias,
    out_weight,
    out_bias,
    first_gain,
    first_shift,
    up_weight,
    up_bias,
    down_weight,
    down_bias,
    second_gain,
    second_shift,
):
    own_rows = tokens.shape[0]
    seq_count, doc_count = doc_lengths.shape
    all_rows = own_rows * lax.axis_size("mp")
    length = all_rows // seq_count
    head_count = query_weight.shape[1] // HEAD
    block_rows = min(512, length)
    block_count = length // block_rows
    score_scale = HEAD ** (-0.5)
    first_row = lax.axis_index("mp") * own_rows
    segment = segment_ids(doc_lengths, length)
    valid_all = (segment < doc_count - 1).reshape(all_rows)
    valid_rows = lax.dynamic_slice_in_dim(valid_all, first_row, own_rows, 0)
    shape_blocks = (seq_count, block_count, block_rows, head_count, HEAD)
    shape_seqs = (seq_count, length, head_count, HEAD)
    gain_first = first_gain.astype(jnp.float32)
    shift_first = first_shift.astype(jnp.float32)
    gathered = lax.all_gather(tokens, "mp", axis=0, tiled=True)
    queries = (matmul(gathered, query_weight) + query_bias).astype(jnp.bfloat16)
    key_rows = matmul(gathered, key_weight).astype(jnp.bfloat16)
    values = (matmul(gathered, value_weight) + value_bias).astype(jnp.bfloat16)

    def attend_sequence(members):
        q_seq, k_seq, v_seq, s_seq = members

        def attend_block(pieces):
            q_block, s_block = pieces
            scores = score_block(q_block, s_block, k_seq, s_seq)
            row_max = jnp.max(scores, axis=-1, keepdims=True)
            exponent = jnp.exp(scores - row_max)
            row_sum = jnp.sum(exponent, axis=-1, keepdims=True)
            attn_probs = (exponent / row_sum).astype(jnp.bfloat16)
            blended = jnp.einsum(
                "hqk,khd->qhd", attn_probs, v_seq, preferred_element_type=jnp.float32
            )
            return (blended.astype(jnp.bfloat16), (row_max + jnp.log(row_sum))[..., 0])

        return lax.map(attend_block, (q_seq, s_seq.reshape(block_count, block_rows)))

    context, log_mass = lax.map(
        attend_sequence,
        (
            queries.reshape(shape_blocks),
            key_rows.reshape(shape_seqs),
            values.reshape(shape_seqs),
            segment,
        ),
    )
    context = context.reshape(all_rows, head_count * HEAD)
    attn_part = lax.psum_scatter(matmul(context, out_weight), "mp", scatter_dimension=0, tiled=True)
    middle = attn_part + out_bias + tokens.astype(jnp.float32)
    hidden, norm_first = jax.vjp(layer_norm, middle, gain_first, shift_first)
    hidden_rows = lax.all_gather(hidden.astype(jnp.bfloat16), "mp", axis=0, tiled=True)
    pre = matmul(hidden_rows, up_weight) + up_bias
    act_exact, gelu_back = jax.vjp(lambda inputs: jax.nn.gelu(inputs, approximate=False), pre)
    act = act_exact.astype(jnp.bfloat16)
    ffn_part = lax.psum_scatter(matmul(act, down_weight), "mp", scatter_dimension=0, tiled=True)
    final = ffn_part + down_bias + hidden
    result, norm_second = jax.vjp(
        layer_norm, final, second_gain.astype(jnp.float32), second_shift.astype(jnp.float32)
    )
    upstream = cotangent.astype(jnp.float32) * valid_rows[:, None].astype(jnp.float32)
    d_final, grad_second_gain, grad_second_shift = norm_second(upstream)
    grad_down_bias = jnp.sum(d_final, axis=0)
    final_rows = lax.all_gather(d_final.astype(jnp.bfloat16), "mp", axis=0, tiled=True)
    grad_down_weight = matmul_tn(act, final_rows)
    d_pre = gelu_back(matmul_nt(final_rows, down_weight))[0].astype(jnp.bfloat16)
    grad_up_weight = matmul_tn(hidden_rows, d_pre)
    grad_up_bias = jnp.sum(d_pre, axis=0, dtype=jnp.float32)
    d_hidden = (
        lax.psum_scatter(matmul_nt(d_pre, up_weight), "mp", scatter_dimension=0, tiled=True)
        + d_final
    )
    d_middle, grad_first_gain, grad_first_shift = norm_first(d_hidden)
    grad_out_bias = jnp.sum(d_middle, axis=0)
    middle_rows = lax.all_gather(d_middle.astype(jnp.bfloat16), "mp", axis=0, tiled=True)
    grad_out_weight = matmul_tn(context, middle_rows)
    d_context = matmul_nt(middle_rows, out_weight).astype(jnp.bfloat16)

    def back_sequence(members):
        q_seq, k_seq, v_seq, s_seq, l_seq, g_seq = members

        def back_block(carried, pieces):
            grad_keys, grad_values = carried
            q_block, s_block, l_block, g_block = pieces
            scores = score_block(q_block, s_block, k_seq, s_seq)
            attn_probs = jnp.exp(scores - l_block[..., None])
            d_probs = jnp.einsum("qhd,khd->hqk", g_block, v_seq, preferred_element_type=jnp.float32)
            row_inner = jnp.sum(attn_probs * d_probs, axis=-1, keepdims=True)
            d_scores = (attn_probs * (d_probs - row_inner)).astype(jnp.bfloat16)
            d_block = (
                jnp.einsum("hqk,khd->qhd", d_scores, k_seq, preferred_element_type=jnp.float32)
                * score_scale
            )
            grad_keys = (
                grad_keys
                + jnp.einsum("hqk,qhd->khd", d_scores, q_block, preferred_element_type=jnp.float32)
                * score_scale
            )
            grad_values = grad_values + jnp.einsum(
                "hqk,qhd->khd",
                attn_probs.astype(jnp.bfloat16),
                g_block,
                preferred_element_type=jnp.float32,
            )
            return ((grad_keys, grad_values), d_block.astype(jnp.bfloat16))

        zero_grads = jnp.zeros((length, head_count, HEAD), jnp.float32)
        (grad_keys, grad_values), d_blocks = lax.scan(
            back_block,
            (zero_grads, zero_grads),
            (q_seq, s_seq.reshape(block_count, block_rows), l_seq, g_seq),
        )
        return (d_blocks, grad_keys.astype(jnp.bfloat16), grad_values.astype(jnp.bfloat16))

    d_queries, d_keys, d_values = lax.map(
        back_sequence,
        (
            queries.reshape(shape_blocks),
            key_rows.reshape(shape_seqs),
            values.reshape(shape_seqs),
            segment,
            log_mass,
            d_context.reshape(shape_blocks),
        ),
    )
    d_queries = d_queries.reshape(all_rows, head_count * HEAD)
    d_keys = d_keys.reshape(all_rows, head_count * HEAD)
    d_values = d_values.reshape(all_rows, head_count * HEAD)
    grad_query_weight = matmul_tn(gathered, d_queries)
    grad_key_weight = matmul_tn(gathered, d_keys)
    grad_value_weight = matmul_tn(gathered, d_values)
    grad_query_bias = jnp.sum(d_queries, axis=0, dtype=jnp.float32)
    grad_value_bias = jnp.sum(d_values, axis=0, dtype=jnp.float32)
    total_grad = matmul_nt(d_queries, query_weight)
    total_grad = total_grad + matmul_nt(d_keys, key_weight)
    input_grad = (
        lax.psum_scatter(
            (total_grad + matmul_nt(d_values, value_weight)).astype(jnp.bfloat16),
            "mp",
            scatter_dimension=0,
            tiled=True,
        ).astype(jnp.float32)
        + d_middle
    )
    (
        grad_out_bias,
        grad_first_gain,
        grad_first_shift,
        grad_down_bias,
        grad_second_gain,
        grad_second_shift,
    ) = lax.psum(
        (
            grad_out_bias,
            grad_first_gain,
            grad_first_shift,
            grad_down_bias,
            grad_second_gain,
            grad_second_shift,
        ),
        ("dp", "mp"),
    )
    (
        grad_query_weight,
        grad_query_bias,
        grad_key_weight,
        grad_value_weight,
        grad_value_bias,
        grad_out_weight,
        grad_up_weight,
        grad_up_bias,
        grad_down_weight,
    ) = (
        lax.psum(grad_query_weight.astype(jnp.bfloat16), "dp").astype(jnp.float32),
        lax.psum(grad_query_bias.astype(jnp.bfloat16), "dp").astype(jnp.float32),
        lax.psum(grad_key_weight.astype(jnp.bfloat16), "dp").astype(jnp.float32),
        lax.psum(grad_value_weight.astype(jnp.bfloat16), "dp").astype(jnp.float32),
        lax.psum(grad_value_bias.astype(jnp.bfloat16), "dp").astype(jnp.float32),
        lax.psum(grad_out_weight.astype(jnp.bfloat16), "dp").astype(jnp.float32),
        lax.psum(grad_up_weight.astype(jnp.bfloat16), "dp").astype(jnp.float32),
        lax.psum(grad_up_bias.astype(jnp.bfloat16), "dp").astype(jnp.float32),
        lax.psum(grad_down_weight.astype(jnp.bfloat16), "dp").astype(jnp.float32),
    )
    return (
        result.astype(jnp.bfloat16),
        input_grad,
        grad_query_weight,
        grad_query_bias,
        grad_key_weight,
        grad_value_weight,
        grad_value_bias,
        grad_out_weight,
        grad_out_bias,
        grad_first_gain,
        grad_first_shift,
        grad_up_weight,
        grad_up_bias,
        grad_down_weight,
        grad_down_bias,
        grad_second_gain,
        grad_second_shift,
    )


def swap(rows):
    return lax.ppermute(rows, "mp", [(0, 1), (1, 0)])


def normal_parts(pre):
    size = jnp.abs(pre) * (0.5**0.5)
    t = 1.0 / (1.0 + 0.3275911 * size)
    bell = jnp.exp(-size * size)
    series = t * (
        0.254829592
        + t * (-0.284496736 + t * (1.421413741 + t * (-1.453152027 + t * 1.061405429)))
    )
    tail = 0.5 * series * bell
    return jnp.where(pre < 0, tail, 1.0 - tail), pre * bell * 0.3989422804014327


def gelu_parts(pre):
    cumulative, slope = normal_parts(pre)
    return (pre * cumulative).astype(jnp.bfloat16), (cumulative + slope).astype(jnp.bfloat16)


def norm_stats(inputs):
    center = inputs - jnp.mean(inputs, axis=-1, keepdims=True)
    spread = jnp.mean(center * center, axis=-1, keepdims=True)
    inverse = lax.rsqrt(spread + epsilon)
    return center * inverse, inverse


def norm_back(upstream, normal, inverse, gain):
    scaled = upstream * gain
    mean = jnp.mean(scaled, axis=-1, keepdims=True)
    along = jnp.mean(scaled * normal, axis=-1, keepdims=True)
    back = (scaled - mean - normal * along) * inverse
    return back, jnp.sum(upstream * normal, axis=0), jnp.sum(upstream, axis=0)


def body_pair(
    tokens,
    doc_lengths,
    cotangent,
    query_weight,
    query_bias,
    key_weight,
    value_weight,
    value_bias,
    out_weight,
    out_bias,
    first_gain,
    first_shift,
    up_weight,
    up_bias,
    down_weight,
    down_bias,
    second_gain,
    second_shift,
):
    own_rows = tokens.shape[0]
    length = 2 * own_rows
    doc_count = doc_lengths.shape[1]
    side = lax.axis_index("mp")
    first = side == 0
    f32 = jnp.float32
    bf16 = jnp.bfloat16

    def in_order(own, other):
        return jnp.concatenate([jnp.where(first, own, other), jnp.where(first, other, own)])

    def split(whole):
        own = lax.dynamic_slice_in_dim(whole, side * own_rows, own_rows, 0)
        other = lax.dynamic_slice_in_dim(whole, (1 - side) * own_rows, own_rows, 0)
        return own, other

    segment = segment_ids(doc_lengths, length)[0]
    valid_rows = lax.dynamic_slice_in_dim(segment < doc_count - 1, side * own_rows, own_rows, 0)
    gain_first = first_gain.astype(f32)
    gain_second = second_gain.astype(f32)

    gathered = in_order(tokens, swap(tokens))
    out_other = swap(out_weight)
    queries = (matmul(gathered, query_weight) + query_bias).astype(bf16)
    key_rows = matmul(gathered, key_weight).astype(bf16)
    values = (matmul(gathered, value_weight) + value_bias).astype(bf16)
    context, log_mass = attention_forward(queries, key_rows, values, segment)
    context_own, context_away = split(context)
    context_here = swap(context_away)

    middle = (
        matmul(context_own, out_weight)
        + matmul(context_here, out_other)
        + out_bias
        + tokens.astype(f32)
    )
    normal_first, inverse_first = norm_stats(middle)
    hidden = normal_first * gain_first + first_shift
    hidden_own = hidden.astype(bf16)
    hidden_other = swap(hidden_own)

    act_own, slope_own = gelu_parts(matmul(hidden_own, up_weight) + up_bias)
    act_other, slope_other = gelu_parts(matmul(hidden_other, up_weight) + up_bias)
    back = swap(matmul(act_other, down_weight).astype(bf16))
    final = matmul(act_own, down_weight) + back.astype(f32) + down_bias + hidden
    normal_second, inverse_second = norm_stats(final)
    output = (normal_second * gain_second + second_shift).astype(bf16)
    upstream = cotangent.astype(f32) * valid_rows[:, None].astype(f32)
    d_final, grad_second_gain, grad_second_shift = norm_back(
        upstream, normal_second, inverse_second, gain_second
    )
    grad_down_bias = jnp.sum(d_final, axis=0)
    final_own = d_final.astype(bf16)
    final_other = swap(final_own)
    d_pre_own = (matmul_nt(final_own, down_weight) * slope_own).astype(bf16)
    d_pre_other = (matmul_nt(final_other, down_weight) * slope_other).astype(bf16)
    back = swap(matmul_nt(d_pre_other, up_weight).astype(bf16))
    d_hidden = matmul_nt(d_pre_own, up_weight) + back.astype(f32) + d_final
    grad_down_weight = matmul_tn(act_own, final_own) + matmul_tn(act_other, final_other)
    grad_up_weight = matmul_tn(hidden_own, d_pre_own) + matmul_tn(hidden_other, d_pre_other)
    grad_up_bias = jnp.sum(d_pre_own, axis=0, dtype=f32) + jnp.sum(d_pre_other, axis=0, dtype=f32)

    d_middle, grad_first_gain, grad_first_shift = norm_back(
        d_hidden, normal_first, inverse_first, gain_first
    )
    grad_out_bias = jnp.sum(d_middle, axis=0)
    middle_own = d_middle.astype(bf16)
    d_context_away = swap(matmul_nt(middle_own, out_other).astype(bf16))
    d_context = in_order(matmul_nt(middle_own, out_weight).astype(bf16), d_context_away)
    grad_out_weight = matmul_tn(context_own, middle_own) + swap(
        matmul_tn(context_here, middle_own).astype(bf16)
    ).astype(f32)

    d_queries, d_keys, d_values = attention_backward(
        queries, key_rows, values, d_context, context, log_mass, segment
    )
    dq_own, dq_other = split(d_queries)
    dk_own, dk_other = split(d_keys)
    dv_own, dv_other = split(d_values)
    back = swap(
        (
            matmul_nt(dq_other, query_weight)
            + matmul_nt(dk_other, key_weight)
            + matmul_nt(dv_other, value_weight)
        ).astype(bf16)
    )
    input_grad = (
        matmul_nt(dq_own, query_weight)
        + matmul_nt(dk_own, key_weight)
        + matmul_nt(dv_own, value_weight)
        + back.astype(f32)
        + d_middle
    )
    grad_query_weight = matmul_tn(gathered, d_queries)
    grad_key_weight = matmul_tn(gathered, d_keys)
    grad_value_weight = matmul_tn(gathered, d_values)
    grad_query_bias = jnp.sum(d_queries, axis=0, dtype=f32)
    grad_value_bias = jnp.sum(d_values, axis=0, dtype=f32)

    shared = jnp.stack(
        [
            grad_out_bias,
            grad_first_gain,
            grad_first_shift,
            grad_down_bias,
            grad_second_gain,
            grad_second_shift,
        ]
    )
    shared = (shared + swap(shared)).astype(bf16)
    low = lambda items: tuple(item.astype(bf16) for item in items)
    grad_down_weight, grad_up_weight = lax.psum(low((grad_down_weight, grad_up_weight)), "dp")
    (
        grad_down_weight,
        grad_up_weight,
        grad_query_weight,
        grad_key_weight,
        grad_value_weight,
        grad_out_weight,
    ) = lax.optimization_barrier(
        (
            grad_down_weight,
            grad_up_weight,
            grad_query_weight,
            grad_key_weight,
            grad_value_weight,
            grad_out_weight,
        )
    )
    (
        grad_query_weight,
        grad_key_weight,
        grad_value_weight,
        grad_out_weight,
        grad_query_bias,
        grad_value_bias,
        grad_up_bias,
        shared,
    ) = lax.psum(
        low(
            (
                grad_query_weight,
                grad_key_weight,
                grad_value_weight,
                grad_out_weight,
                grad_query_bias,
                grad_value_bias,
                grad_up_bias,
                shared,
            )
        ),
        "dp",
    )
    shared = shared.astype(f32)
    return (
        output,
        input_grad,
        grad_query_weight.astype(f32),
        grad_query_bias.astype(f32),
        grad_key_weight.astype(f32),
        grad_value_weight.astype(f32),
        grad_value_bias.astype(f32),
        grad_out_weight.astype(f32),
        shared[0],
        shared[1],
        shared[2],
        grad_up_weight.astype(f32),
        grad_up_bias.astype(f32),
        grad_down_weight.astype(f32),
        shared[3],
        shared[4],
        shared[5],
    )


def solution(mesh):
    in_specs = (
        P(("dp", "mp"), None),
        P("dp", None),
        P(("dp", "mp"), None),
        P(None, "mp"),
        P("mp"),
        P(None, "mp"),
        P(None, "mp"),
        P("mp"),
        P("mp", None),
        P(),
        P(),
        P(),
        P(None, "mp"),
        P("mp"),
        P("mp", None),
        P(),
        P(),
        P(),
    )
    out_specs = (
        P(("dp", "mp"), None),
        P(("dp", "mp"), None),
        P(None, "mp"),
        P("mp"),
        P(None, "mp"),
        P(None, "mp"),
        P("mp"),
        P("mp", None),
        P(),
        P(),
        P(),
        P(None, "mp"),
        P("mp"),
        P("mp", None),
        P(),
        P(),
        P(),
    )
    body = body_pair if mesh.shape["mp"] == 2 else body_general
    return jax.shard_map(body, mesh=mesh, in_specs=in_specs, out_specs=out_specs, check_vma=False)
```

```python
import functools
import jax
import jax.numpy as jnp
from jax import lax
from jax.experimental import pallas as pl
from jax.experimental.pallas import tpu as pltpu
from jax.sharding import PartitionSpec as P

HEAD = 64
LANES = 128


epsilon = 1e-05
masked_score = -1000000000.0


def work(flops):
    return pl.CostEstimate(flops=flops, bytes_accessed=0, transcendentals=0)


def dot_nn(left, right):
    return lax.dot_general(left, right, (((1,), (0,)), ((), ())), preferred_element_type=jnp.float32)


def dot_nt(left, right):
    return lax.dot_general(left, right, (((1,), (1,)), ((), ())), preferred_element_type=jnp.float32)


def dot_tn(left, right):
    return lax.dot_general(left, right, (((0,), (0,)), ((), ())), preferred_element_type=jnp.float32)


def forward_kernel(pairs, q_ref, k_ref, v_ref, row_ref, col_ref, ctx_ref, lse_ref, bias_ref):
    bias_ref[...] = jnp.where(col_ref[...] == row_ref[...], 0.0, masked_score)
    rows = q_ref.shape[0]
    lane = lax.broadcasted_iota(jnp.int32, (rows, LANES), 1)
    stats = jnp.zeros((rows, LANES), jnp.float32)
    for pair in range(pairs):
        cols = slice(pair * LANES, (pair + 1) * LANES)
        q_pair = q_ref[:, cols] * jnp.bfloat16(HEAD ** (-0.5))
        k_pair = k_ref[:, cols]
        v_pair = v_ref[:, cols]
        halves = []
        for half in range(2):
            keep = (lane >= HEAD) == (half == 1)
            q_half = jnp.where(keep, q_pair, jnp.bfloat16(0))
            scores = dot_nt(q_half, k_pair) + bias_ref[...]
            row_max = jnp.max(scores, axis=-1, keepdims=True)
            exponent = jnp.exp(scores - row_max)
            row_sum = jnp.sum(exponent, axis=-1, keepdims=True)
            blended = dot_nn(exponent.astype(jnp.bfloat16), v_pair)
            halves.append(blended * (1.0 / row_sum))
            stats = jnp.where(lane == 2 * pair + half, row_max + jnp.log(row_sum), stats)
        ctx_ref[:, cols] = jnp.where(lane >= HEAD, halves[1], halves[0]).astype(ctx_ref.dtype)
    lse_ref[...] = jnp.transpose(stats)[: lse_ref.shape[0], :]


def attention_forward(queries, key_rows, values, row_segment, segment, block=256):
    rows, width = queries.shape
    length = key_rows.shape[0]
    pairs = width // LANES
    heads = width // HEAD
    whole = lambda shape: pl.BlockSpec(shape, lambda i: (0, 0))
    return pl.pallas_call(
        functools.partial(forward_kernel, pairs),
        grid=(rows // block,),
        in_specs=[
            pl.BlockSpec((block, width), lambda i: (i, 0)),
            whole((length, width)),
            whole((length, width)),
            whole((1, length)),
            pl.BlockSpec((block, 1), lambda i: (i, 0)),
        ],
        out_specs=[
            pl.BlockSpec((block, width), lambda i: (i, 0)),
            pl.BlockSpec((heads, block), lambda i: (0, i)),
        ],
        out_shape=[
            jax.ShapeDtypeStruct((rows, width), jnp.bfloat16),
            jax.ShapeDtypeStruct((heads, rows), jnp.float32),
        ],
        scratch_shapes=[pltpu.VMEM((block, length), jnp.float32)],
        compiler_params=pltpu.CompilerParams(vmem_limit_bytes=48 * 1024 * 1024),
        name="attention_forward",
        cost_estimate=work(2 * 8 * rows * length * width),
    )(queries, key_rows, values, segment.reshape(1, length), row_segment.reshape(rows, 1))


def backward_kernel(
    pairs, start, q_ref, k_ref, v_ref, g_ref, c_ref, lse_ref, row_ref, col_ref,
    out_q_ref, out_k_ref, out_v_ref, bias_ref, dk_sum, dv_sum,
):
    step = pl.program_id(0)
    bias_ref[...] = jnp.where(col_ref[...] == row_ref[...], 0.0, masked_score)
    rows = q_ref.shape[0]
    lane = lax.broadcasted_iota(jnp.int32, (rows, LANES), 1)
    key_lane = lax.broadcasted_iota(jnp.int32, (k_ref.shape[0], LANES), 1)
    inner = jnp.zeros((rows, LANES), jnp.float32)
    for pair in range(pairs):
        cols = slice(pair * LANES, (pair + 1) * LANES)
        both = g_ref[:, cols].astype(jnp.float32) * c_ref[:, cols].astype(jnp.float32)
        low = jnp.sum(jnp.where(lane < HEAD, both, 0.0), axis=-1, keepdims=True)
        high = jnp.sum(jnp.where(lane < HEAD, 0.0, both), axis=-1, keepdims=True)
        inner = jnp.where(lane == 2 * pair, low, jnp.where(lane == 2 * pair + 1, high, inner))
    inner = jnp.transpose(inner)

    @pl.when(step == 0)
    def _():
        dk_sum[...] = jnp.zeros_like(dk_sum)
        dv_sum[...] = jnp.zeros_like(dv_sum)

    for pair in range(pairs):
        cols = slice(pair * LANES, (pair + 1) * LANES)
        q_pair = q_ref[:, cols] * jnp.bfloat16(HEAD ** (-0.5))
        k_pair = k_ref[:, cols]
        v_pair = v_ref[:, cols]
        g_pair = g_ref[:, cols]
        dq = None
        for half in range(2):
            head = 2 * pair + half
            keep = (lane >= HEAD) == (half == 1)
            q_half = jnp.where(keep, q_pair, jnp.bfloat16(0))
            g_half = jnp.where(keep, g_pair, jnp.bfloat16(0))
            k_half = jnp.where((key_lane >= HEAD) == (half == 1), k_pair, jnp.bfloat16(0))
            mass = lse_ref[start + head : start + head + 1, :]
            probs = jnp.exp(dot_nt(k_pair, q_half) + bias_ref[...] - mass)
            d_probs = dot_nt(v_pair, g_half)
            d_scores = (probs * (d_probs - inner[head : head + 1, :])).astype(jnp.bfloat16)
            dv_sum[:, cols] += dot_nn(probs.astype(jnp.bfloat16), g_half)
            dk_sum[:, cols] += dot_nn(d_scores, q_half)
            part = dot_tn(d_scores, k_half)
            dq = part if dq is None else dq + part
        out_q_ref[:, cols] = (dq * HEAD ** (-0.5)).astype(out_q_ref.dtype)

    @pl.when(step == pl.num_programs(0) - 1)
    def _():
        out_k_ref[...] = dk_sum[...].astype(out_k_ref.dtype)
        out_v_ref[...] = dv_sum[...].astype(out_v_ref.dtype)


def attention_backward(
    queries, key_rows, values, d_context, context, lse, segment, at, of, block=256
):
    rows, width = queries.shape
    length = key_rows.shape[0]
    width = width // of
    pairs = width // LANES
    heads = lse.shape[0]
    part = pl.BlockSpec((block, width), lambda i: (i, at))
    keys = pl.BlockSpec((length, width), lambda i: (0, at))
    whole = pl.BlockSpec((length, width), lambda i: (0, 0))
    return pl.pallas_call(
        functools.partial(backward_kernel, pairs, at * (heads // of)),
        grid=(rows // block,),
        in_specs=[
            part, keys, keys, part, part,
            pl.BlockSpec((heads, block), lambda i: (0, i)),
            pl.BlockSpec((1, block), lambda i: (0, i)),
            pl.BlockSpec((length, 1), lambda i: (0, 0)),
        ],
        out_specs=[pl.BlockSpec((block, width), lambda i: (i, 0)), whole, whole],
        out_shape=[jax.ShapeDtypeStruct((rows, width), jnp.bfloat16)]
        + [jax.ShapeDtypeStruct((length, width), jnp.bfloat16)] * 2,
        scratch_shapes=[
            pltpu.VMEM((length, block), jnp.float32),
            pltpu.VMEM((length, width), jnp.float32),
            pltpu.VMEM((length, width), jnp.float32),
        ],
        compiler_params=pltpu.CompilerParams(vmem_limit_bytes=48 * 1024 * 1024),
        name="attention_backward",
        cost_estimate=work(2 * 4 * rows * length * width),
    )(queries, key_rows, values, d_context, context, lse,
      segment.reshape(1, rows), segment.reshape(length, 1))


def matmul(left, right):
    return jnp.dot(left, right, preferred_element_type=jnp.float32)


def matmul_tn(left, right):
    return lax.dot_general(
        left, right, (((0,), (0,)), ((), ())), preferred_element_type=jnp.float32
    )


def matmul_nt(left, right):
    return lax.dot_general(
        left, right, (((1,), (1,)), ((), ())), preferred_element_type=jnp.float32
    )


def layer_norm(inputs, gain, shift):
    center = inputs - jnp.mean(inputs, axis=-1, keepdims=True)
    spread = jnp.mean(center * center, axis=-1, keepdims=True)
    return center * lax.rsqrt(spread + epsilon) * gain + shift


def segment_ids(lengths, length):
    ends = jnp.cumsum(lengths, axis=-1)
    places = jnp.arange(length, dtype=jnp.int32)
    return jnp.sum((places[None, None, :] >= ends[:, :, None]).astype(jnp.int32), axis=1)


def score_block(q_block, s_block, key_rows, segment):
    raw = jnp.einsum(
        "qhd,khd->hqk", q_block, key_rows, preferred_element_type=jnp.float32
    ) * HEAD ** (-0.5)
    same = s_block[:, None] == segment[None, :]
    return jnp.where(same[None], raw, masked_score)


def body_general(
    tokens,
    doc_lengths,
    cotangent,
    query_weight,
    query_bias,
    key_weight,
    value_weight,
    value_bias,
    out_weight,
    out_bias,
    first_gain,
    first_shift,
    up_weight,
    up_bias,
    down_weight,
    down_bias,
    second_gain,
    second_shift,
):
    own_rows = tokens.shape[0]
    seq_count, doc_count = doc_lengths.shape
    all_rows = own_rows * lax.axis_size("mp")
    length = all_rows // seq_count
    head_count = query_weight.shape[1] // HEAD
    block_rows = min(512, length)
    block_count = length // block_rows
    score_scale = HEAD ** (-0.5)
    first_row = lax.axis_index("mp") * own_rows
    segment = segment_ids(doc_lengths, length)
    valid_all = (segment < doc_count - 1).reshape(all_rows)
    valid_rows = lax.dynamic_slice_in_dim(valid_all, first_row, own_rows, 0)
    shape_blocks = (seq_count, block_count, block_rows, head_count, HEAD)
    shape_seqs = (seq_count, length, head_count, HEAD)
    gain_first = first_gain.astype(jnp.float32)
    shift_first = first_shift.astype(jnp.float32)
    gathered = lax.all_gather(tokens, "mp", axis=0, tiled=True)
    queries = (matmul(gathered, query_weight) + query_bias).astype(jnp.bfloat16)
    key_rows = matmul(gathered, key_weight).astype(jnp.bfloat16)
    values = (matmul(gathered, value_weight) + value_bias).astype(jnp.bfloat16)

    def attend_sequence(members):
        q_seq, k_seq, v_seq, s_seq = members

        def attend_block(pieces):
            q_block, s_block = pieces
            scores = score_block(q_block, s_block, k_seq, s_seq)
            row_max = jnp.max(scores, axis=-1, keepdims=True)
            exponent = jnp.exp(scores - row_max)
            row_sum = jnp.sum(exponent, axis=-1, keepdims=True)
            attn_probs = (exponent / row_sum).astype(jnp.bfloat16)
            blended = jnp.einsum(
                "hqk,khd->qhd", attn_probs, v_seq, preferred_element_type=jnp.float32
            )
            return (blended.astype(jnp.bfloat16), (row_max + jnp.log(row_sum))[..., 0])

        return lax.map(attend_block, (q_seq, s_seq.reshape(block_count, block_rows)))

    context, log_mass = lax.map(
        attend_sequence,
        (
            queries.reshape(shape_blocks),
            key_rows.reshape(shape_seqs),
            values.reshape(shape_seqs),
            segment,
        ),
    )
    context = context.reshape(all_rows, head_count * HEAD)
    attn_part = lax.psum_scatter(matmul(context, out_weight), "mp", scatter_dimension=0, tiled=True)
    middle = attn_part + out_bias + tokens.astype(jnp.float32)
    hidden, norm_first = jax.vjp(layer_norm, middle, gain_first, shift_first)
    hidden_rows = lax.all_gather(hidden.astype(jnp.bfloat16), "mp", axis=0, tiled=True)
    pre = matmul(hidden_rows, up_weight) + up_bias
    act_exact, gelu_back = jax.vjp(lambda inputs: jax.nn.gelu(inputs, approximate=False), pre)
    act = act_exact.astype(jnp.bfloat16)
    ffn_part = lax.psum_scatter(matmul(act, down_weight), "mp", scatter_dimension=0, tiled=True)
    final = ffn_part + down_bias + hidden
    result, norm_second = jax.vjp(
        layer_norm, final, second_gain.astype(jnp.float32), second_shift.astype(jnp.float32)
    )
    upstream = cotangent.astype(jnp.float32) * valid_rows[:, None].astype(jnp.float32)
    d_final, grad_second_gain, grad_second_shift = norm_second(upstream)
    grad_down_bias = jnp.sum(d_final, axis=0)
    final_rows = lax.all_gather(d_final.astype(jnp.bfloat16), "mp", axis=0, tiled=True)
    grad_down_weight = matmul_tn(act, final_rows)
    d_pre = gelu_back(matmul_nt(final_rows, down_weight))[0].astype(jnp.bfloat16)
    grad_up_weight = matmul_tn(hidden_rows, d_pre)
    grad_up_bias = jnp.sum(d_pre, axis=0, dtype=jnp.float32)
    d_hidden = (
        lax.psum_scatter(matmul_nt(d_pre, up_weight), "mp", scatter_dimension=0, tiled=True)
        + d_final
    )
    d_middle, grad_first_gain, grad_first_shift = norm_first(d_hidden)
    grad_out_bias = jnp.sum(d_middle, axis=0)
    middle_rows = lax.all_gather(d_middle.astype(jnp.bfloat16), "mp", axis=0, tiled=True)
    grad_out_weight = matmul_tn(context, middle_rows)
    d_context = matmul_nt(middle_rows, out_weight).astype(jnp.bfloat16)

    def back_sequence(members):
        q_seq, k_seq, v_seq, s_seq, l_seq, g_seq = members

        def back_block(carried, pieces):
            grad_keys, grad_values = carried
            q_block, s_block, l_block, g_block = pieces
            scores = score_block(q_block, s_block, k_seq, s_seq)
            attn_probs = jnp.exp(scores - l_block[..., None])
            d_probs = jnp.einsum("qhd,khd->hqk", g_block, v_seq, preferred_element_type=jnp.float32)
            row_inner = jnp.sum(attn_probs * d_probs, axis=-1, keepdims=True)
            d_scores = (attn_probs * (d_probs - row_inner)).astype(jnp.bfloat16)
            d_block = (
                jnp.einsum("hqk,khd->qhd", d_scores, k_seq, preferred_element_type=jnp.float32)
                * score_scale
            )
            grad_keys = (
                grad_keys
                + jnp.einsum("hqk,qhd->khd", d_scores, q_block, preferred_element_type=jnp.float32)
                * score_scale
            )
            grad_values = grad_values + jnp.einsum(
                "hqk,qhd->khd",
                attn_probs.astype(jnp.bfloat16),
                g_block,
                preferred_element_type=jnp.float32,
            )
            return ((grad_keys, grad_values), d_block.astype(jnp.bfloat16))

        zero_grads = jnp.zeros((length, head_count, HEAD), jnp.float32)
        (grad_keys, grad_values), d_blocks = lax.scan(
            back_block,
            (zero_grads, zero_grads),
            (q_seq, s_seq.reshape(block_count, block_rows), l_seq, g_seq),
        )
        return (d_blocks, grad_keys.astype(jnp.bfloat16), grad_values.astype(jnp.bfloat16))

    d_queries, d_keys, d_values = lax.map(
        back_sequence,
        (
            queries.reshape(shape_blocks),
            key_rows.reshape(shape_seqs),
            values.reshape(shape_seqs),
            segment,
            log_mass,
            d_context.reshape(shape_blocks),
        ),
    )
    d_queries = d_queries.reshape(all_rows, head_count * HEAD)
    d_keys = d_keys.reshape(all_rows, head_count * HEAD)
    d_values = d_values.reshape(all_rows, head_count * HEAD)
    grad_query_weight = matmul_tn(gathered, d_queries)
    grad_key_weight = matmul_tn(gathered, d_keys)
    grad_value_weight = matmul_tn(gathered, d_values)
    grad_query_bias = jnp.sum(d_queries, axis=0, dtype=jnp.float32)
    grad_value_bias = jnp.sum(d_values, axis=0, dtype=jnp.float32)
    total_grad = matmul_nt(d_queries, query_weight)
    total_grad = total_grad + matmul_nt(d_keys, key_weight)
    input_grad = (
        lax.psum_scatter(
            (total_grad + matmul_nt(d_values, value_weight)).astype(jnp.bfloat16),
            "mp",
            scatter_dimension=0,
            tiled=True,
        ).astype(jnp.float32)
        + d_middle
    )
    (
        grad_out_bias,
        grad_first_gain,
        grad_first_shift,
        grad_down_bias,
        grad_second_gain,
        grad_second_shift,
    ) = lax.psum(
        (
            grad_out_bias,
            grad_first_gain,
            grad_first_shift,
            grad_down_bias,
            grad_second_gain,
            grad_second_shift,
        ),
        ("dp", "mp"),
    )
    (
        grad_query_weight,
        grad_query_bias,
        grad_key_weight,
        grad_value_weight,
        grad_value_bias,
        grad_out_weight,
        grad_up_weight,
        grad_up_bias,
        grad_down_weight,
    ) = (
        lax.psum(grad_query_weight.astype(jnp.bfloat16), "dp").astype(jnp.float32),
        lax.psum(grad_query_bias.astype(jnp.bfloat16), "dp").astype(jnp.float32),
        lax.psum(grad_key_weight.astype(jnp.bfloat16), "dp").astype(jnp.float32),
        lax.psum(grad_value_weight.astype(jnp.bfloat16), "dp").astype(jnp.float32),
        lax.psum(grad_value_bias.astype(jnp.bfloat16), "dp").astype(jnp.float32),
        lax.psum(grad_out_weight.astype(jnp.bfloat16), "dp").astype(jnp.float32),
        lax.psum(grad_up_weight.astype(jnp.bfloat16), "dp").astype(jnp.float32),
        lax.psum(grad_up_bias.astype(jnp.bfloat16), "dp").astype(jnp.float32),
        lax.psum(grad_down_weight.astype(jnp.bfloat16), "dp").astype(jnp.float32),
    )
    return (
        result.astype(jnp.bfloat16),
        input_grad,
        grad_query_weight,
        grad_query_bias,
        grad_key_weight,
        grad_value_weight,
        grad_value_bias,
        grad_out_weight,
        grad_out_bias,
        grad_first_gain,
        grad_first_shift,
        grad_up_weight,
        grad_up_bias,
        grad_down_weight,
        grad_down_bias,
        grad_second_gain,
        grad_second_shift,
    )


def swap(rows):
    return lax.ppermute(rows, "mp", [(0, 1), (1, 0)])


def normal_parts(pre):
    size = jnp.abs(pre) * (0.5**0.5)
    t = 1.0 / (1.0 + 0.3275911 * size)
    bell = jnp.exp(-size * size)
    series = t * (
        0.254829592
        + t * (-0.284496736 + t * (1.421413741 + t * (-1.453152027 + t * 1.061405429)))
    )
    tail = 0.5 * series * bell
    return jnp.where(pre < 0, tail, 1.0 - tail), pre * bell * 0.3989422804014327


def gelu_parts(pre):
    cumulative, slope = normal_parts(pre)
    return (pre * cumulative).astype(jnp.bfloat16), (cumulative + slope).astype(jnp.bfloat16)


def mean_of(rows):
    return jnp.mean(rows, axis=-1, keepdims=True)


def column_sums(rows):
    return jnp.sum(rows, axis=0, keepdims=True)


def pack_kernel(place_ref, up_ref, down_ref, out_ref):
    rows = up_ref.shape[0]
    half = down_ref.shape[2]
    out_ref[:rows, :] = up_ref[...]
    out_ref[rows:, :half] = down_ref[0]
    out_ref[rows:, half:] = down_ref[1]


def pack_weights(place, count, up_weight, down_weight):
    depth, units = up_weight.shape
    rows = depth // count
    return pl.pallas_call(
        pack_kernel,
        grid_spec=pltpu.PrefetchScalarGridSpec(
            num_scalar_prefetch=1,
            grid=(1,),
            in_specs=[
                pl.BlockSpec((rows, units), lambda i, at: (at[0], 0)),
                pl.BlockSpec((2, rows, depth), lambda i, at: (0, at[0], 0)),
            ],
            out_specs=pl.BlockSpec((2 * rows, units), lambda i, at: (0, 0)),
        ),
        out_shape=jax.ShapeDtypeStruct((2 * rows, units), up_weight.dtype),
        name="pack_weights",
        cost_estimate=work(rows * units * 4096),
    )(place, up_weight, down_weight.reshape(2, units // 2, depth))


BIG = 56 * 1024 * 1024


def middle_kernel(own_ref, here_ref, w_own_ref, w_other_ref, bias_ref, tokens_ref, gain_ref,
                  shift_ref, hidden_ref, low_ref, normal_ref, inverse_ref):
    middle = (
        dot_nn(own_ref[...], w_own_ref[...])
        + dot_nn(here_ref[...], w_other_ref[...])
        + bias_ref[...]
        + tokens_ref[...].astype(jnp.float32)
    )
    center = middle - mean_of(middle)
    inverse = lax.rsqrt(mean_of(center * center) + epsilon)
    normal = center * inverse
    hidden = normal * gain_ref[...] + shift_ref[...]
    hidden_ref[...] = hidden
    low_ref[...] = hidden.astype(jnp.bfloat16)
    normal_ref[...] = normal
    inverse_ref[...] = inverse


def middle_norm(context_own, context_here, out_weight, out_other, bias, tokens, gain, shift,
                block=256):
    rows, depth = tokens.shape
    heads = context_own.shape[1]
    part = lambda width: pl.BlockSpec((block, width), lambda i: (i, 0))
    whole = lambda shape: pl.BlockSpec(shape, lambda i: (0, 0))
    return pl.pallas_call(
        middle_kernel,
        grid=(rows // block,),
        in_specs=[part(heads), part(heads), whole((heads, depth)), whole((heads, depth)),
                  whole((1, depth)), part(depth), whole((1, depth)), whole((1, depth))],
        out_specs=[part(depth), part(depth), part(depth), part(1)],
        out_shape=[
            jax.ShapeDtypeStruct((rows, depth), jnp.float32),
            jax.ShapeDtypeStruct((rows, depth), jnp.bfloat16),
            jax.ShapeDtypeStruct((rows, depth), jnp.float32),
            jax.ShapeDtypeStruct((rows, 1), jnp.float32),
        ],
        compiler_params=pltpu.CompilerParams(vmem_limit_bytes=BIG),
        name="middle_norm",
        cost_estimate=work(8 * rows * depth * heads),
    )(context_own, context_here, out_weight, out_other, bias, tokens, gain, shift)


UNITS = 512
PIECE = 512
STRIP = 64


def gelu_block(h_ref, up, bias_ref, act_ref, slope_ref, pre_scr):
    pre_scr[...] = dot_nn(h_ref[...], up)
    bias = bias_ref[...]
    for at in range(0, pre_scr.shape[0], STRIP):
        rows = slice(at, at + STRIP)
        act, slope = gelu_parts(pre_scr[rows, :] + bias)
        act_ref[rows, :] = act
        slope_ref[rows, :] = slope


def forward_own_kernel(h_ref, up_ref, bias_ref, down_ref, act_ref, slope_ref, base_ref, pre_scr):
    step = pl.program_id(0)

    @pl.when(step == 0)
    def _():
        base_ref[...] = jnp.zeros_like(base_ref)

    gelu_block(h_ref, up_ref[...], bias_ref, act_ref, slope_ref, pre_scr)
    base_ref[...] += dot_nn(act_ref[...], down_ref[...])


def forward_own(hidden, up_weight, up_bias, down_weight):
    rows, depth = hidden.shape
    units = up_weight.shape[1]
    return pl.pallas_call(
        forward_own_kernel,
        grid=(units // UNITS,),
        in_specs=[
            pl.BlockSpec((rows, depth), lambda j: (0, 0)),
            pl.BlockSpec((depth, UNITS), lambda j: (0, j)),
            pl.BlockSpec((1, UNITS), lambda j: (0, j)),
            pl.BlockSpec((UNITS, depth), lambda j: (j, 0)),
        ],
        out_specs=[
            pl.BlockSpec((rows, UNITS), lambda j: (0, j)),
            pl.BlockSpec((rows, UNITS), lambda j: (0, j)),
            pl.BlockSpec((rows, depth), lambda j: (0, 0)),
        ],
        out_shape=[
            jax.ShapeDtypeStruct((rows, units), jnp.bfloat16),
            jax.ShapeDtypeStruct((rows, units), jnp.bfloat16),
            jax.ShapeDtypeStruct((rows, depth), jnp.float32),
        ],
        scratch_shapes=[pltpu.VMEM((rows, UNITS), jnp.float32)],
        compiler_params=pltpu.CompilerParams(vmem_limit_bytes=BIG),
        name="forward_own",
        cost_estimate=work(6 * rows * depth * units),
    )(hidden, up_weight, up_bias, down_weight)


def packed_specs(packs, at):
    count, _, features, _ = packs.shape
    groups = UNITS // features
    split = count // groups
    depth = count * features
    up = pl.BlockSpec((count, 1, features, UNITS), lambda j: (0, 0, 0, at(j)))
    down = pl.BlockSpec(
        (groups, 1, features, depth), lambda j: (at(j) % split, 1, 0, at(j) // split)
    )
    return up, down


def flat(ref):
    count, _, features, width = ref.shape
    return ref[...].reshape(count * features, width)


def forward_other_kernel(h_ref, up_ref, bias_ref, down_ref, base_ref, hidden_ref, down_bias_ref,
                         outer_ref, valid_ref, gain_ref, shift_ref,
                         slope_ref, out_ref, d_ref, low_ref, sums_ref, total, act_scr, pre_scr):
    step = pl.program_id(0)

    @pl.when(step == 0)
    def _():
        total[...] = base_ref[...]

    gelu_block(h_ref, flat(up_ref), bias_ref, act_scr, slope_ref, pre_scr)
    total[...] += dot_nn(act_scr[...], flat(down_ref))

    @pl.when(step == pl.num_programs(0) - 1)
    def _():
        gain = gain_ref[...]
        for_gain = for_shift = for_bias = 0.0
        for at in range(0, h_ref.shape[0], PIECE):
            rows = slice(at, at + PIECE)
            final = total[rows, :] + down_bias_ref[...] + hidden_ref[rows, :]
            center = final - mean_of(final)
            inverse = lax.rsqrt(mean_of(center * center) + epsilon)
            normal = center * inverse
            out_ref[rows, :] = (normal * gain + shift_ref[...]).astype(jnp.bfloat16)
            upstream = outer_ref[rows, :].astype(jnp.float32) * valid_ref[rows, :]
            scaled = upstream * gain
            back = (scaled - mean_of(scaled) - normal * mean_of(scaled * normal)) * inverse
            d_ref[rows, :] = back
            low_ref[rows, :] = back.astype(jnp.bfloat16)
            for_gain += column_sums(upstream * normal)
            for_shift += column_sums(upstream)
            for_bias += column_sums(back)
        sums_ref[...] = jnp.zeros_like(sums_ref)
        sums_ref[0:1, :] = for_gain
        sums_ref[1:2, :] = for_shift
        sums_ref[2:3, :] = for_bias


def forward_other(hidden_low, packs, bias, base, hidden, down_bias, outer, valid, gain, shift):
    rows, depth = hidden_low.shape
    units = packs.shape[3]
    up, down = packed_specs(packs, lambda j: j)
    whole = lambda shape: pl.BlockSpec(shape, lambda j: (0, 0))
    return pl.pallas_call(
        forward_other_kernel,
        grid=(units // UNITS,),
        in_specs=[
            whole((rows, depth)), up, pl.BlockSpec((1, UNITS), lambda j: (0, j)), down,
            whole((rows, depth)), whole((rows, depth)), whole((1, depth)), whole((rows, depth)),
            whole((rows, 1)), whole((1, depth)), whole((1, depth)),
        ],
        out_specs=[
            pl.BlockSpec((rows, UNITS), lambda j: (0, j)),
            whole((rows, depth)), whole((rows, depth)), whole((rows, depth)), whole((8, depth)),
        ],
        out_shape=[
            jax.ShapeDtypeStruct((rows, units), jnp.bfloat16),
            jax.ShapeDtypeStruct((rows, depth), jnp.bfloat16),
            jax.ShapeDtypeStruct((rows, depth), jnp.float32),
            jax.ShapeDtypeStruct((rows, depth), jnp.bfloat16),
            jax.ShapeDtypeStruct((8, depth), jnp.float32),
        ],
        scratch_shapes=[
            pltpu.VMEM((rows, depth), jnp.float32), pltpu.VMEM((rows, UNITS), jnp.bfloat16),
            pltpu.VMEM((rows, UNITS), jnp.float32),
        ],
        compiler_params=pltpu.CompilerParams(vmem_limit_bytes=BIG),
        name="forward_other",
        cost_estimate=work(8 * rows * depth * units),
    )(hidden_low, packs, bias, packs, base, hidden, down_bias, outer, valid, gain, shift)


def backward_rows_kernel(half, f_ref, slope_own_ref, slope_other_ref, up_ref, down_ref,
                         up_pack_ref, down_pack_ref, d_ref, normal_ref, inverse_ref, gain_ref,
                         d_pre_ref, middle_ref, low_ref, sums_ref, total):
    step = pl.program_id(0)

    def block(up, down, slope_ref, keep):
        for at in range(0, f_ref.shape[0], PIECE):
            rows = slice(at, at + PIECE)
            d_pre = (dot_nt(f_ref[rows, :], down) * slope_ref[rows, :]).astype(jnp.bfloat16)
            if keep:
                d_pre_ref[rows, :] = d_pre
            total[rows, :] += dot_nt(d_pre, up)

    @pl.when(step == 0)
    def _():
        total[...] = d_ref[...]

    @pl.when(step < half)
    def _():
        block(up_ref[...], down_ref[...], slope_own_ref, True)

    @pl.when(step >= half)
    def _():
        block(flat(up_pack_ref), flat(down_pack_ref), slope_other_ref, False)

    @pl.when(step == pl.num_programs(0) - 1)
    def _():
        gain = gain_ref[...]
        for_gain = for_shift = for_bias = 0.0
        for at in range(0, f_ref.shape[0], PIECE):
            rows = slice(at, at + PIECE)
            upstream = total[rows, :]
            normal = normal_ref[rows, :]
            scaled = upstream * gain
            back = (
                scaled - mean_of(scaled) - normal * mean_of(scaled * normal)
            ) * inverse_ref[rows, :]
            middle_ref[rows, :] = back
            low_ref[rows, :] = back.astype(jnp.bfloat16)
            for_gain += column_sums(upstream * normal)
            for_shift += column_sums(upstream)
            for_bias += column_sums(back)
        sums_ref[...] = jnp.zeros_like(sums_ref)
        sums_ref[0:1, :] = for_gain
        sums_ref[1:2, :] = for_shift
        sums_ref[2:3, :] = for_bias


def backward_rows(final_low, slope_own, slope_other, up_weight, down_weight, packs, d_final,
                  normal, inverse, gain):
    rows, depth = final_low.shape
    units = up_weight.shape[1]
    half = units // UNITS
    own = lambda j: jnp.minimum(j, half - 1)
    other = lambda j: jnp.maximum(j - half, 0)
    up, down = packed_specs(packs, other)
    whole = lambda shape: pl.BlockSpec(shape, lambda j: (0, 0))
    return pl.pallas_call(
        functools.partial(backward_rows_kernel, half),
        grid=(2 * half,),
        in_specs=[
            whole((rows, depth)),
            pl.BlockSpec((rows, UNITS), lambda j: (0, own(j))),
            pl.BlockSpec((rows, UNITS), lambda j: (0, other(j))),
            pl.BlockSpec((depth, UNITS), lambda j: (0, own(j))),
            pl.BlockSpec((UNITS, depth), lambda j: (own(j), 0)),
            up, down,
            whole((rows, depth)), whole((rows, depth)), whole((rows, 1)), whole((1, depth)),
        ],
        out_specs=[
            pl.BlockSpec((rows, UNITS), lambda j: (0, own(j))),
            whole((rows, depth)), whole((rows, depth)), whole((8, depth)),
        ],
        out_shape=[
            jax.ShapeDtypeStruct((rows, units), jnp.bfloat16),
            jax.ShapeDtypeStruct((rows, depth), jnp.float32),
            jax.ShapeDtypeStruct((rows, depth), jnp.bfloat16),
            jax.ShapeDtypeStruct((8, depth), jnp.float32),
        ],
        scratch_shapes=[pltpu.VMEM((rows, depth), jnp.float32)],
        compiler_params=pltpu.CompilerParams(vmem_limit_bytes=BIG),
        name="backward_rows",
        cost_estimate=work(10 * rows * depth * units),
    )(final_low, slope_own, slope_other, up_weight, down_weight, packs, packs, d_final, normal,
      inverse, gain)


def down_grad_kernel(h_ref, up_ref, bias_ref, act_ref, f_own_ref, f_other_ref,
                     slope_ref, grad_ref, act_scr, pre_scr):
    gelu_block(h_ref, up_ref[...], bias_ref, act_scr, slope_ref, pre_scr)
    grad_ref[...] = (
        dot_tn(act_ref[...], f_own_ref[...]) + dot_tn(act_scr[...], f_other_ref[...])
    ).astype(jnp.bfloat16)


def down_grad(hidden_other, up_weight, up_bias, act_own, final_own, final_other):
    rows, depth = hidden_other.shape
    units = up_weight.shape[1]
    whole = lambda shape: pl.BlockSpec(shape, lambda j: (0, 0))
    return pl.pallas_call(
        down_grad_kernel,
        grid=(units // UNITS,),
        in_specs=[
            whole((rows, depth)),
            pl.BlockSpec((depth, UNITS), lambda j: (0, j)),
            pl.BlockSpec((1, UNITS), lambda j: (0, j)),
            pl.BlockSpec((rows, UNITS), lambda j: (0, j)),
            whole((rows, depth)), whole((rows, depth)),
        ],
        out_specs=[
            pl.BlockSpec((rows, UNITS), lambda j: (0, j)),
            pl.BlockSpec((UNITS, depth), lambda j: (j, 0)),
        ],
        out_shape=[
            jax.ShapeDtypeStruct((rows, units), jnp.bfloat16),
            jax.ShapeDtypeStruct((units, depth), jnp.bfloat16),
        ],
        scratch_shapes=[pltpu.VMEM((rows, UNITS), jnp.bfloat16), pltpu.VMEM((rows, UNITS), jnp.float32)],
        compiler_params=pltpu.CompilerParams(vmem_limit_bytes=BIG),
        name="down_grad",
        cost_estimate=work(8 * rows * depth * units),
    )(hidden_other, up_weight, up_bias, act_own, final_own, final_other)


def up_grad_kernel(f_ref, down_ref, slope_ref, d_pre_ref, h_own_ref, h_other_ref,
                   grad_ref, sums_ref, d_scr):
    for at in range(0, f_ref.shape[0], PIECE):
        rows = slice(at, at + PIECE)
        d_scr[rows, :] = (
            dot_nt(f_ref[rows, :], down_ref[...]) * slope_ref[rows, :]
        ).astype(jnp.bfloat16)
    grad_ref[...] = (
        dot_tn(h_own_ref[...], d_pre_ref[...]) + dot_tn(h_other_ref[...], d_scr[...])
    ).astype(jnp.bfloat16)
    sums_ref[...] = column_sums(d_pre_ref[...].astype(jnp.float32)) + column_sums(
        d_scr[...].astype(jnp.float32)
    )


def up_grad(final_other, down_weight, slope_other, d_pre_own, hidden_own, hidden_other):
    rows, depth = hidden_own.shape
    units = down_weight.shape[0]
    whole = lambda shape: pl.BlockSpec(shape, lambda j: (0, 0))
    part = pl.BlockSpec((rows, UNITS), lambda j: (0, j))
    return pl.pallas_call(
        up_grad_kernel,
        grid=(units // UNITS,),
        in_specs=[
            whole((rows, depth)),
            pl.BlockSpec((UNITS, depth), lambda j: (j, 0)),
            part, part,
            whole((rows, depth)), whole((rows, depth)),
        ],
        out_specs=[
            pl.BlockSpec((depth, UNITS), lambda j: (0, j)),
            pl.BlockSpec((1, UNITS), lambda j: (0, j)),
        ],
        out_shape=[
            jax.ShapeDtypeStruct((depth, units), jnp.bfloat16),
            jax.ShapeDtypeStruct((1, units), jnp.float32),
        ],
        scratch_shapes=[pltpu.VMEM((rows, UNITS), jnp.bfloat16)],
        compiler_params=pltpu.CompilerParams(vmem_limit_bytes=BIG),
        name="up_grad",
        cost_estimate=work(6 * rows * depth * units),
    )(final_other, down_weight, slope_other, d_pre_own, hidden_own, hidden_other)


def after(value, *earlier):
    return lax.optimization_barrier((value,) + earlier)[0]


def join_halves(kept, arrived):
    return (kept.astype(jnp.float32) + arrived.astype(jnp.float32)).astype(jnp.bfloat16)


class Chain:
    def __init__(self, item, swapped=False):
        self.count = lax.axis_size("dp")
        bits = list(range(self.count.bit_length() - 1))
        if swapped:
            bits[1:3] = bits[1:3][::-1]
        self.steps = [("fold", bit) for bit in bits] + [("spread", bit) for bit in reversed(bits)]
        self.held = item.astype(jnp.bfloat16)
        self.flying = None

    def end(self, *earlier):
        if self.flying is not None:
            kind, bit, kept, arrived = self.flying
            self.flying = None
            if earlier:
                arrived = after(arrived, *earlier)
            if kind == "fold":
                self.held = join_halves(kept, arrived)
            else:
                low = (lax.axis_index("dp") >> bit) & 1 == 0
                self.held = jnp.concatenate(
                    [jnp.where(low, kept, arrived), jnp.where(low, arrived, kept)]
                )

    def push(self, *earlier):
        self.end(*earlier)
        if self.steps:
            kind, bit = self.steps.pop(0)
            perm = [(at, at ^ (1 << bit)) for at in range(self.count)]
            kept = sent = self.held
            if kind == "fold":
                rows = self.held.shape[0] // 2
                place = (lax.axis_index("dp") >> bit) & 1
                kept = lax.dynamic_slice_in_dim(self.held, place * rows, rows, 0)
                sent = lax.dynamic_slice_in_dim(self.held, (1 - place) * rows, rows, 0)
            self.flying = kind, bit, kept, lax.ppermute(sent, "dp", perm)
        return self

    def gate(self, value):
        return after(value, self.held)

    def done(self):
        return not self.steps and self.flying is None


def sum_small(values):
    count = lax.axis_size("dp")
    for bit in range(count.bit_length() - 1):
        perm = [(at, at ^ (1 << bit)) for at in range(count)]
        values = values + lax.ppermute(values, "dp", perm)
    return values


def body_pair(
    tokens,
    doc_lengths,
    cotangent,
    query_weight,
    query_bias,
    key_weight,
    value_weight,
    value_bias,
    out_weight,
    out_bias,
    first_gain,
    first_shift,
    up_weight,
    up_bias,
    down_weight,
    down_bias,
    second_gain,
    second_shift,
):
    own_rows = tokens.shape[0]
    length = 2 * own_rows
    doc_count = doc_lengths.shape[1]
    side = lax.axis_index("mp")
    first = side == 0
    f32 = jnp.float32
    bf16 = jnp.bfloat16

    def parts(rows, count=2):
        size = rows.shape[0] // count
        return [rows[at * size : (at + 1) * size] for at in range(count)]

    row = lambda vector: vector.astype(f32).reshape(1, -1)
    whole_segment = segment_ids(doc_lengths, length)[0]
    segment_own = lax.dynamic_slice_in_dim(whole_segment, side * own_rows, own_rows, 0)
    segment_other = lax.dynamic_slice_in_dim(whole_segment, (1 - side) * own_rows, own_rows, 0)
    segment = jnp.concatenate([segment_own, segment_other])
    valid = (segment_own < doc_count - 1).astype(f32)[:, None]

    place = lax.axis_index("dp")
    count = lax.axis_size("dp")
    pack = swap(pack_weights(place.reshape(1), count, up_weight, down_weight))
    packs = lax.all_gather(pack, "dp", axis=0)
    packs = packs.reshape(count, 2, pack.shape[0] // 2, pack.shape[1])
    bias_other = swap(up_bias)

    tokens_other = swap(after(tokens, pack))
    out_other = swap(after(out_weight, tokens_other))
    project = lambda rows: (
        (matmul(rows, query_weight) + query_bias).astype(bf16),
        matmul(rows, key_weight).astype(bf16),
        (matmul(rows, value_weight) + value_bias).astype(bf16),
    )
    query_own, key_own, value_own = project(tokens)
    query_other, key_other, value_other = project(tokens_other)
    key_rows = jnp.concatenate([key_own, key_other])
    values = jnp.concatenate([value_own, value_other])
    context_away, mass_other = attention_forward(
        query_other, key_rows, values, segment_other, segment
    )
    context_here = swap(context_away)
    context_own, mass_own = attention_forward(
        query_own, key_rows, values, after(segment_own, context_away, out_other), segment
    )

    hidden, hidden_own, normal_first, inverse_first = middle_norm(
        context_own, context_here, out_weight, out_other, row(out_bias), tokens,
        row(first_gain), row(first_shift),
    )
    hidden_other = swap(hidden_own)

    act_own, slope_own, base = forward_own(hidden_own, up_weight, row(up_bias), down_weight)
    slope_local, output, d_final, final_own, second_sums = forward_other(
        hidden_own, packs, row(bias_other), base, hidden, row(down_bias), cotangent, valid,
        row(second_gain), row(second_shift),
    )
    final_other = swap(final_own)
    d_pre_own, d_middle, middle_own, first_sums = backward_rows(
        final_own, slope_own, slope_local, up_weight, down_weight, packs, d_final,
        normal_first, inverse_first, row(first_gain),
    )
    d_context_away = matmul_nt(middle_own, out_other).astype(bf16)
    d_context_other = swap(d_context_away)
    d_context_own = matmul_nt(middle_own, out_weight).astype(bf16)

    hidden_other = after(hidden_other, d_context_away, d_context_own)
    final_other = after(final_other, d_context_away, d_context_own)
    slope_other, grad_down_weight = down_grad(
        hidden_other, up_weight, row(up_bias), act_own, final_own, final_other
    )
    down_sum = lax.psum(grad_down_weight, "dp")
    queries = jnp.concatenate([query_own, query_other])
    context = jnp.concatenate([context_own, context_away])
    mass = jnp.concatenate([mass_own, mass_other], axis=1)
    d_context_other = after(d_context_other, grad_down_weight)
    d_context = jnp.concatenate([d_context_own, d_context_other])
    gathered = jnp.concatenate([tokens, tokens_other])
    weights = (query_weight, key_weight, value_weight)
    width = query_weight.shape[1]
    once = jnp.minimum(doc_lengths[0, 0], 1)

    def entering(rows):
        return functools.reduce(jnp.add, [matmul_nt(d, w) for d, w in zip(rows, weights)])

    def run(part, start):
        return lax.while_loop(
            lambda carry: carry[0] < once,
            lambda carry: (carry[0] + 1, part(carry[1])),
            (0, start),
        )[1]

    left = []

    def backward_part(carry):
        d_context, final_other, d_middle = carry[0], carry[3], carry[5]
        grad_up_weight, grad_up_bias = up_grad(
            final_other, down_weight, slope_other, d_pre_own, hidden_own, hidden_other
        )
        up_sum = Chain(grad_up_weight).push()
        partial_away = matmul_tn(after(context_here, grad_up_weight), middle_own).astype(bf16)
        partial_here = swap(partial_away)
        up_sum.push(partial_away)
        rows, up_sum.held = lax.optimization_barrier((d_context, up_sum.held))
        d_rows = attention_backward(
            queries, key_rows, values, rows, context, mass, segment, 0, 1
        )
        up_sum.push(*d_rows)
        grads = [matmul_tn(gathered, d).astype(bf16) for d in d_rows]
        grad_out_weight = matmul_tn(after(context_own, d_rows[0]), middle_own)
        grads.append((grad_out_weight + partial_here.astype(f32)).astype(bf16))
        away = [parts(d)[1] for d in d_rows]
        away[0] = after(away[0], *grads)
        away = entering(away).astype(bf16)
        back = swap(away)
        own = [parts(d)[0] for d in d_rows]
        own[0] = after(own[0], away)
        own = entering(own) + d_middle
        biases = [jnp.sum(d_rows[at], axis=0, dtype=f32) for at in (0, 2)]
        up_sum.end(own)
        left[:] = [up_sum.steps]
        return (*grads, up_sum.held, own + back.astype(f32), *biases, grad_up_bias)

    *grads, held, input_grad, query_bias_sum, value_bias_sum, grad_up_bias = run(
        backward_part,
        (
            d_context, jnp.zeros_like(key_rows), jnp.zeros_like(values), final_other,
            jnp.zeros((2 * up_weight.shape[0] // count, up_bias.size), bf16), d_middle,
            jnp.zeros((width,), f32), jnp.zeros((width,), f32),
            jnp.zeros((1, up_bias.size), f32),
        ),
    )
    down_sum, *grads = lax.optimization_barrier((down_sum, *grads))
    *qkv, out_sum = lax.psum(tuple(grads), "dp")

    short = jnp.concatenate(
        [
            first_sums[:3].reshape(-1), second_sums[:3].reshape(-1), grad_up_bias.reshape(-1),
            query_bias_sum, value_bias_sum,
        ]
    )
    sizes = [tokens.shape[1]] * 6 + [up_bias.size, width, width]

    def last_part(carry):
        held, _, short = carry
        up_sum = Chain(held)
        up_sum.steps = list(left[0])
        both = 6 * tokens.shape[1]
        shared = short[:both] + swap(short[:both])
        short = sum_small(jnp.concatenate([shared, short[both:]]))
        while not up_sum.done():
            up_sum.push()
        return held, up_sum.held, short

    held = after(held, grads[0])
    _, up_total, small = run(last_part, (held, jnp.zeros(up_weight.shape, bf16), short))
    pieces, at = [], 0
    for size in sizes:
        pieces.append(small[at : at + size])
        at += size
    return (
        output,
        input_grad,
        qkv[0].astype(f32),
        pieces[7],
        qkv[1].astype(f32),
        qkv[2].astype(f32),
        pieces[8],
        out_sum.astype(f32),
        pieces[2],
        pieces[0],
        pieces[1],
        up_total.astype(f32),
        pieces[6],
        after(down_sum, up_total).astype(f32),
        pieces[5],
        pieces[3],
        pieces[4],
    )


def solution(mesh):
    in_specs = (
        P(("dp", "mp"), None),
        P("dp", None),
        P(("dp", "mp"), None),
        P(None, "mp"),
        P("mp"),
        P(None, "mp"),
        P(None, "mp"),
        P("mp"),
        P("mp", None),
        P(),
        P(),
        P(),
        P(None, "mp"),
        P("mp"),
        P("mp", None),
        P(),
        P(),
        P(),
    )
    out_specs = (
        P(("dp", "mp"), None),
        P(("dp", "mp"), None),
        P(None, "mp"),
        P("mp"),
        P(None, "mp"),
        P(None, "mp"),
        P("mp"),
        P("mp", None),
        P(),
        P(),
        P(),
        P(None, "mp"),
        P("mp"),
        P("mp", None),
        P(),
        P(),
        P(),
    )
    dp, mp = mesh.shape["dp"], mesh.shape["mp"]
    paired = mp == 2 and dp > 1 and dp & (dp - 1) == 0
    body = body_pair if paired else body_general
    return jax.shard_map(body, mesh=mesh, in_specs=in_specs, out_specs=out_specs, check_vma=False)
```

```python
import functools
import jax
import jax.numpy as jnp
from jax import lax
from jax.experimental import pallas as pl
from jax.experimental.pallas import tpu as pltpu
from jax.sharding import PartitionSpec as P

HEAD = 64
LANES = 128


epsilon = 1e-05
masked_score = -1000000000.0


def work(flops):
    return pl.CostEstimate(flops=flops, bytes_accessed=0, transcendentals=0)


def dot_nn(left, right):
    return lax.dot_general(left, right, (((1,), (0,)), ((), ())), preferred_element_type=jnp.float32)


def dot_nt(left, right):
    return lax.dot_general(left, right, (((1,), (1,)), ((), ())), preferred_element_type=jnp.float32)


def dot_tn(left, right):
    return lax.dot_general(left, right, (((0,), (0,)), ((), ())), preferred_element_type=jnp.float32)


def forward_kernel(pairs, q_ref, k_ref, v_ref, row_ref, col_ref, ctx_ref, lse_ref, bias_ref):
    bias_ref[...] = jnp.where(col_ref[...] == row_ref[...], 0.0, masked_score)
    rows = q_ref.shape[0]
    lane = lax.broadcasted_iota(jnp.int32, (rows, LANES), 1)
    stats = jnp.zeros((rows, LANES), jnp.float32)
    for pair in range(pairs):
        cols = slice(pair * LANES, (pair + 1) * LANES)
        q_pair = q_ref[:, cols] * jnp.bfloat16(HEAD ** (-0.5))
        k_pair = k_ref[:, cols]
        v_pair = v_ref[:, cols]
        halves = []
        for half in range(2):
            keep = (lane >= HEAD) == (half == 1)
            q_half = jnp.where(keep, q_pair, jnp.bfloat16(0))
            scores = dot_nt(q_half, k_pair) + bias_ref[...]
            row_max = jnp.max(scores, axis=-1, keepdims=True)
            exponent = jnp.exp(scores - row_max)
            row_sum = jnp.sum(exponent, axis=-1, keepdims=True)
            blended = dot_nn(exponent.astype(jnp.bfloat16), v_pair)
            halves.append(blended * (1.0 / row_sum))
            stats = jnp.where(lane == 2 * pair + half, row_max + jnp.log(row_sum), stats)
        ctx_ref[:, cols] = jnp.where(lane >= HEAD, halves[1], halves[0]).astype(ctx_ref.dtype)
    lse_ref[...] = jnp.transpose(stats)[: lse_ref.shape[0], :]


def attention_forward(queries, key_rows, values, row_segment, segment, block=256):
    rows, width = queries.shape
    length = key_rows.shape[0]
    pairs = width // LANES
    heads = width // HEAD
    whole = lambda shape: pl.BlockSpec(shape, lambda i: (0, 0))
    return pl.pallas_call(
        functools.partial(forward_kernel, pairs),
        grid=(rows // block,),
        in_specs=[
            pl.BlockSpec((block, width), lambda i: (i, 0)),
            whole((length, width)),
            whole((length, width)),
            whole((1, length)),
            pl.BlockSpec((block, 1), lambda i: (i, 0)),
        ],
        out_specs=[
            pl.BlockSpec((block, width), lambda i: (i, 0)),
            pl.BlockSpec((heads, block), lambda i: (0, i)),
        ],
        out_shape=[
            jax.ShapeDtypeStruct((rows, width), jnp.bfloat16),
            jax.ShapeDtypeStruct((heads, rows), jnp.float32),
        ],
        scratch_shapes=[pltpu.VMEM((block, length), jnp.float32)],
        compiler_params=pltpu.CompilerParams(vmem_limit_bytes=48 * 1024 * 1024),
        name="attention_forward",
        cost_estimate=work(2 * 8 * rows * length * width),
    )(queries, key_rows, values, segment.reshape(1, length), row_segment.reshape(rows, 1))


def backward_kernel(
    pairs, start, q_ref, k_ref, v_ref, g_ref, c_ref, lse_ref, row_ref, col_ref,
    out_q_ref, out_k_ref, out_v_ref, bias_ref, dk_sum, dv_sum,
):
    step = pl.program_id(0)
    bias_ref[...] = jnp.where(col_ref[...] == row_ref[...], 0.0, masked_score)
    rows = q_ref.shape[0]
    lane = lax.broadcasted_iota(jnp.int32, (rows, LANES), 1)
    key_lane = lax.broadcasted_iota(jnp.int32, (k_ref.shape[0], LANES), 1)
    inner = jnp.zeros((rows, LANES), jnp.float32)
    for pair in range(pairs):
        cols = slice(pair * LANES, (pair + 1) * LANES)
        both = g_ref[:, cols].astype(jnp.float32) * c_ref[:, cols].astype(jnp.float32)
        low = jnp.sum(jnp.where(lane < HEAD, both, 0.0), axis=-1, keepdims=True)
        high = jnp.sum(jnp.where(lane < HEAD, 0.0, both), axis=-1, keepdims=True)
        inner = jnp.where(lane == 2 * pair, low, jnp.where(lane == 2 * pair + 1, high, inner))
    inner = jnp.transpose(inner)

    @pl.when(step == 0)
    def _():
        dk_sum[...] = jnp.zeros_like(dk_sum)
        dv_sum[...] = jnp.zeros_like(dv_sum)

    for pair in range(pairs):
        cols = slice(pair * LANES, (pair + 1) * LANES)
        q_pair = q_ref[:, cols] * jnp.bfloat16(HEAD ** (-0.5))
        k_pair = k_ref[:, cols]
        v_pair = v_ref[:, cols]
        g_pair = g_ref[:, cols]
        dq = None
        for half in range(2):
            head = 2 * pair + half
            keep = (lane >= HEAD) == (half == 1)
            q_half = jnp.where(keep, q_pair, jnp.bfloat16(0))
            g_half = jnp.where(keep, g_pair, jnp.bfloat16(0))
            k_half = jnp.where((key_lane >= HEAD) == (half == 1), k_pair, jnp.bfloat16(0))
            mass = lse_ref[start + head : start + head + 1, :]
            probs = jnp.exp(dot_nt(k_pair, q_half) + bias_ref[...] - mass)
            d_probs = dot_nt(v_pair, g_half)
            d_scores = (probs * (d_probs - inner[head : head + 1, :])).astype(jnp.bfloat16)
            dv_sum[:, cols] += dot_nn(probs.astype(jnp.bfloat16), g_half)
            dk_sum[:, cols] += dot_nn(d_scores, q_half)
            part = dot_tn(d_scores, k_half)
            dq = part if dq is None else dq + part
        out_q_ref[:, cols] = (dq * HEAD ** (-0.5)).astype(out_q_ref.dtype)

    @pl.when(step == pl.num_programs(0) - 1)
    def _():
        out_k_ref[...] = dk_sum[...].astype(out_k_ref.dtype)
        out_v_ref[...] = dv_sum[...].astype(out_v_ref.dtype)


def attention_backward(
    queries, key_rows, values, d_context, context, lse, segment, at, of, block=256
):
    rows, width = queries.shape
    length = key_rows.shape[0]
    width = width // of
    pairs = width // LANES
    heads = lse.shape[0]
    part = pl.BlockSpec((block, width), lambda i: (i, at))
    keys = pl.BlockSpec((length, width), lambda i: (0, at))
    whole = pl.BlockSpec((length, width), lambda i: (0, 0))
    return pl.pallas_call(
        functools.partial(backward_kernel, pairs, at * (heads // of)),
        grid=(rows // block,),
        in_specs=[
            part, keys, keys, part, part,
            pl.BlockSpec((heads, block), lambda i: (0, i)),
            pl.BlockSpec((1, block), lambda i: (0, i)),
            pl.BlockSpec((length, 1), lambda i: (0, 0)),
        ],
        out_specs=[pl.BlockSpec((block, width), lambda i: (i, 0)), whole, whole],
        out_shape=[jax.ShapeDtypeStruct((rows, width), jnp.bfloat16)]
        + [jax.ShapeDtypeStruct((length, width), jnp.bfloat16)] * 2,
        scratch_shapes=[
            pltpu.VMEM((length, block), jnp.float32),
            pltpu.VMEM((length, width), jnp.float32),
            pltpu.VMEM((length, width), jnp.float32),
        ],
        compiler_params=pltpu.CompilerParams(vmem_limit_bytes=48 * 1024 * 1024),
        name="attention_backward",
        cost_estimate=work(2 * 4 * rows * length * width),
    )(queries, key_rows, values, d_context, context, lse,
      segment.reshape(1, rows), segment.reshape(length, 1))


def matmul(left, right):
    return jnp.dot(left, right, preferred_element_type=jnp.float32)


def matmul_tn(left, right):
    return lax.dot_general(
        left, right, (((0,), (0,)), ((), ())), preferred_element_type=jnp.float32
    )


def matmul_nt(left, right):
    return lax.dot_general(
        left, right, (((1,), (1,)), ((), ())), preferred_element_type=jnp.float32
    )


def layer_norm(inputs, gain, shift):
    center = inputs - jnp.mean(inputs, axis=-1, keepdims=True)
    spread = jnp.mean(center * center, axis=-1, keepdims=True)
    return center * lax.rsqrt(spread + epsilon) * gain + shift


def segment_ids(lengths, length):
    ends = jnp.cumsum(lengths, axis=-1)
    places = jnp.arange(length, dtype=jnp.int32)
    return jnp.sum((places[None, None, :] >= ends[:, :, None]).astype(jnp.int32), axis=1)


def score_block(q_block, s_block, key_rows, segment):
    raw = jnp.einsum(
        "qhd,khd->hqk", q_block, key_rows, preferred_element_type=jnp.float32
    ) * HEAD ** (-0.5)
    same = s_block[:, None] == segment[None, :]
    return jnp.where(same[None], raw, masked_score)


def body_general(
    tokens,
    doc_lengths,
    cotangent,
    query_weight,
    query_bias,
    key_weight,
    value_weight,
    value_bias,
    out_weight,
    out_bias,
    first_gain,
    first_shift,
    up_weight,
    up_bias,
    down_weight,
    down_bias,
    second_gain,
    second_shift,
):
    own_rows = tokens.shape[0]
    seq_count, doc_count = doc_lengths.shape
    all_rows = own_rows * lax.axis_size("mp")
    length = all_rows // seq_count
    head_count = query_weight.shape[1] // HEAD
    block_rows = min(512, length)
    block_count = length // block_rows
    score_scale = HEAD ** (-0.5)
    first_row = lax.axis_index("mp") * own_rows
    segment = segment_ids(doc_lengths, length)
    valid_all = (segment < doc_count - 1).reshape(all_rows)
    valid_rows = lax.dynamic_slice_in_dim(valid_all, first_row, own_rows, 0)
    shape_blocks = (seq_count, block_count, block_rows, head_count, HEAD)
    shape_seqs = (seq_count, length, head_count, HEAD)
    gain_first = first_gain.astype(jnp.float32)
    shift_first = first_shift.astype(jnp.float32)
    gathered = lax.all_gather(tokens, "mp", axis=0, tiled=True)
    queries = (matmul(gathered, query_weight) + query_bias).astype(jnp.bfloat16)
    key_rows = matmul(gathered, key_weight).astype(jnp.bfloat16)
    values = (matmul(gathered, value_weight) + value_bias).astype(jnp.bfloat16)

    def attend_sequence(members):
        q_seq, k_seq, v_seq, s_seq = members

        def attend_block(pieces):
            q_block, s_block = pieces
            scores = score_block(q_block, s_block, k_seq, s_seq)
            row_max = jnp.max(scores, axis=-1, keepdims=True)
            exponent = jnp.exp(scores - row_max)
            row_sum = jnp.sum(exponent, axis=-1, keepdims=True)
            attn_probs = (exponent / row_sum).astype(jnp.bfloat16)
            blended = jnp.einsum(
                "hqk,khd->qhd", attn_probs, v_seq, preferred_element_type=jnp.float32
            )
            return (blended.astype(jnp.bfloat16), (row_max + jnp.log(row_sum))[..., 0])

        return lax.map(attend_block, (q_seq, s_seq.reshape(block_count, block_rows)))

    context, log_mass = lax.map(
        attend_sequence,
        (
            queries.reshape(shape_blocks),
            key_rows.reshape(shape_seqs),
            values.reshape(shape_seqs),
            segment,
        ),
    )
    context = context.reshape(all_rows, head_count * HEAD)
    attn_part = lax.psum_scatter(matmul(context, out_weight), "mp", scatter_dimension=0, tiled=True)
    middle = attn_part + out_bias + tokens.astype(jnp.float32)
    hidden, norm_first = jax.vjp(layer_norm, middle, gain_first, shift_first)
    hidden_rows = lax.all_gather(hidden.astype(jnp.bfloat16), "mp", axis=0, tiled=True)
    pre = matmul(hidden_rows, up_weight) + up_bias
    act_exact, gelu_back = jax.vjp(lambda inputs: jax.nn.gelu(inputs, approximate=False), pre)
    act = act_exact.astype(jnp.bfloat16)
    ffn_part = lax.psum_scatter(matmul(act, down_weight), "mp", scatter_dimension=0, tiled=True)
    final = ffn_part + down_bias + hidden
    result, norm_second = jax.vjp(
        layer_norm, final, second_gain.astype(jnp.float32), second_shift.astype(jnp.float32)
    )
    upstream = cotangent.astype(jnp.float32) * valid_rows[:, None].astype(jnp.float32)
    d_final, grad_second_gain, grad_second_shift = norm_second(upstream)
    grad_down_bias = jnp.sum(d_final, axis=0)
    final_rows = lax.all_gather(d_final.astype(jnp.bfloat16), "mp", axis=0, tiled=True)
    grad_down_weight = matmul_tn(act, final_rows)
    d_pre = gelu_back(matmul_nt(final_rows, down_weight))[0].astype(jnp.bfloat16)
    grad_up_weight = matmul_tn(hidden_rows, d_pre)
    grad_up_bias = jnp.sum(d_pre, axis=0, dtype=jnp.float32)
    d_hidden = (
        lax.psum_scatter(matmul_nt(d_pre, up_weight), "mp", scatter_dimension=0, tiled=True)
        + d_final
    )
    d_middle, grad_first_gain, grad_first_shift = norm_first(d_hidden)
    grad_out_bias = jnp.sum(d_middle, axis=0)
    middle_rows = lax.all_gather(d_middle.astype(jnp.bfloat16), "mp", axis=0, tiled=True)
    grad_out_weight = matmul_tn(context, middle_rows)
    d_context = matmul_nt(middle_rows, out_weight).astype(jnp.bfloat16)

    def back_sequence(members):
        q_seq, k_seq, v_seq, s_seq, l_seq, g_seq = members

        def back_block(carried, pieces):
            grad_keys, grad_values = carried
            q_block, s_block, l_block, g_block = pieces
            scores = score_block(q_block, s_block, k_seq, s_seq)
            attn_probs = jnp.exp(scores - l_block[..., None])
            d_probs = jnp.einsum("qhd,khd->hqk", g_block, v_seq, preferred_element_type=jnp.float32)
            row_inner = jnp.sum(attn_probs * d_probs, axis=-1, keepdims=True)
            d_scores = (attn_probs * (d_probs - row_inner)).astype(jnp.bfloat16)
            d_block = (
                jnp.einsum("hqk,khd->qhd", d_scores, k_seq, preferred_element_type=jnp.float32)
                * score_scale
            )
            grad_keys = (
                grad_keys
                + jnp.einsum("hqk,qhd->khd", d_scores, q_block, preferred_element_type=jnp.float32)
                * score_scale
            )
            grad_values = grad_values + jnp.einsum(
                "hqk,qhd->khd",
                attn_probs.astype(jnp.bfloat16),
                g_block,
                preferred_element_type=jnp.float32,
            )
            return ((grad_keys, grad_values), d_block.astype(jnp.bfloat16))

        zero_grads = jnp.zeros((length, head_count, HEAD), jnp.float32)
        (grad_keys, grad_values), d_blocks = lax.scan(
            back_block,
            (zero_grads, zero_grads),
            (q_seq, s_seq.reshape(block_count, block_rows), l_seq, g_seq),
        )
        return (d_blocks, grad_keys.astype(jnp.bfloat16), grad_values.astype(jnp.bfloat16))

    d_queries, d_keys, d_values = lax.map(
        back_sequence,
        (
            queries.reshape(shape_blocks),
            key_rows.reshape(shape_seqs),
            values.reshape(shape_seqs),
            segment,
            log_mass,
            d_context.reshape(shape_blocks),
        ),
    )
    d_queries = d_queries.reshape(all_rows, head_count * HEAD)
    d_keys = d_keys.reshape(all_rows, head_count * HEAD)
    d_values = d_values.reshape(all_rows, head_count * HEAD)
    grad_query_weight = matmul_tn(gathered, d_queries)
    grad_key_weight = matmul_tn(gathered, d_keys)
    grad_value_weight = matmul_tn(gathered, d_values)
    grad_query_bias = jnp.sum(d_queries, axis=0, dtype=jnp.float32)
    grad_value_bias = jnp.sum(d_values, axis=0, dtype=jnp.float32)
    total_grad = matmul_nt(d_queries, query_weight)
    total_grad = total_grad + matmul_nt(d_keys, key_weight)
    input_grad = (
        lax.psum_scatter(
            (total_grad + matmul_nt(d_values, value_weight)).astype(jnp.bfloat16),
            "mp",
            scatter_dimension=0,
            tiled=True,
        ).astype(jnp.float32)
        + d_middle
    )
    (
        grad_out_bias,
        grad_first_gain,
        grad_first_shift,
        grad_down_bias,
        grad_second_gain,
        grad_second_shift,
    ) = lax.psum(
        (
            grad_out_bias,
            grad_first_gain,
            grad_first_shift,
            grad_down_bias,
            grad_second_gain,
            grad_second_shift,
        ),
        ("dp", "mp"),
    )
    (
        grad_query_weight,
        grad_query_bias,
        grad_key_weight,
        grad_value_weight,
        grad_value_bias,
        grad_out_weight,
        grad_up_weight,
        grad_up_bias,
        grad_down_weight,
    ) = (
        lax.psum(grad_query_weight.astype(jnp.bfloat16), "dp").astype(jnp.float32),
        lax.psum(grad_query_bias.astype(jnp.bfloat16), "dp").astype(jnp.float32),
        lax.psum(grad_key_weight.astype(jnp.bfloat16), "dp").astype(jnp.float32),
        lax.psum(grad_value_weight.astype(jnp.bfloat16), "dp").astype(jnp.float32),
        lax.psum(grad_value_bias.astype(jnp.bfloat16), "dp").astype(jnp.float32),
        lax.psum(grad_out_weight.astype(jnp.bfloat16), "dp").astype(jnp.float32),
        lax.psum(grad_up_weight.astype(jnp.bfloat16), "dp").astype(jnp.float32),
        lax.psum(grad_up_bias.astype(jnp.bfloat16), "dp").astype(jnp.float32),
        lax.psum(grad_down_weight.astype(jnp.bfloat16), "dp").astype(jnp.float32),
    )
    return (
        result.astype(jnp.bfloat16),
        input_grad,
        grad_query_weight,
        grad_query_bias,
        grad_key_weight,
        grad_value_weight,
        grad_value_bias,
        grad_out_weight,
        grad_out_bias,
        grad_first_gain,
        grad_first_shift,
        grad_up_weight,
        grad_up_bias,
        grad_down_weight,
        grad_down_bias,
        grad_second_gain,
        grad_second_shift,
    )


def swap(rows):
    return lax.ppermute(rows, "mp", [(0, 1), (1, 0)])


def normal_parts(pre):
    size = jnp.abs(pre) * (0.5**0.5)
    t = 1.0 / (1.0 + 0.3275911 * size)
    bell = jnp.exp(-size * size)
    series = t * (
        0.254829592
        + t * (-0.284496736 + t * (1.421413741 + t * (-1.453152027 + t * 1.061405429)))
    )
    tail = 0.5 * series * bell
    return jnp.where(pre < 0, tail, 1.0 - tail), pre * bell * 0.3989422804014327


def gelu_parts(pre):
    cumulative, slope = normal_parts(pre)
    return (pre * cumulative).astype(jnp.bfloat16), (cumulative + slope).astype(jnp.bfloat16)


def blank(shapes):
    return pl.pallas_call(
        lambda *refs: None,
        out_specs=[pl.BlockSpec(memory_space=pl.ANY)] * len(shapes),
        out_shape=[jax.ShapeDtypeStruct(*shape) for shape in shapes],
        name="blank",
    )()


def mean_of(rows):
    return jnp.mean(rows, axis=-1, keepdims=True)


def column_sums(rows):
    return jnp.sum(rows, axis=0, keepdims=True)


def pack_kernel(place_ref, up_ref, down_ref, out_ref):
    rows = up_ref.shape[0]
    half = down_ref.shape[2]
    out_ref[:rows, :] = up_ref[...]
    out_ref[rows:, :half] = down_ref[0]
    out_ref[rows:, half:] = down_ref[1]


def pack_weights(place, count, up_weight, down_weight):
    depth, units = up_weight.shape
    rows = depth // count
    return pl.pallas_call(
        pack_kernel,
        grid_spec=pltpu.PrefetchScalarGridSpec(
            num_scalar_prefetch=1,
            grid=(1,),
            in_specs=[
                pl.BlockSpec((rows, units), lambda i, at: (at[0], 0)),
                pl.BlockSpec((2, rows, depth), lambda i, at: (0, at[0], 0)),
            ],
            out_specs=pl.BlockSpec((2 * rows, units), lambda i, at: (0, 0)),
        ),
        out_shape=jax.ShapeDtypeStruct((2 * rows, units), up_weight.dtype),
        name="pack_weights",
        cost_estimate=work(rows * units * 4096),
    )(place, up_weight, down_weight.reshape(2, units // 2, depth))


BIG = 56 * 1024 * 1024


def middle_kernel(own_ref, here_ref, w_own_ref, w_other_ref, bias_ref, tokens_ref, gain_ref,
                  shift_ref, hidden_ref, low_ref, normal_ref, inverse_ref):
    middle = (
        dot_nn(own_ref[...], w_own_ref[...])
        + dot_nn(here_ref[...], w_other_ref[...])
        + bias_ref[...]
        + tokens_ref[...].astype(jnp.float32)
    )
    center = middle - mean_of(middle)
    inverse = lax.rsqrt(mean_of(center * center) + epsilon)
    normal = center * inverse
    hidden = normal * gain_ref[...] + shift_ref[...]
    hidden_ref[...] = hidden
    low_ref[...] = hidden.astype(jnp.bfloat16)
    normal_ref[...] = normal
    inverse_ref[...] = inverse


def middle_norm(context_own, context_here, out_weight, out_other, bias, tokens, gain, shift,
                block=256):
    rows, depth = tokens.shape
    heads = context_own.shape[1]
    part = lambda width: pl.BlockSpec((block, width), lambda i: (i, 0))
    whole = lambda shape: pl.BlockSpec(shape, lambda i: (0, 0))
    return pl.pallas_call(
        middle_kernel,
        grid=(rows // block,),
        in_specs=[part(heads), part(heads), whole((heads, depth)), whole((heads, depth)),
                  whole((1, depth)), part(depth), whole((1, depth)), whole((1, depth))],
        out_specs=[part(depth), part(depth), part(depth), part(1)],
        out_shape=[
            jax.ShapeDtypeStruct((rows, depth), jnp.float32),
            jax.ShapeDtypeStruct((rows, depth), jnp.bfloat16),
            jax.ShapeDtypeStruct((rows, depth), jnp.float32),
            jax.ShapeDtypeStruct((rows, 1), jnp.float32),
        ],
        compiler_params=pltpu.CompilerParams(vmem_limit_bytes=BIG),
        name="middle_norm",
        cost_estimate=work(8 * rows * depth * heads),
    )(context_own, context_here, out_weight, out_other, bias, tokens, gain, shift)


UNITS = 512
PIECE = 512
STRIP = 64


def gelu_block(h_ref, up, bias_ref, act_ref, slope_ref, pre_scr):
    pre_scr[...] = dot_nn(h_ref[...], up)
    bias = bias_ref[...]
    for at in range(0, pre_scr.shape[0], STRIP):
        rows = slice(at, at + STRIP)
        act, slope = gelu_parts(pre_scr[rows, :] + bias)
        act_ref[rows, :] = act
        slope_ref[rows, :] = slope


def forward_own_kernel(h_ref, up_ref, bias_ref, down_ref, act_ref, slope_ref, base_ref, pre_scr):
    step = pl.program_id(0)

    @pl.when(step == 0)
    def _():
        base_ref[...] = jnp.zeros_like(base_ref)

    gelu_block(h_ref, up_ref[...], bias_ref, act_ref, slope_ref, pre_scr)
    base_ref[...] += dot_nn(act_ref[...], down_ref[...])


def forward_own(hidden, up_weight, up_bias, down_weight):
    rows, depth = hidden.shape
    units = up_weight.shape[1]
    return pl.pallas_call(
        forward_own_kernel,
        grid=(units // UNITS,),
        in_specs=[
            pl.BlockSpec((rows, depth), lambda j: (0, 0)),
            pl.BlockSpec((depth, UNITS), lambda j: (0, j)),
            pl.BlockSpec((1, UNITS), lambda j: (0, j)),
            pl.BlockSpec((UNITS, depth), lambda j: (j, 0)),
        ],
        out_specs=[
            pl.BlockSpec((rows, UNITS), lambda j: (0, j)),
            pl.BlockSpec((rows, UNITS), lambda j: (0, j)),
            pl.BlockSpec((rows, depth), lambda j: (0, 0)),
        ],
        out_shape=[
            jax.ShapeDtypeStruct((rows, units), jnp.bfloat16),
            jax.ShapeDtypeStruct((rows, units), jnp.bfloat16),
            jax.ShapeDtypeStruct((rows, depth), jnp.float32),
        ],
        scratch_shapes=[pltpu.VMEM((rows, UNITS), jnp.float32)],
        compiler_params=pltpu.CompilerParams(vmem_limit_bytes=BIG),
        name="forward_own",
        cost_estimate=work(6 * rows * depth * units),
    )(hidden, up_weight, up_bias, down_weight)


def packed_specs(packs, at):
    count, _, features, _ = packs.shape
    groups = UNITS // features
    split = count // groups
    depth = count * features
    up = pl.BlockSpec((count, 1, features, UNITS), lambda j: (0, 0, 0, at(j)))
    down = pl.BlockSpec(
        (groups, 1, features, depth), lambda j: (at(j) % split, 1, 0, at(j) // split)
    )
    return up, down


def flat(ref):
    count, _, features, width = ref.shape
    return ref[...].reshape(count * features, width)


def forward_other_kernel(h_ref, up_ref, bias_ref, down_ref, base_ref, hidden_ref, down_bias_ref,
                         outer_ref, valid_ref, gain_ref, shift_ref,
                         slope_ref, out_ref, d_ref, low_ref, sums_ref, total, act_scr, pre_scr):
    step = pl.program_id(0)

    @pl.when(step == 0)
    def _():
        total[...] = base_ref[...]

    gelu_block(h_ref, flat(up_ref), bias_ref, act_scr, slope_ref, pre_scr)
    total[...] += dot_nn(act_scr[...], flat(down_ref))

    @pl.when(step == pl.num_programs(0) - 1)
    def _():
        gain = gain_ref[...]
        for_gain = for_shift = for_bias = 0.0
        for at in range(0, h_ref.shape[0], 256):
            rows = slice(at, at + 256)
            final = total[rows, :] + down_bias_ref[...] + hidden_ref[rows, :]
            center = final - mean_of(final)
            inverse = lax.rsqrt(mean_of(center * center) + epsilon)
            normal = center * inverse
            out_ref[rows, :] = (normal * gain + shift_ref[...]).astype(jnp.bfloat16)
            upstream = outer_ref[rows, :].astype(jnp.float32) * valid_ref[rows, :]
            scaled = upstream * gain
            back = (scaled - mean_of(scaled) - normal * mean_of(scaled * normal)) * inverse
            d_ref[rows, :] = back
            low_ref[rows, :] = back.astype(jnp.bfloat16)
            for_gain += column_sums(upstream * normal)
            for_shift += column_sums(upstream)
            for_bias += column_sums(back)
        sums_ref[...] = jnp.zeros_like(sums_ref)
        sums_ref[0:1, :] = for_gain
        sums_ref[1:2, :] = for_shift
        sums_ref[2:3, :] = for_bias


def forward_other(hidden_low, packs, bias, base, hidden, down_bias, outer, valid, gain, shift,
                  at, of, earlier):
    whole_rows, depth = hidden_low.shape
    rows = whole_rows // of
    units = packs.shape[3]
    up, down = packed_specs(packs, lambda j: j)
    whole = lambda shape: pl.BlockSpec(shape, lambda j: (0, 0))
    part = lambda width: pl.BlockSpec((rows, width), lambda j: (at, 0))
    body = forward_other_kernel
    if earlier:
        body = lambda *refs: forward_other_kernel(*refs[:11], *refs[14:])
    return pl.pallas_call(
        body,
        grid=(units // UNITS,),
        in_specs=[
            part(depth), up, pl.BlockSpec((1, UNITS), lambda j: (0, j)), down,
            part(depth), part(depth), whole((1, depth)), part(depth),
            part(1), whole((1, depth)), whole((1, depth)),
        ]
        + [pl.BlockSpec(memory_space=pl.ANY)] * len(earlier),
        out_specs=[
            pl.BlockSpec((rows, UNITS), lambda j: (at, j)),
            part(depth), part(depth), whole((rows, depth)), whole((8, depth)),
        ],
        out_shape=[
            jax.ShapeDtypeStruct((whole_rows, units), jnp.bfloat16),
            jax.ShapeDtypeStruct((whole_rows, depth), jnp.bfloat16),
            jax.ShapeDtypeStruct((whole_rows, depth), jnp.float32),
            jax.ShapeDtypeStruct((rows, depth), jnp.bfloat16),
            jax.ShapeDtypeStruct((8, depth), jnp.float32),
        ],
        scratch_shapes=[
            pltpu.VMEM((rows, depth), jnp.float32), pltpu.VMEM((rows, UNITS), jnp.bfloat16),
            pltpu.VMEM((rows, UNITS), jnp.float32),
        ],
        input_output_aliases={11 + index: index for index in range(len(earlier))},
        compiler_params=pltpu.CompilerParams(vmem_limit_bytes=BIG),
        name="forward_other",
        cost_estimate=work(8 * rows * depth * units),
    )(hidden_low, packs, bias, packs, base, hidden, down_bias, outer, valid, gain, shift,
      *earlier)


def backward_rows_kernel(half, f_ref, slope_own_ref, slope_other_ref, up_ref, down_ref,
                         up_pack_ref, down_pack_ref, d_ref, normal_ref, inverse_ref, gain_ref,
                         d_pre_ref, middle_ref, low_ref, sums_ref, total):
    step = pl.program_id(0)

    def block(up, down, slope_ref, keep):
        for at in range(0, f_ref.shape[0], PIECE):
            rows = slice(at, at + PIECE)
            d_pre = (dot_nt(f_ref[rows, :], down) * slope_ref[rows, :]).astype(jnp.bfloat16)
            if keep:
                d_pre_ref[rows, :] = d_pre
            total[rows, :] += dot_nt(d_pre, up)

    @pl.when(step == 0)
    def _():
        total[...] = d_ref[...]

    @pl.when(step < half)
    def _():
        block(up_ref[...], down_ref[...], slope_own_ref, True)

    @pl.when(step >= half)
    def _():
        block(flat(up_pack_ref), flat(down_pack_ref), slope_other_ref, False)

    @pl.when(step == pl.num_programs(0) - 1)
    def _():
        gain = gain_ref[...]
        for_gain = for_shift = for_bias = 0.0
        for at in range(0, f_ref.shape[0], PIECE):
            rows = slice(at, at + PIECE)
            upstream = total[rows, :]
            normal = normal_ref[rows, :]
            scaled = upstream * gain
            back = (
                scaled - mean_of(scaled) - normal * mean_of(scaled * normal)
            ) * inverse_ref[rows, :]
            middle_ref[rows, :] = back
            low_ref[rows, :] = back.astype(jnp.bfloat16)
            for_gain += column_sums(upstream * normal)
            for_shift += column_sums(upstream)
            for_bias += column_sums(back)
        sums_ref[...] = jnp.zeros_like(sums_ref)
        sums_ref[0:1, :] = for_gain
        sums_ref[1:2, :] = for_shift
        sums_ref[2:3, :] = for_bias


def backward_rows(final_low, slope_own, slope_other, up_weight, down_weight, packs, d_final,
                  normal, inverse, gain):
    rows, depth = final_low.shape
    units = up_weight.shape[1]
    half = units // UNITS
    own = lambda j: jnp.minimum(j, half - 1)
    other = lambda j: jnp.maximum(j - half, 0)
    up, down = packed_specs(packs, other)
    whole = lambda shape: pl.BlockSpec(shape, lambda j: (0, 0))
    return pl.pallas_call(
        functools.partial(backward_rows_kernel, half),
        grid=(2 * half,),
        in_specs=[
            whole((rows, depth)),
            pl.BlockSpec((rows, UNITS), lambda j: (0, own(j))),
            pl.BlockSpec((rows, UNITS), lambda j: (0, other(j))),
            pl.BlockSpec((depth, UNITS), lambda j: (0, own(j))),
            pl.BlockSpec((UNITS, depth), lambda j: (own(j), 0)),
            up, down,
            whole((rows, depth)), whole((rows, depth)), whole((rows, 1)), whole((1, depth)),
        ],
        out_specs=[
            pl.BlockSpec((rows, UNITS), lambda j: (0, own(j))),
            whole((rows, depth)), whole((rows, depth)), whole((8, depth)),
        ],
        out_shape=[
            jax.ShapeDtypeStruct((rows, units), jnp.bfloat16),
            jax.ShapeDtypeStruct((rows, depth), jnp.float32),
            jax.ShapeDtypeStruct((rows, depth), jnp.bfloat16),
            jax.ShapeDtypeStruct((8, depth), jnp.float32),
        ],
        scratch_shapes=[pltpu.VMEM((rows, depth), jnp.float32)],
        compiler_params=pltpu.CompilerParams(vmem_limit_bytes=BIG),
        name="backward_rows",
        cost_estimate=work(10 * rows * depth * units),
    )(final_low, slope_own, slope_other, up_weight, down_weight, packs, packs, d_final, normal,
      inverse, gain)


def gelu_kernel(h_ref, up_ref, bias_ref, act_ref, slope_ref, pre_scr):
    gelu_block(h_ref, up_ref[...], bias_ref, act_ref, slope_ref, pre_scr)


def gelu_rows(hidden, up_weight, up_bias):
    rows, depth = hidden.shape
    units = up_weight.shape[1]
    return pl.pallas_call(
        gelu_kernel,
        grid=(units // UNITS,),
        in_specs=[
            pl.BlockSpec((rows, depth), lambda j: (0, 0)),
            pl.BlockSpec((depth, UNITS), lambda j: (0, j)),
            pl.BlockSpec((1, UNITS), lambda j: (0, j)),
        ],
        out_specs=[pl.BlockSpec((rows, UNITS), lambda j: (0, j))] * 2,
        out_shape=[jax.ShapeDtypeStruct((rows, units), jnp.bfloat16)] * 2,
        scratch_shapes=[pltpu.VMEM((rows, UNITS), jnp.float32)],
        compiler_params=pltpu.CompilerParams(vmem_limit_bytes=BIG),
        name="gelu_rows",
        cost_estimate=work(rows * depth),
    )(hidden, up_weight, up_bias)


def down_grad_kernel(count, own_ref, other_ref, *refs):
    grad_ref = refs[-1]
    total = None
    rows = own_ref.shape[0] // count
    for at in range(count):
        span = slice(at * rows, (at + 1) * rows)
        part = dot_tn(own_ref[span, :], refs[at][...]) + dot_tn(
            other_ref[span, :], refs[count + at][...]
        )
        total = part if total is None else total + part
    grad_ref[...] = total.astype(jnp.bfloat16)


def down_grad(act_own, act_other, final_own, final_other):
    rows, units = act_own.shape
    count = len(final_own)
    depth = final_own[0].shape[1]
    part = pl.BlockSpec((rows, UNITS), lambda j: (0, j))
    return pl.pallas_call(
        functools.partial(down_grad_kernel, count),
        grid=(units // UNITS,),
        in_specs=[part, part]
        + [pl.BlockSpec((rows // count, depth), lambda j: (0, 0))] * (2 * count),
        out_specs=pl.BlockSpec((UNITS, depth), lambda j: (j, 0)),
        out_shape=jax.ShapeDtypeStruct((units, depth), jnp.bfloat16),
        compiler_params=pltpu.CompilerParams(vmem_limit_bytes=BIG),
        name="down_grad",
        cost_estimate=work(4 * rows * depth * units),
    )(act_own, act_other, *final_own, *final_other)


def up_grad_kernel(f_ref, down_ref, slope_ref, d_pre_ref, h_own_ref, h_other_ref,
                   grad_ref, sums_ref, d_scr):
    for at in range(0, f_ref.shape[0], PIECE):
        rows = slice(at, at + PIECE)
        d_scr[rows, :] = (
            dot_nt(f_ref[rows, :], down_ref[...]) * slope_ref[rows, :]
        ).astype(jnp.bfloat16)
    grad_ref[...] = (
        dot_tn(h_own_ref[...], d_pre_ref[...]) + dot_tn(h_other_ref[...], d_scr[...])
    ).astype(jnp.bfloat16)
    sums_ref[...] = column_sums(d_pre_ref[...].astype(jnp.float32)) + column_sums(
        d_scr[...].astype(jnp.float32)
    )


def up_grad(final_other, down_weight, slope_other, d_pre_own, hidden_own, hidden_other):
    rows, depth = hidden_own.shape
    units = down_weight.shape[0]
    whole = lambda shape: pl.BlockSpec(shape, lambda j: (0, 0))
    part = pl.BlockSpec((rows, UNITS), lambda j: (0, j))
    return pl.pallas_call(
        up_grad_kernel,
        grid=(units // UNITS,),
        in_specs=[
            whole((rows, depth)),
            pl.BlockSpec((UNITS, depth), lambda j: (j, 0)),
            part, part,
            whole((rows, depth)), whole((rows, depth)),
        ],
        out_specs=[
            pl.BlockSpec((depth, UNITS), lambda j: (0, j)),
            pl.BlockSpec((1, UNITS), lambda j: (0, j)),
        ],
        out_shape=[
            jax.ShapeDtypeStruct((depth, units), jnp.bfloat16),
            jax.ShapeDtypeStruct((1, units), jnp.float32),
        ],
        scratch_shapes=[pltpu.VMEM((rows, UNITS), jnp.bfloat16)],
        compiler_params=pltpu.CompilerParams(vmem_limit_bytes=BIG),
        name="up_grad",
        cost_estimate=work(6 * rows * depth * units),
    )(final_other, down_weight, slope_other, d_pre_own, hidden_own, hidden_other)


def after(value, *earlier):
    return lax.optimization_barrier((value,) + earlier)[0]


def join_halves(kept, arrived):
    return (kept.astype(jnp.float32) + arrived.astype(jnp.float32)).astype(jnp.bfloat16)


class Chain:
    def __init__(self, item, swapped=False):
        self.count = lax.axis_size("dp")
        bits = list(range(self.count.bit_length() - 1))
        if swapped:
            bits[1:3] = bits[1:3][::-1]
        self.steps = [("fold", bit) for bit in bits] + [("spread", bit) for bit in reversed(bits)]
        self.held = item.astype(jnp.bfloat16)
        self.flying = None

    def end(self, *earlier):
        if self.flying is not None:
            kind, bit, kept, arrived = self.flying
            self.flying = None
            if earlier:
                arrived = after(arrived, *earlier)
            if kind == "fold":
                self.held = join_halves(kept, arrived)
            else:
                low = (lax.axis_index("dp") >> bit) & 1 == 0
                self.held = jnp.concatenate(
                    [jnp.where(low, kept, arrived), jnp.where(low, arrived, kept)]
                )

    def push(self, *earlier):
        self.end(*earlier)
        if self.steps:
            kind, bit = self.steps.pop(0)
            perm = [(at, at ^ (1 << bit)) for at in range(self.count)]
            kept = sent = self.held
            if kind == "fold":
                rows = self.held.shape[0] // 2
                place = (lax.axis_index("dp") >> bit) & 1
                kept = lax.dynamic_slice_in_dim(self.held, place * rows, rows, 0)
                sent = lax.dynamic_slice_in_dim(self.held, (1 - place) * rows, rows, 0)
            self.flying = kind, bit, kept, lax.ppermute(sent, "dp", perm)
        return self

    def gate(self, value):
        return after(value, self.held)

    def done(self):
        return not self.steps and self.flying is None


def body_pair(
    tokens,
    doc_lengths,
    cotangent,
    query_weight,
    query_bias,
    key_weight,
    value_weight,
    value_bias,
    out_weight,
    out_bias,
    first_gain,
    first_shift,
    up_weight,
    up_bias,
    down_weight,
    down_bias,
    second_gain,
    second_shift,
):
    own_rows = tokens.shape[0]
    length = 2 * own_rows
    doc_count = doc_lengths.shape[1]
    side = lax.axis_index("mp")
    first = side == 0
    f32 = jnp.float32
    bf16 = jnp.bfloat16

    def parts(rows, count=2):
        size = rows.shape[0] // count
        return [rows[at * size : (at + 1) * size] for at in range(count)]

    row = lambda vector: vector.astype(f32).reshape(1, -1)
    whole_segment = segment_ids(doc_lengths, length)[0]
    segment_own = lax.dynamic_slice_in_dim(whole_segment, side * own_rows, own_rows, 0)
    segment_other = lax.dynamic_slice_in_dim(whole_segment, (1 - side) * own_rows, own_rows, 0)
    segment = jnp.concatenate([segment_own, segment_other])
    valid = (segment_own < doc_count - 1).astype(f32)[:, None]

    place = lax.axis_index("dp")
    count = lax.axis_size("dp")
    pack = swap(pack_weights(place.reshape(1), count, up_weight, down_weight))
    packs = lax.all_gather(pack, "dp", axis=0)
    packs = packs.reshape(count, 2, pack.shape[0] // 2, pack.shape[1])
    bias_other = swap(up_bias)

    tokens_other = swap(after(tokens, pack))
    out_other = swap(after(out_weight, tokens_other))
    project = lambda rows: (
        (matmul(rows, query_weight) + query_bias).astype(bf16),
        matmul(rows, key_weight).astype(bf16),
        (matmul(rows, value_weight) + value_bias).astype(bf16),
    )
    fills = blank(
        [
            *[((length, query_weight.shape[1]), bf16)] * 3,
            ((own_rows, tokens.shape[1]), bf16),
            ((4 * up_weight.shape[0] // count, up_bias.size), bf16),
            (up_weight.shape, f32),
            (down_weight.shape, f32),
        ]
    )
    query_own, key_own, value_own = project(tokens)
    query_other, key_other, value_other = project(tokens_other)
    key_rows = jnp.concatenate([key_own, key_other])
    values = jnp.concatenate([value_own, value_other])
    context_away, mass_other = attention_forward(
        query_other, key_rows, values, segment_other, segment
    )
    context_here = swap(context_away)
    context_own, mass_own = attention_forward(
        query_own, key_rows, values, after(segment_own, context_away, out_other), segment
    )

    hidden, hidden_own, normal_first, inverse_first = middle_norm(
        context_own, context_here, out_weight, out_other, row(out_bias), tokens,
        row(first_gain), row(first_shift),
    )
    hidden_other = swap(hidden_own)

    act_own, slope_own, base = forward_own(hidden_own, up_weight, row(up_bias), down_weight)
    earlier, final_own, second_sums = (), [], 0.0
    for at in range(2):
        *earlier, low_rows, sums = forward_other(
            hidden_own, packs, row(bias_other), base, hidden, row(down_bias), cotangent, valid,
            row(second_gain), row(second_shift), at, 2, earlier,
        )
        final_own.append(low_rows)
        second_sums = second_sums + sums
    slope_local, output, d_final = earlier
    final_other = [swap(rows) for rows in final_own]
    act_other, slope_other = gelu_rows(
        after(hidden_other, *final_own, final_other[0]), up_weight, row(up_bias)
    )
    grad_down_weight = down_grad(act_own, act_other, final_own, final_other)
    down_sum = lax.psum(grad_down_weight, "dp")

    *final_own, grad_down_weight = lax.optimization_barrier((*final_own, grad_down_weight))
    final_rows = jnp.concatenate(final_own)
    final_away = jnp.concatenate(final_other)
    queries = jnp.concatenate([query_own, query_other])
    context = jnp.concatenate([context_own, context_away])
    mass = jnp.concatenate([mass_own, mass_other], axis=1)
    gathered = jnp.concatenate([tokens, tokens_other])
    weights = (query_weight, key_weight, value_weight)
    width = query_weight.shape[1]
    once = jnp.minimum(doc_lengths[0, 0], 1)

    def entering(rows):
        return functools.reduce(jnp.add, [matmul_nt(d, w) for d, w in zip(rows, weights)])

    def run(part, start):
        return lax.while_loop(
            lambda carry: carry[0] < once,
            lambda carry: (carry[0] + 1, part(carry[1])),
            (0, start),
        )[1]

    left = []

    def backward_part(carry):
        final_rows, d_final = carry[0][3], carry[3]
        d_pre_own, d_middle, middle_own, first_sums = backward_rows(
            final_rows, slope_own, slope_local, up_weight, down_weight, packs, d_final,
            normal_first, inverse_first, row(first_gain),
        )
        d_context_away = matmul_nt(middle_own, out_other).astype(bf16)
        d_context_other = swap(d_context_away)
        d_context_own = matmul_nt(middle_own, out_weight).astype(bf16)
        grad_up_weight, grad_up_bias = up_grad(
            after(final_away, d_context_away, d_context_own), down_weight, slope_other,
            d_pre_own, hidden_own, hidden_other,
        )
        d_context = jnp.concatenate([d_context_own, d_context_other])
        up_sum = Chain(grad_up_weight).push()
        partial_away = matmul_tn(after(context_here, grad_up_weight), middle_own).astype(bf16)
        partial_here = swap(partial_away)
        up_sum.push(partial_away)
        rows, up_sum.held = lax.optimization_barrier((d_context, up_sum.held))
        d_rows = attention_backward(
            queries, key_rows, values, rows, context, mass, segment, 0, 1
        )
        up_sum.end(*d_rows)
        left[:] = [up_sum.steps]
        d_rows, up_sum.held = lax.optimization_barrier((d_rows, up_sum.held))
        grads = [matmul_tn(gathered, d).astype(bf16) for d in d_rows]
        grad_out_weight = matmul_tn(after(context_own, d_rows[0]), middle_own)
        grads.append((grad_out_weight + partial_here.astype(f32)).astype(bf16))
        away = entering([parts(d)[1] for d in d_rows]).astype(bf16)
        own = entering([parts(d)[0] for d in d_rows]) + d_middle
        biases = [jnp.sum(d_rows[at], axis=0, dtype=f32) for at in (0, 2)]
        return grads, away, up_sum.held, own, biases, grad_up_bias, first_sums

    final_rows = after(final_rows, grad_down_weight)
    grads, away, held, own, biases, grad_up_bias, first_sums = run(
        backward_part,
        (
            [*fills[:3], final_rows], fills[3], fills[4], d_final,
            [jnp.zeros((width,), f32)] * 2, jnp.zeros((1, up_bias.size), f32),
            jnp.zeros_like(second_sums),
        ),
    )
    down_sum, grads = lax.optimization_barrier((down_sum, grads))
    *qkv, out_sum = lax.psum(tuple(grads), "dp")

    short = jnp.concatenate(
        [
            first_sums[:3].reshape(-1), second_sums[:3].reshape(-1), grad_up_bias.reshape(-1),
            *biases,
        ]
    )
    sizes = [tokens.shape[1]] * 6 + [up_bias.size, width, width]

    def last_part(carry):
        held, _, _, short, own = carry
        down_total = after(down_sum, short).astype(f32)
        up_sum = Chain(held)
        up_sum.steps = list(left[0])
        up_sum.push()
        back = swap(after(away, short))
        both = 6 * tokens.shape[1]
        shared = short[:both] + swap(short[:both])
        short = jnp.concatenate([shared, short[both:]])
        up_sum.push(short, down_total)
        for step in range(count.bit_length() - 1):
            short = short + lax.ppermute(
                short, "dp", [(at, at ^ (1 << step)) for at in range(count)]
            )
            up_sum.push(short)
        total_grad = own + back.astype(f32)
        while not up_sum.done():
            up_sum.push(total_grad)
        return held, up_sum.held.astype(f32), down_total, short, total_grad

    held = after(held, grads[0])
    _, up_total, down_total, small, input_grad = run(
        last_part, (held, fills[5], fills[6], short, own)
    )
    up_total, qkv, out_sum = lax.optimization_barrier((up_total, qkv, out_sum))
    pieces, at = [], 0
    for size in sizes:
        pieces.append(small[at : at + size])
        at += size
    return (
        output,
        input_grad,
        qkv[0].astype(f32),
        pieces[7],
        qkv[1].astype(f32),
        qkv[2].astype(f32),
        pieces[8],
        out_sum.astype(f32),
        pieces[2],
        pieces[0],
        pieces[1],
        up_total,
        pieces[6],
        down_total,
        pieces[5],
        pieces[3],
        pieces[4],
    )


def solution(mesh):
    in_specs = (
        P(("dp", "mp"), None),
        P("dp", None),
        P(("dp", "mp"), None),
        P(None, "mp"),
        P("mp"),
        P(None, "mp"),
        P(None, "mp"),
        P("mp"),
        P("mp", None),
        P(),
        P(),
        P(),
        P(None, "mp"),
        P("mp"),
        P("mp", None),
        P(),
        P(),
        P(),
    )
    out_specs = (
        P(("dp", "mp"), None),
        P(("dp", "mp"), None),
        P(None, "mp"),
        P("mp"),
        P(None, "mp"),
        P(None, "mp"),
        P("mp"),
        P("mp", None),
        P(),
        P(),
        P(),
        P(None, "mp"),
        P("mp"),
        P("mp", None),
        P(),
        P(),
        P(),
    )
    dp, mp = mesh.shape["dp"], mesh.shape["mp"]
    paired = mp == 2 and dp > 1 and dp & (dp - 1) == 0
    body = body_pair if paired else body_general
    return jax.shard_map(body, mesh=mesh, in_specs=in_specs, out_specs=out_specs, check_vma=False)
```

```python
import functools
import jax
import jax.numpy as jnp
from jax import lax
from jax.experimental import pallas as pl
from jax.experimental.pallas import tpu as pltpu
from jax.sharding import PartitionSpec as P

HEAD = 64
LANES = 128


epsilon = 1e-05
masked_score = -1000000000.0


def work(flops):
    return pl.CostEstimate(flops=flops, bytes_accessed=0, transcendentals=0)


def dot_nn(left, right):
    return lax.dot_general(left, right, (((1,), (0,)), ((), ())), preferred_element_type=jnp.float32)


def dot_nt(left, right):
    return lax.dot_general(left, right, (((1,), (1,)), ((), ())), preferred_element_type=jnp.float32)


def dot_tn(left, right):
    return lax.dot_general(left, right, (((0,), (0,)), ((), ())), preferred_element_type=jnp.float32)


def forward_kernel(pairs, q_ref, k_ref, v_ref, row_ref, col_ref, ctx_ref, lse_ref, bias_ref):
    bias_ref[...] = jnp.where(col_ref[...] == row_ref[...], 0.0, masked_score)
    rows = q_ref.shape[0]
    lane = lax.broadcasted_iota(jnp.int32, (rows, LANES), 1)
    stats = jnp.zeros((rows, LANES), jnp.float32)
    for pair in range(pairs):
        cols = slice(pair * LANES, (pair + 1) * LANES)
        q_pair = q_ref[:, cols] * jnp.bfloat16(HEAD ** (-0.5))
        k_pair = k_ref[:, cols]
        v_pair = v_ref[:, cols]
        halves = []
        for half in range(2):
            keep = (lane >= HEAD) == (half == 1)
            q_half = jnp.where(keep, q_pair, jnp.bfloat16(0))
            scores = dot_nt(q_half, k_pair) + bias_ref[...]
            row_max = jnp.max(scores, axis=-1, keepdims=True)
            exponent = jnp.exp(scores - row_max)
            row_sum = jnp.sum(exponent, axis=-1, keepdims=True)
            blended = dot_nn(exponent.astype(jnp.bfloat16), v_pair)
            halves.append(blended * (1.0 / row_sum))
            stats = jnp.where(lane == 2 * pair + half, row_max + jnp.log(row_sum), stats)
        ctx_ref[:, cols] = jnp.where(lane >= HEAD, halves[1], halves[0]).astype(ctx_ref.dtype)
    lse_ref[...] = jnp.transpose(stats)[: lse_ref.shape[0], :]


def attention_forward(queries, key_rows, values, row_segment, segment, block=512):
    rows, width = queries.shape
    length = key_rows.shape[0]
    pairs = width // LANES
    heads = width // HEAD
    whole = lambda shape: pl.BlockSpec(shape, lambda i: (0, 0))
    return pl.pallas_call(
        functools.partial(forward_kernel, pairs),
        grid=(rows // block,),
        in_specs=[
            pl.BlockSpec((block, width), lambda i: (i, 0)),
            whole((length, width)),
            whole((length, width)),
            whole((1, length)),
            pl.BlockSpec((block, 1), lambda i: (i, 0)),
        ],
        out_specs=[
            pl.BlockSpec((block, width), lambda i: (i, 0)),
            pl.BlockSpec((heads, block), lambda i: (0, i)),
        ],
        out_shape=[
            jax.ShapeDtypeStruct((rows, width), jnp.bfloat16),
            jax.ShapeDtypeStruct((heads, rows), jnp.float32),
        ],
        scratch_shapes=[pltpu.VMEM((block, length), jnp.float32)],
        compiler_params=pltpu.CompilerParams(vmem_limit_bytes=48 * 1024 * 1024),
        name="attention_forward",
        cost_estimate=work(2 * 8 * rows * length * width),
    )(queries, key_rows, values, segment.reshape(1, length), row_segment.reshape(rows, 1))


def backward_kernel(
    pairs, start, q_ref, k_ref, v_ref, g_ref, c_ref, lse_ref, row_ref, col_ref,
    out_q_ref, out_k_ref, out_v_ref, bias_ref, dk_sum, dv_sum,
):
    step = pl.program_id(0)
    bias_ref[...] = jnp.where(col_ref[...] == row_ref[...], 0.0, masked_score)
    rows = q_ref.shape[0]
    lane = lax.broadcasted_iota(jnp.int32, (rows, LANES), 1)
    key_lane = lax.broadcasted_iota(jnp.int32, (k_ref.shape[0], LANES), 1)
    inner = jnp.zeros((rows, LANES), jnp.float32)
    for pair in range(pairs):
        cols = slice(pair * LANES, (pair + 1) * LANES)
        both = g_ref[:, cols].astype(jnp.float32) * c_ref[:, cols].astype(jnp.float32)
        low = jnp.sum(jnp.where(lane < HEAD, both, 0.0), axis=-1, keepdims=True)
        high = jnp.sum(jnp.where(lane < HEAD, 0.0, both), axis=-1, keepdims=True)
        inner = jnp.where(lane == 2 * pair, low, jnp.where(lane == 2 * pair + 1, high, inner))
    inner = jnp.transpose(inner)

    @pl.when(step == 0)
    def _():
        dk_sum[...] = jnp.zeros_like(dk_sum)
        dv_sum[...] = jnp.zeros_like(dv_sum)

    for pair in range(pairs):
        cols = slice(pair * LANES, (pair + 1) * LANES)
        q_pair = q_ref[:, cols] * jnp.bfloat16(HEAD ** (-0.5))
        k_pair = k_ref[:, cols]
        v_pair = v_ref[:, cols]
        g_pair = g_ref[:, cols]
        dq = None
        for half in range(2):
            head = 2 * pair + half
            keep = (lane >= HEAD) == (half == 1)
            q_half = jnp.where(keep, q_pair, jnp.bfloat16(0))
            g_half = jnp.where(keep, g_pair, jnp.bfloat16(0))
            k_half = jnp.where((key_lane >= HEAD) == (half == 1), k_pair, jnp.bfloat16(0))
            mass = lse_ref[start + head : start + head + 1, :]
            probs = jnp.exp(dot_nt(k_pair, q_half) + bias_ref[...] - mass)
            d_probs = dot_nt(v_pair, g_half)
            d_scores = (probs * (d_probs - inner[head : head + 1, :])).astype(jnp.bfloat16)
            dv_sum[:, cols] += dot_nn(probs.astype(jnp.bfloat16), g_half)
            dk_sum[:, cols] += dot_nn(d_scores, q_half)
            part = dot_tn(d_scores, k_half)
            dq = part if dq is None else dq + part
        out_q_ref[:, cols] = (dq * HEAD ** (-0.5)).astype(out_q_ref.dtype)

    @pl.when(step == pl.num_programs(0) - 1)
    def _():
        out_k_ref[...] = dk_sum[...].astype(out_k_ref.dtype)
        out_v_ref[...] = dv_sum[...].astype(out_v_ref.dtype)


def attention_backward(
    queries, key_rows, values, d_context, context, lse, segment, at, of, block=256
):
    rows, width = queries.shape
    length = key_rows.shape[0]
    width = width // of
    pairs = width // LANES
    heads = lse.shape[0]
    part = pl.BlockSpec((block, width), lambda i: (i, at))
    keys = pl.BlockSpec((length, width), lambda i: (0, at))
    whole = pl.BlockSpec((length, width), lambda i: (0, 0))
    return pl.pallas_call(
        functools.partial(backward_kernel, pairs, at * (heads // of)),
        grid=(rows // block,),
        in_specs=[
            part, keys, keys, part, part,
            pl.BlockSpec((heads, block), lambda i: (0, i)),
            pl.BlockSpec((1, block), lambda i: (0, i)),
            pl.BlockSpec((length, 1), lambda i: (0, 0)),
        ],
        out_specs=[pl.BlockSpec((block, width), lambda i: (i, 0)), whole, whole],
        out_shape=[jax.ShapeDtypeStruct((rows, width), jnp.bfloat16)]
        + [jax.ShapeDtypeStruct((length, width), jnp.bfloat16)] * 2,
        scratch_shapes=[
            pltpu.VMEM((length, block), jnp.float32),
            pltpu.VMEM((length, width), jnp.float32),
            pltpu.VMEM((length, width), jnp.float32),
        ],
        compiler_params=pltpu.CompilerParams(vmem_limit_bytes=48 * 1024 * 1024),
        name="attention_backward",
        cost_estimate=work(2 * 4 * rows * length * width),
    )(queries, key_rows, values, d_context, context, lse,
      segment.reshape(1, rows), segment.reshape(length, 1))


def matmul(left, right):
    return jnp.dot(left, right, preferred_element_type=jnp.float32)


def matmul_tn(left, right):
    return lax.dot_general(
        left, right, (((0,), (0,)), ((), ())), preferred_element_type=jnp.float32
    )


def matmul_nt(left, right):
    return lax.dot_general(
        left, right, (((1,), (1,)), ((), ())), preferred_element_type=jnp.float32
    )


def layer_norm(inputs, gain, shift):
    center = inputs - jnp.mean(inputs, axis=-1, keepdims=True)
    spread = jnp.mean(center * center, axis=-1, keepdims=True)
    return center * lax.rsqrt(spread + epsilon) * gain + shift


def segment_ids(lengths, length):
    ends = jnp.cumsum(lengths, axis=-1)
    places = jnp.arange(length, dtype=jnp.int32)
    return jnp.sum((places[None, None, :] >= ends[:, :, None]).astype(jnp.int32), axis=1)


def score_block(q_block, s_block, key_rows, segment):
    raw = jnp.einsum(
        "qhd,khd->hqk", q_block, key_rows, preferred_element_type=jnp.float32
    ) * HEAD ** (-0.5)
    same = s_block[:, None] == segment[None, :]
    return jnp.where(same[None], raw, masked_score)


def body_general(
    tokens,
    doc_lengths,
    cotangent,
    query_weight,
    query_bias,
    key_weight,
    value_weight,
    value_bias,
    out_weight,
    out_bias,
    first_gain,
    first_shift,
    up_weight,
    up_bias,
    down_weight,
    down_bias,
    second_gain,
    second_shift,
):
    own_rows = tokens.shape[0]
    seq_count, doc_count = doc_lengths.shape
    all_rows = own_rows * lax.axis_size("mp")
    length = all_rows // seq_count
    head_count = query_weight.shape[1] // HEAD
    block_rows = min(512, length)
    block_count = length // block_rows
    score_scale = HEAD ** (-0.5)
    first_row = lax.axis_index("mp") * own_rows
    segment = segment_ids(doc_lengths, length)
    valid_all = (segment < doc_count - 1).reshape(all_rows)
    valid_rows = lax.dynamic_slice_in_dim(valid_all, first_row, own_rows, 0)
    shape_blocks = (seq_count, block_count, block_rows, head_count, HEAD)
    shape_seqs = (seq_count, length, head_count, HEAD)
    gain_first = first_gain.astype(jnp.float32)
    shift_first = first_shift.astype(jnp.float32)
    gathered = lax.all_gather(tokens, "mp", axis=0, tiled=True)
    queries = (matmul(gathered, query_weight) + query_bias).astype(jnp.bfloat16)
    key_rows = matmul(gathered, key_weight).astype(jnp.bfloat16)
    values = (matmul(gathered, value_weight) + value_bias).astype(jnp.bfloat16)

    def attend_sequence(members):
        q_seq, k_seq, v_seq, s_seq = members

        def attend_block(pieces):
            q_block, s_block = pieces
            scores = score_block(q_block, s_block, k_seq, s_seq)
            row_max = jnp.max(scores, axis=-1, keepdims=True)
            exponent = jnp.exp(scores - row_max)
            row_sum = jnp.sum(exponent, axis=-1, keepdims=True)
            attn_probs = (exponent / row_sum).astype(jnp.bfloat16)
            blended = jnp.einsum(
                "hqk,khd->qhd", attn_probs, v_seq, preferred_element_type=jnp.float32
            )
            return (blended.astype(jnp.bfloat16), (row_max + jnp.log(row_sum))[..., 0])

        return lax.map(attend_block, (q_seq, s_seq.reshape(block_count, block_rows)))

    context, log_mass = lax.map(
        attend_sequence,
        (
            queries.reshape(shape_blocks),
            key_rows.reshape(shape_seqs),
            values.reshape(shape_seqs),
            segment,
        ),
    )
    context = context.reshape(all_rows, head_count * HEAD)
    attn_part = lax.psum_scatter(matmul(context, out_weight), "mp", scatter_dimension=0, tiled=True)
    middle = attn_part + out_bias + tokens.astype(jnp.float32)
    hidden, norm_first = jax.vjp(layer_norm, middle, gain_first, shift_first)
    hidden_rows = lax.all_gather(hidden.astype(jnp.bfloat16), "mp", axis=0, tiled=True)
    pre = matmul(hidden_rows, up_weight) + up_bias
    act_exact, gelu_back = jax.vjp(lambda inputs: jax.nn.gelu(inputs, approximate=False), pre)
    act = act_exact.astype(jnp.bfloat16)
    ffn_part = lax.psum_scatter(matmul(act, down_weight), "mp", scatter_dimension=0, tiled=True)
    final = ffn_part + down_bias + hidden
    result, norm_second = jax.vjp(
        layer_norm, final, second_gain.astype(jnp.float32), second_shift.astype(jnp.float32)
    )
    upstream = cotangent.astype(jnp.float32) * valid_rows[:, None].astype(jnp.float32)
    d_final, grad_second_gain, grad_second_shift = norm_second(upstream)
    grad_down_bias = jnp.sum(d_final, axis=0)
    final_rows = lax.all_gather(d_final.astype(jnp.bfloat16), "mp", axis=0, tiled=True)
    grad_down_weight = matmul_tn(act, final_rows)
    d_pre = gelu_back(matmul_nt(final_rows, down_weight))[0].astype(jnp.bfloat16)
    grad_up_weight = matmul_tn(hidden_rows, d_pre)
    grad_up_bias = jnp.sum(d_pre, axis=0, dtype=jnp.float32)
    d_hidden = (
        lax.psum_scatter(matmul_nt(d_pre, up_weight), "mp", scatter_dimension=0, tiled=True)
        + d_final
    )
    d_middle, grad_first_gain, grad_first_shift = norm_first(d_hidden)
    grad_out_bias = jnp.sum(d_middle, axis=0)
    middle_rows = lax.all_gather(d_middle.astype(jnp.bfloat16), "mp", axis=0, tiled=True)
    grad_out_weight = matmul_tn(context, middle_rows)
    d_context = matmul_nt(middle_rows, out_weight).astype(jnp.bfloat16)

    def back_sequence(members):
        q_seq, k_seq, v_seq, s_seq, l_seq, g_seq = members

        def back_block(carried, pieces):
            grad_keys, grad_values = carried
            q_block, s_block, l_block, g_block = pieces
            scores = score_block(q_block, s_block, k_seq, s_seq)
            attn_probs = jnp.exp(scores - l_block[..., None])
            d_probs = jnp.einsum("qhd,khd->hqk", g_block, v_seq, preferred_element_type=jnp.float32)
            row_inner = jnp.sum(attn_probs * d_probs, axis=-1, keepdims=True)
            d_scores = (attn_probs * (d_probs - row_inner)).astype(jnp.bfloat16)
            d_block = (
                jnp.einsum("hqk,khd->qhd", d_scores, k_seq, preferred_element_type=jnp.float32)
                * score_scale
            )
            grad_keys = (
                grad_keys
                + jnp.einsum("hqk,qhd->khd", d_scores, q_block, preferred_element_type=jnp.float32)
                * score_scale
            )
            grad_values = grad_values + jnp.einsum(
                "hqk,qhd->khd",
                attn_probs.astype(jnp.bfloat16),
                g_block,
                preferred_element_type=jnp.float32,
            )
            return ((grad_keys, grad_values), d_block.astype(jnp.bfloat16))

        zero_grads = jnp.zeros((length, head_count, HEAD), jnp.float32)
        (grad_keys, grad_values), d_blocks = lax.scan(
            back_block,
            (zero_grads, zero_grads),
            (q_seq, s_seq.reshape(block_count, block_rows), l_seq, g_seq),
        )
        return (d_blocks, grad_keys.astype(jnp.bfloat16), grad_values.astype(jnp.bfloat16))

    d_queries, d_keys, d_values = lax.map(
        back_sequence,
        (
            queries.reshape(shape_blocks),
            key_rows.reshape(shape_seqs),
            values.reshape(shape_seqs),
            segment,
            log_mass,
            d_context.reshape(shape_blocks),
        ),
    )
    d_queries = d_queries.reshape(all_rows, head_count * HEAD)
    d_keys = d_keys.reshape(all_rows, head_count * HEAD)
    d_values = d_values.reshape(all_rows, head_count * HEAD)
    grad_query_weight = matmul_tn(gathered, d_queries)
    grad_key_weight = matmul_tn(gathered, d_keys)
    grad_value_weight = matmul_tn(gathered, d_values)
    grad_query_bias = jnp.sum(d_queries, axis=0, dtype=jnp.float32)
    grad_value_bias = jnp.sum(d_values, axis=0, dtype=jnp.float32)
    total_grad = matmul_nt(d_queries, query_weight)
    total_grad = total_grad + matmul_nt(d_keys, key_weight)
    input_grad = (
        lax.psum_scatter(
            (total_grad + matmul_nt(d_values, value_weight)).astype(jnp.bfloat16),
            "mp",
            scatter_dimension=0,
            tiled=True,
        ).astype(jnp.float32)
        + d_middle
    )
    (
        grad_out_bias,
        grad_first_gain,
        grad_first_shift,
        grad_down_bias,
        grad_second_gain,
        grad_second_shift,
    ) = lax.psum(
        (
            grad_out_bias,
            grad_first_gain,
            grad_first_shift,
            grad_down_bias,
            grad_second_gain,
            grad_second_shift,
        ),
        ("dp", "mp"),
    )
    (
        grad_query_weight,
        grad_query_bias,
        grad_key_weight,
        grad_value_weight,
        grad_value_bias,
        grad_out_weight,
        grad_up_weight,
        grad_up_bias,
        grad_down_weight,
    ) = (
        lax.psum(grad_query_weight.astype(jnp.bfloat16), "dp").astype(jnp.float32),
        lax.psum(grad_query_bias.astype(jnp.bfloat16), "dp").astype(jnp.float32),
        lax.psum(grad_key_weight.astype(jnp.bfloat16), "dp").astype(jnp.float32),
        lax.psum(grad_value_weight.astype(jnp.bfloat16), "dp").astype(jnp.float32),
        lax.psum(grad_value_bias.astype(jnp.bfloat16), "dp").astype(jnp.float32),
        lax.psum(grad_out_weight.astype(jnp.bfloat16), "dp").astype(jnp.float32),
        lax.psum(grad_up_weight.astype(jnp.bfloat16), "dp").astype(jnp.float32),
        lax.psum(grad_up_bias.astype(jnp.bfloat16), "dp").astype(jnp.float32),
        lax.psum(grad_down_weight.astype(jnp.bfloat16), "dp").astype(jnp.float32),
    )
    return (
        result.astype(jnp.bfloat16),
        input_grad,
        grad_query_weight,
        grad_query_bias,
        grad_key_weight,
        grad_value_weight,
        grad_value_bias,
        grad_out_weight,
        grad_out_bias,
        grad_first_gain,
        grad_first_shift,
        grad_up_weight,
        grad_up_bias,
        grad_down_weight,
        grad_down_bias,
        grad_second_gain,
        grad_second_shift,
    )


def swap(rows):
    return lax.ppermute(rows, "mp", [(0, 1), (1, 0)])


def normal_parts(pre):
    size = jnp.abs(pre) * (0.5**0.5)
    t = 1.0 / (1.0 + 0.3275911 * size)
    bell = jnp.exp(-size * size)
    series = t * (
        0.254829592
        + t * (-0.284496736 + t * (1.421413741 + t * (-1.453152027 + t * 1.061405429)))
    )
    tail = 0.5 * series * bell
    return jnp.where(pre < 0, tail, 1.0 - tail), pre * bell * 0.3989422804014327


def gelu_parts(pre):
    cumulative, slope = normal_parts(pre)
    return (pre * cumulative).astype(jnp.bfloat16), (cumulative + slope).astype(jnp.bfloat16)


def blank(shapes):
    return pl.pallas_call(
        lambda *refs: None,
        out_specs=[pl.BlockSpec(memory_space=pl.ANY)] * len(shapes),
        out_shape=[jax.ShapeDtypeStruct(*shape) for shape in shapes],
        name="blank",
    )()


def mean_of(rows):
    return jnp.mean(rows, axis=-1, keepdims=True)


def column_sums(rows):
    return jnp.sum(rows, axis=0, keepdims=True)


def pack_kernel(place_ref, up_ref, down_ref, out_ref):
    rows = up_ref.shape[0]
    half = down_ref.shape[2]
    out_ref[:rows, :] = up_ref[...]
    out_ref[rows:, :half] = down_ref[0]
    out_ref[rows:, half:] = down_ref[1]


def pack_weights(place, count, up_weight, down_weight):
    depth, units = up_weight.shape
    rows = depth // count
    return pl.pallas_call(
        pack_kernel,
        grid_spec=pltpu.PrefetchScalarGridSpec(
            num_scalar_prefetch=1,
            grid=(1,),
            in_specs=[
                pl.BlockSpec((rows, units), lambda i, at: (at[0], 0)),
                pl.BlockSpec((2, rows, depth), lambda i, at: (0, at[0], 0)),
            ],
            out_specs=pl.BlockSpec((2 * rows, units), lambda i, at: (0, 0)),
        ),
        out_shape=jax.ShapeDtypeStruct((2 * rows, units), up_weight.dtype),
        name="pack_weights",
        cost_estimate=work(rows * units * 4096),
    )(place, up_weight, down_weight.reshape(2, units // 2, depth))


BIG = 56 * 1024 * 1024


def middle_kernel(own_ref, here_ref, w_own_ref, w_other_ref, bias_ref, tokens_ref, gain_ref,
                  shift_ref, hidden_ref, low_ref, normal_ref, inverse_ref):
    middle = (
        dot_nn(own_ref[...], w_own_ref[...])
        + dot_nn(here_ref[...], w_other_ref[...])
        + bias_ref[...]
        + tokens_ref[...].astype(jnp.float32)
    )
    center = middle - mean_of(middle)
    inverse = lax.rsqrt(mean_of(center * center) + epsilon)
    normal = center * inverse
    hidden = normal * gain_ref[...] + shift_ref[...]
    hidden_ref[...] = hidden
    low_ref[...] = hidden.astype(jnp.bfloat16)
    normal_ref[...] = normal
    inverse_ref[...] = inverse


def middle_norm(context_own, context_here, out_weight, out_other, bias, tokens, gain, shift,
                block=256):
    rows, depth = tokens.shape
    heads = context_own.shape[1]
    part = lambda width: pl.BlockSpec((block, width), lambda i: (i, 0))
    whole = lambda shape: pl.BlockSpec(shape, lambda i: (0, 0))
    return pl.pallas_call(
        middle_kernel,
        grid=(rows // block,),
        in_specs=[part(heads), part(heads), whole((heads, depth)), whole((heads, depth)),
                  whole((1, depth)), part(depth), whole((1, depth)), whole((1, depth))],
        out_specs=[part(depth), part(depth), part(depth), part(1)],
        out_shape=[
            jax.ShapeDtypeStruct((rows, depth), jnp.float32),
            jax.ShapeDtypeStruct((rows, depth), jnp.bfloat16),
            jax.ShapeDtypeStruct((rows, depth), jnp.float32),
            jax.ShapeDtypeStruct((rows, 1), jnp.float32),
        ],
        compiler_params=pltpu.CompilerParams(vmem_limit_bytes=BIG),
        name="middle_norm",
        cost_estimate=work(8 * rows * depth * heads),
    )(context_own, context_here, out_weight, out_other, bias, tokens, gain, shift)


UNITS = 512
PIECE = 512
STRIP = 64


def gelu_block(h_ref, up, bias_ref, act_ref, slope_ref, pre_scr):
    pre_scr[...] = dot_nn(h_ref[...], up)
    bias = bias_ref[...]
    for at in range(0, pre_scr.shape[0], STRIP):
        rows = slice(at, at + STRIP)
        act, slope = gelu_parts(pre_scr[rows, :] + bias)
        act_ref[rows, :] = act
        slope_ref[rows, :] = slope


def forward_own_kernel(h_ref, up_ref, bias_ref, down_ref, act_ref, slope_ref, base_ref, pre_scr):
    step = pl.program_id(0)

    @pl.when(step == 0)
    def _():
        base_ref[...] = jnp.zeros_like(base_ref)

    gelu_block(h_ref, up_ref[...], bias_ref, act_ref, slope_ref, pre_scr)
    base_ref[...] += dot_nn(act_ref[...], down_ref[...])


def forward_own(hidden, up_weight, up_bias, down_weight):
    rows, depth = hidden.shape
    units = up_weight.shape[1]
    return pl.pallas_call(
        forward_own_kernel,
        grid=(units // UNITS,),
        in_specs=[
            pl.BlockSpec((rows, depth), lambda j: (0, 0)),
            pl.BlockSpec((depth, UNITS), lambda j: (0, j)),
            pl.BlockSpec((1, UNITS), lambda j: (0, j)),
            pl.BlockSpec((UNITS, depth), lambda j: (j, 0)),
        ],
        out_specs=[
            pl.BlockSpec((rows, UNITS), lambda j: (0, j)),
            pl.BlockSpec((rows, UNITS), lambda j: (0, j)),
            pl.BlockSpec((rows, depth), lambda j: (0, 0)),
        ],
        out_shape=[
            jax.ShapeDtypeStruct((rows, units), jnp.bfloat16),
            jax.ShapeDtypeStruct((rows, units), jnp.bfloat16),
            jax.ShapeDtypeStruct((rows, depth), jnp.float32),
        ],
        scratch_shapes=[pltpu.VMEM((rows, UNITS), jnp.float32)],
        compiler_params=pltpu.CompilerParams(vmem_limit_bytes=BIG),
        name="forward_own",
        cost_estimate=work(6 * rows * depth * units),
    )(hidden, up_weight, up_bias, down_weight)


def packed_specs(packs, at):
    count, _, features, _ = packs.shape
    groups = UNITS // features
    split = count // groups
    depth = count * features
    up = pl.BlockSpec((count, 1, features, UNITS), lambda j: (0, 0, 0, at(j)))
    down = pl.BlockSpec(
        (groups, 1, features, depth), lambda j: (at(j) % split, 1, 0, at(j) // split)
    )
    return up, down


def flat(ref):
    count, _, features, width = ref.shape
    return ref[...].reshape(count * features, width)


def forward_other_kernel(h_ref, up_ref, bias_ref, down_ref, base_ref, hidden_ref, down_bias_ref,
                         outer_ref, valid_ref, gain_ref, shift_ref,
                         slope_ref, out_ref, d_ref, low_ref, sums_ref, total, act_scr, pre_scr):
    step = pl.program_id(0)

    @pl.when(step == 0)
    def _():
        total[...] = base_ref[...]

    gelu_block(h_ref, flat(up_ref), bias_ref, act_scr, slope_ref, pre_scr)
    total[...] += dot_nn(act_scr[...], flat(down_ref))

    @pl.when(step == pl.num_programs(0) - 1)
    def _():
        gain = gain_ref[...]
        for_gain = for_shift = for_bias = 0.0
        for at in range(0, h_ref.shape[0], 256):
            rows = slice(at, at + 256)
            final = total[rows, :] + down_bias_ref[...] + hidden_ref[rows, :]
            center = final - mean_of(final)
            inverse = lax.rsqrt(mean_of(center * center) + epsilon)
            normal = center * inverse
            out_ref[rows, :] = (normal * gain + shift_ref[...]).astype(jnp.bfloat16)
            upstream = outer_ref[rows, :].astype(jnp.float32) * valid_ref[rows, :]
            scaled = upstream * gain
            back = (scaled - mean_of(scaled) - normal * mean_of(scaled * normal)) * inverse
            d_ref[rows, :] = back
            low_ref[rows, :] = back.astype(jnp.bfloat16)
            for_gain += column_sums(upstream * normal)
            for_shift += column_sums(upstream)
            for_bias += column_sums(back)
        sums_ref[...] = jnp.zeros_like(sums_ref)
        sums_ref[0:1, :] = for_gain
        sums_ref[1:2, :] = for_shift
        sums_ref[2:3, :] = for_bias


def forward_other(hidden_low, packs, bias, base, hidden, down_bias, outer, valid, gain, shift,
                  at, of, earlier):
    whole_rows, depth = hidden_low.shape
    rows = whole_rows // of
    units = packs.shape[3]
    up, down = packed_specs(packs, lambda j: j)
    whole = lambda shape: pl.BlockSpec(shape, lambda j: (0, 0))
    part = lambda width: pl.BlockSpec((rows, width), lambda j: (at, 0))
    body = forward_other_kernel
    if earlier:
        body = lambda *refs: forward_other_kernel(*refs[:11], *refs[14:])
    return pl.pallas_call(
        body,
        grid=(units // UNITS,),
        in_specs=[
            part(depth), up, pl.BlockSpec((1, UNITS), lambda j: (0, j)), down,
            part(depth), part(depth), whole((1, depth)), part(depth),
            part(1), whole((1, depth)), whole((1, depth)),
        ]
        + [pl.BlockSpec(memory_space=pl.ANY)] * len(earlier),
        out_specs=[
            pl.BlockSpec((rows, UNITS), lambda j: (at, j)),
            part(depth), part(depth), whole((rows, depth)), whole((8, depth)),
        ],
        out_shape=[
            jax.ShapeDtypeStruct((whole_rows, units), jnp.bfloat16),
            jax.ShapeDtypeStruct((whole_rows, depth), jnp.bfloat16),
            jax.ShapeDtypeStruct((whole_rows, depth), jnp.float32),
            jax.ShapeDtypeStruct((rows, depth), jnp.bfloat16),
            jax.ShapeDtypeStruct((8, depth), jnp.float32),
        ],
        scratch_shapes=[
            pltpu.VMEM((rows, depth), jnp.float32), pltpu.VMEM((rows, UNITS), jnp.bfloat16),
            pltpu.VMEM((rows, UNITS), jnp.float32),
        ],
        input_output_aliases={11 + index: index for index in range(len(earlier))},
        compiler_params=pltpu.CompilerParams(vmem_limit_bytes=BIG),
        name="forward_other",
        cost_estimate=work(8 * rows * depth * units),
    )(hidden_low, packs, bias, packs, base, hidden, down_bias, outer, valid, gain, shift,
      *earlier)


def backward_rows_kernel(half, f_ref, slope_own_ref, slope_other_ref, up_ref, down_ref,
                         up_pack_ref, down_pack_ref, d_ref, normal_ref, inverse_ref, gain_ref,
                         d_pre_ref, middle_ref, low_ref, sums_ref, total):
    step = pl.program_id(0)

    def block(up, down, slope_ref, keep):
        for at in range(0, f_ref.shape[0], PIECE):
            rows = slice(at, at + PIECE)
            d_pre = (dot_nt(f_ref[rows, :], down) * slope_ref[rows, :]).astype(jnp.bfloat16)
            if keep:
                d_pre_ref[rows, :] = d_pre
            total[rows, :] += dot_nt(d_pre, up)

    @pl.when(step == 0)
    def _():
        total[...] = d_ref[...]

    @pl.when(step < half)
    def _():
        block(up_ref[...], down_ref[...], slope_own_ref, True)

    @pl.when(step >= half)
    def _():
        block(flat(up_pack_ref), flat(down_pack_ref), slope_other_ref, False)

    @pl.when(step == pl.num_programs(0) - 1)
    def _():
        gain = gain_ref[...]
        for_gain = for_shift = for_bias = 0.0
        for at in range(0, f_ref.shape[0], PIECE):
            rows = slice(at, at + PIECE)
            upstream = total[rows, :]
            normal = normal_ref[rows, :]
            scaled = upstream * gain
            back = (
                scaled - mean_of(scaled) - normal * mean_of(scaled * normal)
            ) * inverse_ref[rows, :]
            middle_ref[rows, :] = back
            low_ref[rows, :] = back.astype(jnp.bfloat16)
            for_gain += column_sums(upstream * normal)
            for_shift += column_sums(upstream)
            for_bias += column_sums(back)
        sums_ref[...] = jnp.zeros_like(sums_ref)
        sums_ref[0:1, :] = for_gain
        sums_ref[1:2, :] = for_shift
        sums_ref[2:3, :] = for_bias


def backward_rows(final_low, slope_own, slope_other, up_weight, down_weight, packs, d_final,
                  normal, inverse, gain):
    rows, depth = final_low.shape
    units = up_weight.shape[1]
    half = units // UNITS
    own = lambda j: jnp.minimum(j, half - 1)
    other = lambda j: jnp.maximum(j - half, 0)
    up, down = packed_specs(packs, other)
    whole = lambda shape: pl.BlockSpec(shape, lambda j: (0, 0))
    return pl.pallas_call(
        functools.partial(backward_rows_kernel, half),
        grid=(2 * half,),
        in_specs=[
            whole((rows, depth)),
            pl.BlockSpec((rows, UNITS), lambda j: (0, own(j))),
            pl.BlockSpec((rows, UNITS), lambda j: (0, other(j))),
            pl.BlockSpec((depth, UNITS), lambda j: (0, own(j))),
            pl.BlockSpec((UNITS, depth), lambda j: (own(j), 0)),
            up, down,
            whole((rows, depth)), whole((rows, depth)), whole((rows, 1)), whole((1, depth)),
        ],
        out_specs=[
            pl.BlockSpec((rows, UNITS), lambda j: (0, own(j))),
            whole((rows, depth)), whole((rows, depth)), whole((8, depth)),
        ],
        out_shape=[
            jax.ShapeDtypeStruct((rows, units), jnp.bfloat16),
            jax.ShapeDtypeStruct((rows, depth), jnp.float32),
            jax.ShapeDtypeStruct((rows, depth), jnp.bfloat16),
            jax.ShapeDtypeStruct((8, depth), jnp.float32),
        ],
        scratch_shapes=[pltpu.VMEM((rows, depth), jnp.float32)],
        compiler_params=pltpu.CompilerParams(vmem_limit_bytes=BIG),
        name="backward_rows",
        cost_estimate=work(10 * rows * depth * units),
    )(final_low, slope_own, slope_other, up_weight, down_weight, packs, packs, d_final, normal,
      inverse, gain)


def gelu_kernel(h_ref, up_ref, bias_ref, act_ref, slope_ref, pre_scr):
    gelu_block(h_ref, up_ref[...], bias_ref, act_ref, slope_ref, pre_scr)


def gelu_rows(hidden, up_weight, up_bias):
    rows, depth = hidden.shape
    units = up_weight.shape[1]
    return pl.pallas_call(
        gelu_kernel,
        grid=(units // UNITS,),
        in_specs=[
            pl.BlockSpec((rows, depth), lambda j: (0, 0)),
            pl.BlockSpec((depth, UNITS), lambda j: (0, j)),
            pl.BlockSpec((1, UNITS), lambda j: (0, j)),
        ],
        out_specs=[pl.BlockSpec((rows, UNITS), lambda j: (0, j))] * 2,
        out_shape=[jax.ShapeDtypeStruct((rows, units), jnp.bfloat16)] * 2,
        scratch_shapes=[pltpu.VMEM((rows, UNITS), jnp.float32)],
        compiler_params=pltpu.CompilerParams(vmem_limit_bytes=BIG),
        name="gelu_rows",
        cost_estimate=work(rows * depth),
    )(hidden, up_weight, up_bias)


def down_grad_kernel(count, own_ref, other_ref, *refs):
    grad_ref = refs[-1]
    total = None
    rows = own_ref.shape[0] // count
    for at in range(count):
        span = slice(at * rows, (at + 1) * rows)
        part = dot_tn(own_ref[span, :], refs[at][...]) + dot_tn(
            other_ref[span, :], refs[count + at][...]
        )
        total = part if total is None else total + part
    grad_ref[...] = total.astype(jnp.bfloat16)


def down_grad(act_own, act_other, final_own, final_other):
    rows, units = act_own.shape
    count = len(final_own)
    depth = final_own[0].shape[1]
    part = pl.BlockSpec((rows, UNITS), lambda j: (0, j))
    return pl.pallas_call(
        functools.partial(down_grad_kernel, count),
        grid=(units // UNITS,),
        in_specs=[part, part]
        + [pl.BlockSpec((rows // count, depth), lambda j: (0, 0))] * (2 * count),
        out_specs=pl.BlockSpec((UNITS, depth), lambda j: (j, 0)),
        out_shape=jax.ShapeDtypeStruct((units, depth), jnp.bfloat16),
        compiler_params=pltpu.CompilerParams(vmem_limit_bytes=BIG),
        name="down_grad",
        cost_estimate=work(4 * rows * depth * units),
    )(act_own, act_other, *final_own, *final_other)


def up_grad_kernel(f_ref, down_ref, slope_ref, d_pre_ref, h_own_ref, h_other_ref,
                   grad_ref, sums_ref, d_scr):
    for at in range(0, f_ref.shape[0], PIECE):
        rows = slice(at, at + PIECE)
        d_scr[rows, :] = (
            dot_nt(f_ref[rows, :], down_ref[...]) * slope_ref[rows, :]
        ).astype(jnp.bfloat16)
    grad_ref[...] = (
        dot_tn(h_own_ref[...], d_pre_ref[...]) + dot_tn(h_other_ref[...], d_scr[...])
    ).astype(jnp.bfloat16)
    sums_ref[...] = column_sums(d_pre_ref[...].astype(jnp.float32)) + column_sums(
        d_scr[...].astype(jnp.float32)
    )


def up_grad(final_other, down_weight, slope_other, d_pre_own, hidden_own, hidden_other):
    rows, depth = hidden_own.shape
    units = down_weight.shape[0]
    whole = lambda shape: pl.BlockSpec(shape, lambda j: (0, 0))
    part = pl.BlockSpec((rows, UNITS), lambda j: (0, j))
    return pl.pallas_call(
        up_grad_kernel,
        grid=(units // UNITS,),
        in_specs=[
            whole((rows, depth)),
            pl.BlockSpec((UNITS, depth), lambda j: (j, 0)),
            part, part,
            whole((rows, depth)), whole((rows, depth)),
        ],
        out_specs=[
            pl.BlockSpec((depth, UNITS), lambda j: (0, j)),
            pl.BlockSpec((1, UNITS), lambda j: (0, j)),
        ],
        out_shape=[
            jax.ShapeDtypeStruct((depth, units), jnp.bfloat16),
            jax.ShapeDtypeStruct((1, units), jnp.float32),
        ],
        scratch_shapes=[pltpu.VMEM((rows, UNITS), jnp.bfloat16)],
        compiler_params=pltpu.CompilerParams(vmem_limit_bytes=BIG),
        name="up_grad",
        cost_estimate=work(6 * rows * depth * units),
    )(final_other, down_weight, slope_other, d_pre_own, hidden_own, hidden_other)


def after(value, *earlier):
    return lax.optimization_barrier((value,) + earlier)[0]


def join_halves(kept, arrived):
    return (kept.astype(jnp.float32) + arrived.astype(jnp.float32)).astype(jnp.bfloat16)


class Chain:
    def __init__(self, item, swapped=False):
        self.count = lax.axis_size("dp")
        bits = list(range(self.count.bit_length() - 1))
        if swapped:
            bits[1:3] = bits[1:3][::-1]
        self.steps = [("fold", bit) for bit in bits] + [("spread", bit) for bit in reversed(bits)]
        self.held = item.astype(jnp.bfloat16)
        self.flying = None

    def end(self, *earlier):
        if self.flying is not None:
            kind, bit, kept, arrived = self.flying
            self.flying = None
            if earlier:
                arrived = after(arrived, *earlier)
            if kind == "fold":
                self.held = join_halves(kept, arrived)
            else:
                low = (lax.axis_index("dp") >> bit) & 1 == 0
                self.held = jnp.concatenate(
                    [jnp.where(low, kept, arrived), jnp.where(low, arrived, kept)]
                )

    def push(self, *earlier):
        self.end(*earlier)
        if self.steps:
            kind, bit = self.steps.pop(0)
            perm = [(at, at ^ (1 << bit)) for at in range(self.count)]
            kept = sent = self.held
            if kind == "fold":
                rows = self.held.shape[0] // 2
                place = (lax.axis_index("dp") >> bit) & 1
                kept = lax.dynamic_slice_in_dim(self.held, place * rows, rows, 0)
                sent = lax.dynamic_slice_in_dim(self.held, (1 - place) * rows, rows, 0)
            self.flying = kind, bit, kept, lax.ppermute(sent, "dp", perm)
        return self

    def gate(self, value):
        return after(value, self.held)

    def done(self):
        return not self.steps and self.flying is None


def body_pair(
    tokens,
    doc_lengths,
    cotangent,
    query_weight,
    query_bias,
    key_weight,
    value_weight,
    value_bias,
    out_weight,
    out_bias,
    first_gain,
    first_shift,
    up_weight,
    up_bias,
    down_weight,
    down_bias,
    second_gain,
    second_shift,
):
    own_rows = tokens.shape[0]
    length = 2 * own_rows
    doc_count = doc_lengths.shape[1]
    side = lax.axis_index("mp")
    first = side == 0
    f32 = jnp.float32
    bf16 = jnp.bfloat16

    def parts(rows, count=2):
        size = rows.shape[0] // count
        return [rows[at * size : (at + 1) * size] for at in range(count)]

    row = lambda vector: vector.astype(f32).reshape(1, -1)
    whole_segment = segment_ids(doc_lengths, length)[0]
    segment_own = lax.dynamic_slice_in_dim(whole_segment, side * own_rows, own_rows, 0)
    segment_other = lax.dynamic_slice_in_dim(whole_segment, (1 - side) * own_rows, own_rows, 0)
    segment = jnp.concatenate([segment_own, segment_other])
    valid = (segment_own < doc_count - 1).astype(f32)[:, None]

    place = lax.axis_index("dp")
    count = lax.axis_size("dp")
    pack = swap(pack_weights(place.reshape(1), count, up_weight, down_weight))
    packs = lax.all_gather(pack, "dp", axis=0)
    packs = packs.reshape(count, 2, pack.shape[0] // 2, pack.shape[1])
    bias_other = swap(up_bias)

    tokens_other = swap(after(tokens, pack))
    out_other = swap(after(out_weight, tokens_other))
    project = lambda rows: (
        (matmul(rows, query_weight) + query_bias).astype(bf16),
        matmul(rows, key_weight).astype(bf16),
        (matmul(rows, value_weight) + value_bias).astype(bf16),
    )
    fills = blank(
        [
            *[((length, query_weight.shape[1]), bf16)] * 3,
            ((own_rows, tokens.shape[1]), bf16),
            ((4 * up_weight.shape[0] // count, up_bias.size), bf16),
            (up_weight.shape, f32),
            (down_weight.shape, f32),
        ]
    )
    query_own, key_own, value_own = project(tokens)
    query_other, key_other, value_other = project(tokens_other)
    key_rows = jnp.concatenate([key_own, key_other])
    values = jnp.concatenate([value_own, value_other])
    context_away, mass_other = attention_forward(
        query_other, key_rows, values, segment_other, segment
    )
    context_here = swap(context_away)
    context_own, mass_own = attention_forward(
        query_own, key_rows, values, after(segment_own, context_away, out_other), segment
    )

    hidden, hidden_own, normal_first, inverse_first = middle_norm(
        context_own, context_here, out_weight, out_other, row(out_bias), tokens,
        row(first_gain), row(first_shift),
    )
    hidden_other = swap(hidden_own)

    act_own, slope_own, base = forward_own(hidden_own, up_weight, row(up_bias), down_weight)
    earlier, final_own, second_sums = (), [], 0.0
    for at in range(2):
        *earlier, low_rows, sums = forward_other(
            hidden_own, packs, row(bias_other), base, hidden, row(down_bias), cotangent, valid,
            row(second_gain), row(second_shift), at, 2, earlier,
        )
        final_own.append(low_rows)
        second_sums = second_sums + sums
    slope_local, output, d_final = earlier
    final_other = [swap(rows) for rows in final_own]
    act_other, slope_other = gelu_rows(
        after(hidden_other, *final_own, final_other[0]), up_weight, row(up_bias)
    )
    grad_down_weight = down_grad(act_own, act_other, final_own, final_other)
    down_sum = lax.psum(grad_down_weight, "dp")

    *final_own, grad_down_weight = lax.optimization_barrier((*final_own, grad_down_weight))
    final_rows = jnp.concatenate(final_own)
    final_away = jnp.concatenate(final_other)
    queries = jnp.concatenate([query_own, query_other])
    context = jnp.concatenate([context_own, context_away])
    mass = jnp.concatenate([mass_own, mass_other], axis=1)
    gathered = jnp.concatenate([tokens, tokens_other])
    weights = (query_weight, key_weight, value_weight)
    width = query_weight.shape[1]
    once = jnp.minimum(doc_lengths[0, 0], 1)

    def entering(rows):
        return functools.reduce(jnp.add, [matmul_nt(d, w) for d, w in zip(rows, weights)])

    def run(part, start):
        return lax.while_loop(
            lambda carry: carry[0] < once,
            lambda carry: (carry[0] + 1, part(carry[1])),
            (0, start),
        )[1]

    left = []

    def backward_part(carry):
        final_rows, d_final = carry[0][3], carry[3]
        d_pre_own, d_middle, middle_own, first_sums = backward_rows(
            final_rows, slope_own, slope_local, up_weight, down_weight, packs, d_final,
            normal_first, inverse_first, row(first_gain),
        )
        d_context_away = matmul_nt(middle_own, out_other).astype(bf16)
        d_context_other = swap(d_context_away)
        d_context_own = matmul_nt(middle_own, out_weight).astype(bf16)
        grad_up_weight, grad_up_bias = up_grad(
            after(final_away, d_context_away, d_context_own), down_weight, slope_other,
            d_pre_own, hidden_own, hidden_other,
        )
        d_context = jnp.concatenate([d_context_own, d_context_other])
        up_sum = Chain(grad_up_weight).push()
        partial_away = matmul_tn(after(context_here, grad_up_weight), middle_own).astype(bf16)
        partial_here = swap(partial_away)
        up_sum.push(partial_away)
        rows, up_sum.held = lax.optimization_barrier((d_context, up_sum.held))
        d_rows = attention_backward(
            queries, key_rows, values, rows, context, mass, segment, 0, 1
        )
        up_sum.end(*d_rows)
        left[:] = [up_sum.steps]
        d_rows, up_sum.held = lax.optimization_barrier((d_rows, up_sum.held))
        grads = [matmul_tn(gathered, d).astype(bf16) for d in d_rows]
        grad_out_weight = matmul_tn(after(context_own, d_rows[0]), middle_own)
        grads.append((grad_out_weight + partial_here.astype(f32)).astype(bf16))
        away = entering([parts(d)[1] for d in d_rows]).astype(bf16)
        own = entering([parts(d)[0] for d in d_rows]) + d_middle
        biases = [jnp.sum(d_rows[at], axis=0, dtype=f32) for at in (0, 2)]
        return grads, away, up_sum.held, own, biases, grad_up_bias, first_sums

    final_rows = after(final_rows, grad_down_weight)
    grads, away, held, own, biases, grad_up_bias, first_sums = run(
        backward_part,
        (
            [*fills[:3], final_rows], fills[3], fills[4], d_final,
            [jnp.zeros((width,), f32)] * 2, jnp.zeros((1, up_bias.size), f32),
            jnp.zeros_like(second_sums),
        ),
    )
    down_sum, grads = lax.optimization_barrier((down_sum, grads))
    *qkv, out_sum = lax.psum(tuple(grads), "dp")

    short = jnp.concatenate(
        [
            first_sums[:3].reshape(-1), second_sums[:3].reshape(-1), grad_up_bias.reshape(-1),
            *biases,
        ]
    )
    sizes = [tokens.shape[1]] * 6 + [up_bias.size, width, width]

    def last_part(carry):
        held, _, _, short, own = carry
        down_total = after(down_sum, short).astype(f32)
        up_sum = Chain(held)
        up_sum.steps = list(left[0])
        up_sum.push()
        back = swap(after(away, short))
        both = 6 * tokens.shape[1]
        shared = short[:both] + swap(short[:both])
        short = jnp.concatenate([shared, short[both:]])
        up_sum.push(short, down_total)
        for step in range(count.bit_length() - 1):
            short = short + lax.ppermute(
                short, "dp", [(at, at ^ (1 << step)) for at in range(count)]
            )
            up_sum.push(short)
        total_grad = own + back.astype(f32)
        while not up_sum.done():
            up_sum.push(total_grad)
        return held, up_sum.held.astype(f32), down_total, short, total_grad

    held = after(held, grads[0])
    _, up_total, down_total, small, input_grad = run(
        last_part, (held, fills[5], fills[6], short, own)
    )
    up_total, qkv, out_sum = lax.optimization_barrier((up_total, qkv, out_sum))
    pieces, at = [], 0
    for size in sizes:
        pieces.append(small[at : at + size])
        at += size
    return (
        output,
        input_grad,
        qkv[0].astype(f32),
        pieces[7],
        qkv[1].astype(f32),
        qkv[2].astype(f32),
        pieces[8],
        out_sum.astype(f32),
        pieces[2],
        pieces[0],
        pieces[1],
        up_total,
        pieces[6],
        down_total,
        pieces[5],
        pieces[3],
        pieces[4],
    )


def solution(mesh):
    in_specs = (
        P(("dp", "mp"), None),
        P("dp", None),
        P(("dp", "mp"), None),
        P(None, "mp"),
        P("mp"),
        P(None, "mp"),
        P(None, "mp"),
        P("mp"),
        P("mp", None),
        P(),
        P(),
        P(),
        P(None, "mp"),
        P("mp"),
        P("mp", None),
        P(),
        P(),
        P(),
    )
    out_specs = (
        P(("dp", "mp"), None),
        P(("dp", "mp"), None),
        P(None, "mp"),
        P("mp"),
        P(None, "mp"),
        P(None, "mp"),
        P("mp"),
        P("mp", None),
        P(),
        P(),
        P(),
        P(None, "mp"),
        P("mp"),
        P("mp", None),
        P(),
        P(),
        P(),
    )
    dp, mp = mesh.shape["dp"], mesh.shape["mp"]
    paired = mp == 2 and dp > 1 and dp & (dp - 1) == 0
    body = body_pair if paired else body_general
    return jax.shard_map(body, mesh=mesh, in_specs=in_specs, out_specs=out_specs, check_vma=False)
```

```python
import functools
import jax
import jax.numpy as jnp
from jax import lax
from jax.experimental import pallas as pl
from jax.experimental.pallas import tpu as pltpu
from jax.sharding import PartitionSpec as P

HEAD = 64
LANES = 128


epsilon = 1e-05
masked_score = -1000000000.0


def work(flops):
    return pl.CostEstimate(flops=flops, bytes_accessed=0, transcendentals=0)


def dot_nn(left, right):
    return lax.dot_general(left, right, (((1,), (0,)), ((), ())), preferred_element_type=jnp.float32)


def dot_nt(left, right):
    return lax.dot_general(left, right, (((1,), (1,)), ((), ())), preferred_element_type=jnp.float32)


def dot_tn(left, right):
    return lax.dot_general(left, right, (((0,), (0,)), ((), ())), preferred_element_type=jnp.float32)


def forward_kernel(pairs, q_ref, k_ref, v_ref, row_ref, col_ref, ctx_ref, lse_ref, bias_ref):
    bias_ref[...] = jnp.where(col_ref[...] == row_ref[...], 0.0, masked_score)
    rows = q_ref.shape[0]
    lane = lax.broadcasted_iota(jnp.int32, (rows, LANES), 1)
    stats = jnp.zeros((rows, LANES), jnp.float32)
    for pair in range(pairs):
        cols = slice(pair * LANES, (pair + 1) * LANES)
        q_pair = q_ref[:, cols] * jnp.bfloat16(HEAD ** (-0.5))
        k_pair = k_ref[:, cols]
        v_pair = v_ref[:, cols]
        halves = []
        for half in range(2):
            keep = (lane >= HEAD) == (half == 1)
            q_half = jnp.where(keep, q_pair, jnp.bfloat16(0))
            scores = dot_nt(q_half, k_pair) + bias_ref[...]
            row_max = jnp.max(scores, axis=-1, keepdims=True)
            exponent = jnp.exp(scores - row_max)
            row_sum = jnp.sum(exponent, axis=-1, keepdims=True)
            blended = dot_nn(exponent.astype(jnp.bfloat16), v_pair)
            halves.append(blended * (1.0 / row_sum))
            stats = jnp.where(lane == 2 * pair + half, row_max + jnp.log(row_sum), stats)
        ctx_ref[:, cols] = jnp.where(lane >= HEAD, halves[1], halves[0]).astype(ctx_ref.dtype)
    lse_ref[...] = jnp.transpose(stats)[: lse_ref.shape[0], :]


def attention_forward(queries, key_rows, values, row_segment, segment, block=512):
    rows, width = queries.shape
    length = key_rows.shape[0]
    pairs = width // LANES
    heads = width // HEAD
    whole = lambda shape: pl.BlockSpec(shape, lambda i: (0, 0))
    return pl.pallas_call(
        functools.partial(forward_kernel, pairs),
        grid=(rows // block,),
        in_specs=[
            pl.BlockSpec((block, width), lambda i: (i, 0)),
            whole((length, width)),
            whole((length, width)),
            whole((1, length)),
            pl.BlockSpec((block, 1), lambda i: (i, 0)),
        ],
        out_specs=[
            pl.BlockSpec((block, width), lambda i: (i, 0)),
            pl.BlockSpec((heads, block), lambda i: (0, i)),
        ],
        out_shape=[
            jax.ShapeDtypeStruct((rows, width), jnp.bfloat16),
            jax.ShapeDtypeStruct((heads, rows), jnp.float32),
        ],
        scratch_shapes=[pltpu.VMEM((block, length), jnp.float32)],
        compiler_params=pltpu.CompilerParams(vmem_limit_bytes=48 * 1024 * 1024),
        name="attention_forward",
        cost_estimate=work(2 * 8 * rows * length * width),
    )(queries, key_rows, values, segment.reshape(1, length), row_segment.reshape(rows, 1))


def backward_kernel(
    pairs, start, q_ref, k_ref, v_ref, g_ref, c_ref, lse_ref, row_ref, col_ref,
    out_q_ref, out_k_ref, out_v_ref, bias_ref, dk_sum, dv_sum,
):
    step = pl.program_id(0)
    bias_ref[...] = jnp.where(col_ref[...] == row_ref[...], 0.0, masked_score)
    rows = q_ref.shape[0]
    lane = lax.broadcasted_iota(jnp.int32, (rows, LANES), 1)
    key_lane = lax.broadcasted_iota(jnp.int32, (k_ref.shape[0], LANES), 1)
    inner = jnp.zeros((rows, LANES), jnp.float32)
    for pair in range(pairs):
        cols = slice(pair * LANES, (pair + 1) * LANES)
        both = g_ref[:, cols].astype(jnp.float32) * c_ref[:, cols].astype(jnp.float32)
        low = jnp.sum(jnp.where(lane < HEAD, both, 0.0), axis=-1, keepdims=True)
        high = jnp.sum(jnp.where(lane < HEAD, 0.0, both), axis=-1, keepdims=True)
        inner = jnp.where(lane == 2 * pair, low, jnp.where(lane == 2 * pair + 1, high, inner))
    inner = jnp.transpose(inner)

    @pl.when(step == 0)
    def _():
        dk_sum[...] = jnp.zeros_like(dk_sum)
        dv_sum[...] = jnp.zeros_like(dv_sum)

    for pair in range(pairs):
        cols = slice(pair * LANES, (pair + 1) * LANES)
        q_pair = q_ref[:, cols] * jnp.bfloat16(HEAD ** (-0.5))
        k_pair = k_ref[:, cols]
        v_pair = v_ref[:, cols]
        g_pair = g_ref[:, cols]
        dq = None
        for half in range(2):
            head = 2 * pair + half
            keep = (lane >= HEAD) == (half == 1)
            q_half = jnp.where(keep, q_pair, jnp.bfloat16(0))
            g_half = jnp.where(keep, g_pair, jnp.bfloat16(0))
            k_half = jnp.where((key_lane >= HEAD) == (half == 1), k_pair, jnp.bfloat16(0))
            mass = lse_ref[start + head : start + head + 1, :]
            probs = jnp.exp(dot_nt(k_pair, q_half) + bias_ref[...] - mass)
            d_probs = dot_nt(v_pair, g_half)
            d_scores = (probs * (d_probs - inner[head : head + 1, :])).astype(jnp.bfloat16)
            dv_sum[:, cols] += dot_nn(probs.astype(jnp.bfloat16), g_half)
            dk_sum[:, cols] += dot_nn(d_scores, q_half)
            part = dot_tn(d_scores, k_half)
            dq = part if dq is None else dq + part
        out_q_ref[:, cols] = (dq * HEAD ** (-0.5)).astype(out_q_ref.dtype)

    @pl.when(step == pl.num_programs(0) - 1)
    def _():
        out_k_ref[...] = dk_sum[...].astype(out_k_ref.dtype)
        out_v_ref[...] = dv_sum[...].astype(out_v_ref.dtype)


def attention_backward(
    queries, key_rows, values, d_context, context, lse, segment, at, of, block=512
):
    rows, width = queries.shape
    length = key_rows.shape[0]
    width = width // of
    pairs = width // LANES
    heads = lse.shape[0]
    part = pl.BlockSpec((block, width), lambda i: (i, at))
    keys = pl.BlockSpec((length, width), lambda i: (0, at))
    whole = pl.BlockSpec((length, width), lambda i: (0, 0))
    return pl.pallas_call(
        functools.partial(backward_kernel, pairs, at * (heads // of)),
        grid=(rows // block,),
        in_specs=[
            part, keys, keys, part, part,
            pl.BlockSpec((heads, block), lambda i: (0, i)),
            pl.BlockSpec((1, block), lambda i: (0, i)),
            pl.BlockSpec((length, 1), lambda i: (0, 0)),
        ],
        out_specs=[pl.BlockSpec((block, width), lambda i: (i, 0)), whole, whole],
        out_shape=[jax.ShapeDtypeStruct((rows, width), jnp.bfloat16)]
        + [jax.ShapeDtypeStruct((length, width), jnp.bfloat16)] * 2,
        scratch_shapes=[
            pltpu.VMEM((length, block), jnp.float32),
            pltpu.VMEM((length, width), jnp.float32),
            pltpu.VMEM((length, width), jnp.float32),
        ],
        compiler_params=pltpu.CompilerParams(vmem_limit_bytes=48 * 1024 * 1024),
        name="attention_backward",
        cost_estimate=work(2 * 4 * rows * length * width),
    )(queries, key_rows, values, d_context, context, lse,
      segment.reshape(1, rows), segment.reshape(length, 1))


def matmul(left, right):
    return jnp.dot(left, right, preferred_element_type=jnp.float32)


def matmul_tn(left, right):
    return lax.dot_general(
        left, right, (((0,), (0,)), ((), ())), preferred_element_type=jnp.float32
    )


def matmul_nt(left, right):
    return lax.dot_general(
        left, right, (((1,), (1,)), ((), ())), preferred_element_type=jnp.float32
    )


def layer_norm(inputs, gain, shift):
    center = inputs - jnp.mean(inputs, axis=-1, keepdims=True)
    spread = jnp.mean(center * center, axis=-1, keepdims=True)
    return center * lax.rsqrt(spread + epsilon) * gain + shift


def segment_ids(lengths, length):
    ends = jnp.cumsum(lengths, axis=-1)
    places = jnp.arange(length, dtype=jnp.int32)
    return jnp.sum((places[None, None, :] >= ends[:, :, None]).astype(jnp.int32), axis=1)


def score_block(q_block, s_block, key_rows, segment):
    raw = jnp.einsum(
        "qhd,khd->hqk", q_block, key_rows, preferred_element_type=jnp.float32
    ) * HEAD ** (-0.5)
    same = s_block[:, None] == segment[None, :]
    return jnp.where(same[None], raw, masked_score)


def body_general(
    tokens,
    doc_lengths,
    cotangent,
    query_weight,
    query_bias,
    key_weight,
    value_weight,
    value_bias,
    out_weight,
    out_bias,
    first_gain,
    first_shift,
    up_weight,
    up_bias,
    down_weight,
    down_bias,
    second_gain,
    second_shift,
):
    own_rows = tokens.shape[0]
    seq_count, doc_count = doc_lengths.shape
    all_rows = own_rows * lax.axis_size("mp")
    length = all_rows // seq_count
    head_count = query_weight.shape[1] // HEAD
    block_rows = min(512, length)
    block_count = length // block_rows
    score_scale = HEAD ** (-0.5)
    first_row = lax.axis_index("mp") * own_rows
    segment = segment_ids(doc_lengths, length)
    valid_all = (segment < doc_count - 1).reshape(all_rows)
    valid_rows = lax.dynamic_slice_in_dim(valid_all, first_row, own_rows, 0)
    shape_blocks = (seq_count, block_count, block_rows, head_count, HEAD)
    shape_seqs = (seq_count, length, head_count, HEAD)
    gain_first = first_gain.astype(jnp.float32)
    shift_first = first_shift.astype(jnp.float32)
    gathered = lax.all_gather(tokens, "mp", axis=0, tiled=True)
    queries = (matmul(gathered, query_weight) + query_bias).astype(jnp.bfloat16)
    key_rows = matmul(gathered, key_weight).astype(jnp.bfloat16)
    values = (matmul(gathered, value_weight) + value_bias).astype(jnp.bfloat16)

    def attend_sequence(members):
        q_seq, k_seq, v_seq, s_seq = members

        def attend_block(pieces):
            q_block, s_block = pieces
            scores = score_block(q_block, s_block, k_seq, s_seq)
            row_max = jnp.max(scores, axis=-1, keepdims=True)
            exponent = jnp.exp(scores - row_max)
            row_sum = jnp.sum(exponent, axis=-1, keepdims=True)
            attn_probs = (exponent / row_sum).astype(jnp.bfloat16)
            blended = jnp.einsum(
                "hqk,khd->qhd", attn_probs, v_seq, preferred_element_type=jnp.float32
            )
            return (blended.astype(jnp.bfloat16), (row_max + jnp.log(row_sum))[..., 0])

        return lax.map(attend_block, (q_seq, s_seq.reshape(block_count, block_rows)))

    context, log_mass = lax.map(
        attend_sequence,
        (
            queries.reshape(shape_blocks),
            key_rows.reshape(shape_seqs),
            values.reshape(shape_seqs),
            segment,
        ),
    )
    context = context.reshape(all_rows, head_count * HEAD)
    attn_part = lax.psum_scatter(matmul(context, out_weight), "mp", scatter_dimension=0, tiled=True)
    middle = attn_part + out_bias + tokens.astype(jnp.float32)
    hidden, norm_first = jax.vjp(layer_norm, middle, gain_first, shift_first)
    hidden_rows = lax.all_gather(hidden.astype(jnp.bfloat16), "mp", axis=0, tiled=True)
    pre = matmul(hidden_rows, up_weight) + up_bias
    act_exact, gelu_back = jax.vjp(lambda inputs: jax.nn.gelu(inputs, approximate=False), pre)
    act = act_exact.astype(jnp.bfloat16)
    ffn_part = lax.psum_scatter(matmul(act, down_weight), "mp", scatter_dimension=0, tiled=True)
    final = ffn_part + down_bias + hidden
    result, norm_second = jax.vjp(
        layer_norm, final, second_gain.astype(jnp.float32), second_shift.astype(jnp.float32)
    )
    upstream = cotangent.astype(jnp.float32) * valid_rows[:, None].astype(jnp.float32)
    d_final, grad_second_gain, grad_second_shift = norm_second(upstream)
    grad_down_bias = jnp.sum(d_final, axis=0)
    final_rows = lax.all_gather(d_final.astype(jnp.bfloat16), "mp", axis=0, tiled=True)
    grad_down_weight = matmul_tn(act, final_rows)
    d_pre = gelu_back(matmul_nt(final_rows, down_weight))[0].astype(jnp.bfloat16)
    grad_up_weight = matmul_tn(hidden_rows, d_pre)
    grad_up_bias = jnp.sum(d_pre, axis=0, dtype=jnp.float32)
    d_hidden = (
        lax.psum_scatter(matmul_nt(d_pre, up_weight), "mp", scatter_dimension=0, tiled=True)
        + d_final
    )
    d_middle, grad_first_gain, grad_first_shift = norm_first(d_hidden)
    grad_out_bias = jnp.sum(d_middle, axis=0)
    middle_rows = lax.all_gather(d_middle.astype(jnp.bfloat16), "mp", axis=0, tiled=True)
    grad_out_weight = matmul_tn(context, middle_rows)
    d_context = matmul_nt(middle_rows, out_weight).astype(jnp.bfloat16)

    def back_sequence(members):
        q_seq, k_seq, v_seq, s_seq, l_seq, g_seq = members

        def back_block(carried, pieces):
            grad_keys, grad_values = carried
            q_block, s_block, l_block, g_block = pieces
            scores = score_block(q_block, s_block, k_seq, s_seq)
            attn_probs = jnp.exp(scores - l_block[..., None])
            d_probs = jnp.einsum("qhd,khd->hqk", g_block, v_seq, preferred_element_type=jnp.float32)
            row_inner = jnp.sum(attn_probs * d_probs, axis=-1, keepdims=True)
            d_scores = (attn_probs * (d_probs - row_inner)).astype(jnp.bfloat16)
            d_block = (
                jnp.einsum("hqk,khd->qhd", d_scores, k_seq, preferred_element_type=jnp.float32)
                * score_scale
            )
            grad_keys = (
                grad_keys
                + jnp.einsum("hqk,qhd->khd", d_scores, q_block, preferred_element_type=jnp.float32)
                * score_scale
            )
            grad_values = grad_values + jnp.einsum(
                "hqk,qhd->khd",
                attn_probs.astype(jnp.bfloat16),
                g_block,
                preferred_element_type=jnp.float32,
            )
            return ((grad_keys, grad_values), d_block.astype(jnp.bfloat16))

        zero_grads = jnp.zeros((length, head_count, HEAD), jnp.float32)
        (grad_keys, grad_values), d_blocks = lax.scan(
            back_block,
            (zero_grads, zero_grads),
            (q_seq, s_seq.reshape(block_count, block_rows), l_seq, g_seq),
        )
        return (d_blocks, grad_keys.astype(jnp.bfloat16), grad_values.astype(jnp.bfloat16))

    d_queries, d_keys, d_values = lax.map(
        back_sequence,
        (
            queries.reshape(shape_blocks),
            key_rows.reshape(shape_seqs),
            values.reshape(shape_seqs),
            segment,
            log_mass,
            d_context.reshape(shape_blocks),
        ),
    )
    d_queries = d_queries.reshape(all_rows, head_count * HEAD)
    d_keys = d_keys.reshape(all_rows, head_count * HEAD)
    d_values = d_values.reshape(all_rows, head_count * HEAD)
    grad_query_weight = matmul_tn(gathered, d_queries)
    grad_key_weight = matmul_tn(gathered, d_keys)
    grad_value_weight = matmul_tn(gathered, d_values)
    grad_query_bias = jnp.sum(d_queries, axis=0, dtype=jnp.float32)
    grad_value_bias = jnp.sum(d_values, axis=0, dtype=jnp.float32)
    total_grad = matmul_nt(d_queries, query_weight)
    total_grad = total_grad + matmul_nt(d_keys, key_weight)
    input_grad = (
        lax.psum_scatter(
            (total_grad + matmul_nt(d_values, value_weight)).astype(jnp.bfloat16),
            "mp",
            scatter_dimension=0,
            tiled=True,
        ).astype(jnp.float32)
        + d_middle
    )
    (
        grad_out_bias,
        grad_first_gain,
        grad_first_shift,
        grad_down_bias,
        grad_second_gain,
        grad_second_shift,
    ) = lax.psum(
        (
            grad_out_bias,
            grad_first_gain,
            grad_first_shift,
            grad_down_bias,
            grad_second_gain,
            grad_second_shift,
        ),
        ("dp", "mp"),
    )
    (
        grad_query_weight,
        grad_query_bias,
        grad_key_weight,
        grad_value_weight,
        grad_value_bias,
        grad_out_weight,
        grad_up_weight,
        grad_up_bias,
        grad_down_weight,
    ) = (
        lax.psum(grad_query_weight.astype(jnp.bfloat16), "dp").astype(jnp.float32),
        lax.psum(grad_query_bias.astype(jnp.bfloat16), "dp").astype(jnp.float32),
        lax.psum(grad_key_weight.astype(jnp.bfloat16), "dp").astype(jnp.float32),
        lax.psum(grad_value_weight.astype(jnp.bfloat16), "dp").astype(jnp.float32),
        lax.psum(grad_value_bias.astype(jnp.bfloat16), "dp").astype(jnp.float32),
        lax.psum(grad_out_weight.astype(jnp.bfloat16), "dp").astype(jnp.float32),
        lax.psum(grad_up_weight.astype(jnp.bfloat16), "dp").astype(jnp.float32),
        lax.psum(grad_up_bias.astype(jnp.bfloat16), "dp").astype(jnp.float32),
        lax.psum(grad_down_weight.astype(jnp.bfloat16), "dp").astype(jnp.float32),
    )
    return (
        result.astype(jnp.bfloat16),
        input_grad,
        grad_query_weight,
        grad_query_bias,
        grad_key_weight,
        grad_value_weight,
        grad_value_bias,
        grad_out_weight,
        grad_out_bias,
        grad_first_gain,
        grad_first_shift,
        grad_up_weight,
        grad_up_bias,
        grad_down_weight,
        grad_down_bias,
        grad_second_gain,
        grad_second_shift,
    )


def swap(rows):
    return lax.ppermute(rows, "mp", [(0, 1), (1, 0)])


def normal_parts(pre):
    size = jnp.abs(pre) * (0.5**0.5)
    t = 1.0 / (1.0 + 0.3275911 * size)
    bell = jnp.exp(-size * size)
    series = t * (
        0.254829592
        + t * (-0.284496736 + t * (1.421413741 + t * (-1.453152027 + t * 1.061405429)))
    )
    tail = 0.5 * series * bell
    return jnp.where(pre < 0, tail, 1.0 - tail), pre * bell * 0.3989422804014327


def gelu_parts(pre):
    cumulative, slope = normal_parts(pre)
    return (pre * cumulative).astype(jnp.bfloat16), (cumulative + slope).astype(jnp.bfloat16)


def blank(shapes):
    return pl.pallas_call(
        lambda *refs: None,
        out_specs=[pl.BlockSpec(memory_space=pl.ANY)] * len(shapes),
        out_shape=[jax.ShapeDtypeStruct(*shape) for shape in shapes],
        name="blank",
    )()


def mean_of(rows):
    return jnp.mean(rows, axis=-1, keepdims=True)


def column_sums(rows):
    return jnp.sum(rows, axis=0, keepdims=True)


def pack_kernel(place_ref, up_ref, down_ref, out_ref):
    rows = up_ref.shape[0]
    half = down_ref.shape[2]
    out_ref[:rows, :] = up_ref[...]
    out_ref[rows:, :half] = down_ref[0]
    out_ref[rows:, half:] = down_ref[1]


def pack_weights(place, count, up_weight, down_weight):
    depth, units = up_weight.shape
    rows = depth // count
    return pl.pallas_call(
        pack_kernel,
        grid_spec=pltpu.PrefetchScalarGridSpec(
            num_scalar_prefetch=1,
            grid=(1,),
            in_specs=[
                pl.BlockSpec((rows, units), lambda i, at: (at[0], 0)),
                pl.BlockSpec((2, rows, depth), lambda i, at: (0, at[0], 0)),
            ],
            out_specs=pl.BlockSpec((2 * rows, units), lambda i, at: (0, 0)),
        ),
        out_shape=jax.ShapeDtypeStruct((2 * rows, units), up_weight.dtype),
        name="pack_weights",
        cost_estimate=work(rows * units * 4096),
    )(place, up_weight, down_weight.reshape(2, units // 2, depth))


BIG = 56 * 1024 * 1024


def middle_kernel(own_ref, here_ref, w_own_ref, w_other_ref, bias_ref, tokens_ref, gain_ref,
                  shift_ref, hidden_ref, low_ref, normal_ref, inverse_ref):
    middle = (
        dot_nn(own_ref[...], w_own_ref[...])
        + dot_nn(here_ref[...], w_other_ref[...])
        + bias_ref[...]
        + tokens_ref[...].astype(jnp.float32)
    )
    center = middle - mean_of(middle)
    inverse = lax.rsqrt(mean_of(center * center) + epsilon)
    normal = center * inverse
    hidden = normal * gain_ref[...] + shift_ref[...]
    hidden_ref[...] = hidden
    low_ref[...] = hidden.astype(jnp.bfloat16)
    normal_ref[...] = normal
    inverse_ref[...] = inverse


def middle_norm(context_own, context_here, out_weight, out_other, bias, tokens, gain, shift,
                block=256):
    rows, depth = tokens.shape
    heads = context_own.shape[1]
    part = lambda width: pl.BlockSpec((block, width), lambda i: (i, 0))
    whole = lambda shape: pl.BlockSpec(shape, lambda i: (0, 0))
    return pl.pallas_call(
        middle_kernel,
        grid=(rows // block,),
        in_specs=[part(heads), part(heads), whole((heads, depth)), whole((heads, depth)),
                  whole((1, depth)), part(depth), whole((1, depth)), whole((1, depth))],
        out_specs=[part(depth), part(depth), part(depth), part(1)],
        out_shape=[
            jax.ShapeDtypeStruct((rows, depth), jnp.float32),
            jax.ShapeDtypeStruct((rows, depth), jnp.bfloat16),
            jax.ShapeDtypeStruct((rows, depth), jnp.float32),
            jax.ShapeDtypeStruct((rows, 1), jnp.float32),
        ],
        compiler_params=pltpu.CompilerParams(vmem_limit_bytes=BIG),
        name="middle_norm",
        cost_estimate=work(8 * rows * depth * heads),
    )(context_own, context_here, out_weight, out_other, bias, tokens, gain, shift)


UNITS = 512
PIECE = 512
STRIP = 64


def gelu_block(h_ref, up, bias_ref, act_ref, slope_ref, pre_scr):
    pre_scr[...] = dot_nn(h_ref[...], up)
    bias = bias_ref[...]
    for at in range(0, pre_scr.shape[0], STRIP):
        rows = slice(at, at + STRIP)
        act, slope = gelu_parts(pre_scr[rows, :] + bias)
        act_ref[rows, :] = act
        slope_ref[rows, :] = slope


def forward_own_kernel(h_ref, up_ref, bias_ref, down_ref, act_ref, slope_ref, base_ref, pre_scr):
    step = pl.program_id(0)

    @pl.when(step == 0)
    def _():
        base_ref[...] = jnp.zeros_like(base_ref)

    gelu_block(h_ref, up_ref[...], bias_ref, act_ref, slope_ref, pre_scr)
    base_ref[...] += dot_nn(act_ref[...], down_ref[...])


def forward_own(hidden, up_weight, up_bias, down_weight):
    rows, depth = hidden.shape
    units = up_weight.shape[1]
    return pl.pallas_call(
        forward_own_kernel,
        grid=(units // UNITS,),
        in_specs=[
            pl.BlockSpec((rows, depth), lambda j: (0, 0)),
            pl.BlockSpec((depth, UNITS), lambda j: (0, j)),
            pl.BlockSpec((1, UNITS), lambda j: (0, j)),
            pl.BlockSpec((UNITS, depth), lambda j: (j, 0)),
        ],
        out_specs=[
            pl.BlockSpec((rows, UNITS), lambda j: (0, j)),
            pl.BlockSpec((rows, UNITS), lambda j: (0, j)),
            pl.BlockSpec((rows, depth), lambda j: (0, 0)),
        ],
        out_shape=[
            jax.ShapeDtypeStruct((rows, units), jnp.bfloat16),
            jax.ShapeDtypeStruct((rows, units), jnp.bfloat16),
            jax.ShapeDtypeStruct((rows, depth), jnp.float32),
        ],
        scratch_shapes=[pltpu.VMEM((rows, UNITS), jnp.float32)],
        compiler_params=pltpu.CompilerParams(vmem_limit_bytes=BIG),
        name="forward_own",
        cost_estimate=work(6 * rows * depth * units),
    )(hidden, up_weight, up_bias, down_weight)


def packed_specs(packs, at):
    count, _, features, _ = packs.shape
    groups = UNITS // features
    split = count // groups
    depth = count * features
    up = pl.BlockSpec((count, 1, features, UNITS), lambda j: (0, 0, 0, at(j)))
    down = pl.BlockSpec(
        (groups, 1, features, depth), lambda j: (at(j) % split, 1, 0, at(j) // split)
    )
    return up, down


def flat(ref):
    count, _, features, width = ref.shape
    return ref[...].reshape(count * features, width)


def forward_other_kernel(h_ref, up_ref, bias_ref, down_ref, base_ref, hidden_ref, down_bias_ref,
                         outer_ref, valid_ref, gain_ref, shift_ref,
                         slope_ref, out_ref, d_ref, low_ref, sums_ref, total, act_scr, pre_scr):
    step = pl.program_id(0)

    @pl.when(step == 0)
    def _():
        total[...] = base_ref[...]

    gelu_block(h_ref, flat(up_ref), bias_ref, act_scr, slope_ref, pre_scr)
    total[...] += dot_nn(act_scr[...], flat(down_ref))

    @pl.when(step == pl.num_programs(0) - 1)
    def _():
        gain = gain_ref[...]
        for_gain = for_shift = for_bias = 0.0
        for at in range(0, h_ref.shape[0], 256):
            rows = slice(at, at + 256)
            final = total[rows, :] + down_bias_ref[...] + hidden_ref[rows, :]
            center = final - mean_of(final)
            inverse = lax.rsqrt(mean_of(center * center) + epsilon)
            normal = center * inverse
            out_ref[rows, :] = (normal * gain + shift_ref[...]).astype(jnp.bfloat16)
            upstream = outer_ref[rows, :].astype(jnp.float32) * valid_ref[rows, :]
            scaled = upstream * gain
            back = (scaled - mean_of(scaled) - normal * mean_of(scaled * normal)) * inverse
            d_ref[rows, :] = back
            low_ref[rows, :] = back.astype(jnp.bfloat16)
            for_gain += column_sums(upstream * normal)
            for_shift += column_sums(upstream)
            for_bias += column_sums(back)
        sums_ref[...] = jnp.zeros_like(sums_ref)
        sums_ref[0:1, :] = for_gain
        sums_ref[1:2, :] = for_shift
        sums_ref[2:3, :] = for_bias


def forward_other(hidden_low, packs, bias, base, hidden, down_bias, outer, valid, gain, shift,
                  at, of, earlier):
    whole_rows, depth = hidden_low.shape
    rows = whole_rows // of
    units = packs.shape[3]
    up, down = packed_specs(packs, lambda j: j)
    whole = lambda shape: pl.BlockSpec(shape, lambda j: (0, 0))
    part = lambda width: pl.BlockSpec((rows, width), lambda j: (at, 0))
    body = forward_other_kernel
    if earlier:
        body = lambda *refs: forward_other_kernel(*refs[:11], *refs[14:])
    return pl.pallas_call(
        body,
        grid=(units // UNITS,),
        in_specs=[
            part(depth), up, pl.BlockSpec((1, UNITS), lambda j: (0, j)), down,
            part(depth), part(depth), whole((1, depth)), part(depth),
            part(1), whole((1, depth)), whole((1, depth)),
        ]
        + [pl.BlockSpec(memory_space=pl.ANY)] * len(earlier),
        out_specs=[
            pl.BlockSpec((rows, UNITS), lambda j: (at, j)),
            part(depth), part(depth), whole((rows, depth)), whole((8, depth)),
        ],
        out_shape=[
            jax.ShapeDtypeStruct((whole_rows, units), jnp.bfloat16),
            jax.ShapeDtypeStruct((whole_rows, depth), jnp.bfloat16),
            jax.ShapeDtypeStruct((whole_rows, depth), jnp.float32),
            jax.ShapeDtypeStruct((rows, depth), jnp.bfloat16),
            jax.ShapeDtypeStruct((8, depth), jnp.float32),
        ],
        scratch_shapes=[
            pltpu.VMEM((rows, depth), jnp.float32), pltpu.VMEM((rows, UNITS), jnp.bfloat16),
            pltpu.VMEM((rows, UNITS), jnp.float32),
        ],
        input_output_aliases={11 + index: index for index in range(len(earlier))},
        compiler_params=pltpu.CompilerParams(vmem_limit_bytes=BIG),
        name="forward_other",
        cost_estimate=work(8 * rows * depth * units),
    )(hidden_low, packs, bias, packs, base, hidden, down_bias, outer, valid, gain, shift,
      *earlier)


def backward_rows_kernel(half, f_ref, slope_own_ref, slope_other_ref, up_ref, down_ref,
                         up_pack_ref, down_pack_ref, d_ref, normal_ref, inverse_ref, gain_ref,
                         d_pre_ref, middle_ref, low_ref, sums_ref, total):
    step = pl.program_id(0)

    def block(up, down, slope_ref, keep):
        for at in range(0, f_ref.shape[0], PIECE):
            rows = slice(at, at + PIECE)
            d_pre = (dot_nt(f_ref[rows, :], down) * slope_ref[rows, :]).astype(jnp.bfloat16)
            if keep:
                d_pre_ref[rows, :] = d_pre
            total[rows, :] += dot_nt(d_pre, up)

    @pl.when(step == 0)
    def _():
        total[...] = d_ref[...]

    @pl.when(step < half)
    def _():
        block(up_ref[...], down_ref[...], slope_own_ref, True)

    @pl.when(step >= half)
    def _():
        block(flat(up_pack_ref), flat(down_pack_ref), slope_other_ref, False)

    @pl.when(step == pl.num_programs(0) - 1)
    def _():
        gain = gain_ref[...]
        for_gain = for_shift = for_bias = 0.0
        for at in range(0, f_ref.shape[0], PIECE):
            rows = slice(at, at + PIECE)
            upstream = total[rows, :]
            normal = normal_ref[rows, :]
            scaled = upstream * gain
            back = (
                scaled - mean_of(scaled) - normal * mean_of(scaled * normal)
            ) * inverse_ref[rows, :]
            middle_ref[rows, :] = back
            low_ref[rows, :] = back.astype(jnp.bfloat16)
            for_gain += column_sums(upstream * normal)
            for_shift += column_sums(upstream)
            for_bias += column_sums(back)
        sums_ref[...] = jnp.zeros_like(sums_ref)
        sums_ref[0:1, :] = for_gain
        sums_ref[1:2, :] = for_shift
        sums_ref[2:3, :] = for_bias


def backward_rows(final_low, slope_own, slope_other, up_weight, down_weight, packs, d_final,
                  normal, inverse, gain):
    rows, depth = final_low.shape
    units = up_weight.shape[1]
    half = units // UNITS
    own = lambda j: jnp.minimum(j, half - 1)
    other = lambda j: jnp.maximum(j - half, 0)
    up, down = packed_specs(packs, other)
    whole = lambda shape: pl.BlockSpec(shape, lambda j: (0, 0))
    return pl.pallas_call(
        functools.partial(backward_rows_kernel, half),
        grid=(2 * half,),
        in_specs=[
            whole((rows, depth)),
            pl.BlockSpec((rows, UNITS), lambda j: (0, own(j))),
            pl.BlockSpec((rows, UNITS), lambda j: (0, other(j))),
            pl.BlockSpec((depth, UNITS), lambda j: (0, own(j))),
            pl.BlockSpec((UNITS, depth), lambda j: (own(j), 0)),
            up, down,
            whole((rows, depth)), whole((rows, depth)), whole((rows, 1)), whole((1, depth)),
        ],
        out_specs=[
            pl.BlockSpec((rows, UNITS), lambda j: (0, own(j))),
            whole((rows, depth)), whole((rows, depth)), whole((8, depth)),
        ],
        out_shape=[
            jax.ShapeDtypeStruct((rows, units), jnp.bfloat16),
            jax.ShapeDtypeStruct((rows, depth), jnp.float32),
            jax.ShapeDtypeStruct((rows, depth), jnp.bfloat16),
            jax.ShapeDtypeStruct((8, depth), jnp.float32),
        ],
        scratch_shapes=[pltpu.VMEM((rows, depth), jnp.float32)],
        compiler_params=pltpu.CompilerParams(vmem_limit_bytes=BIG),
        name="backward_rows",
        cost_estimate=work(10 * rows * depth * units),
    )(final_low, slope_own, slope_other, up_weight, down_weight, packs, packs, d_final, normal,
      inverse, gain)


def gelu_kernel(h_ref, up_ref, bias_ref, act_ref, slope_ref, pre_scr):
    gelu_block(h_ref, up_ref[...], bias_ref, act_ref, slope_ref, pre_scr)


def gelu_rows(hidden, up_weight, up_bias):
    rows, depth = hidden.shape
    units = up_weight.shape[1]
    return pl.pallas_call(
        gelu_kernel,
        grid=(units // UNITS,),
        in_specs=[
            pl.BlockSpec((rows, depth), lambda j: (0, 0)),
            pl.BlockSpec((depth, UNITS), lambda j: (0, j)),
            pl.BlockSpec((1, UNITS), lambda j: (0, j)),
        ],
        out_specs=[pl.BlockSpec((rows, UNITS), lambda j: (0, j))] * 2,
        out_shape=[jax.ShapeDtypeStruct((rows, units), jnp.bfloat16)] * 2,
        scratch_shapes=[pltpu.VMEM((rows, UNITS), jnp.float32)],
        compiler_params=pltpu.CompilerParams(vmem_limit_bytes=BIG),
        name="gelu_rows",
        cost_estimate=work(rows * depth),
    )(hidden, up_weight, up_bias)


def down_grad_kernel(count, own_ref, other_ref, *refs):
    grad_ref = refs[-1]
    total = None
    rows = own_ref.shape[0] // count
    for at in range(count):
        span = slice(at * rows, (at + 1) * rows)
        part = dot_tn(own_ref[span, :], refs[at][...]) + dot_tn(
            other_ref[span, :], refs[count + at][...]
        )
        total = part if total is None else total + part
    grad_ref[...] = total.astype(jnp.bfloat16)


def down_grad(act_own, act_other, final_own, final_other):
    rows, units = act_own.shape
    count = len(final_own)
    depth = final_own[0].shape[1]
    part = pl.BlockSpec((rows, UNITS), lambda j: (0, j))
    return pl.pallas_call(
        functools.partial(down_grad_kernel, count),
        grid=(units // UNITS,),
        in_specs=[part, part]
        + [pl.BlockSpec((rows // count, depth), lambda j: (0, 0))] * (2 * count),
        out_specs=pl.BlockSpec((UNITS, depth), lambda j: (j, 0)),
        out_shape=jax.ShapeDtypeStruct((units, depth), jnp.bfloat16),
        compiler_params=pltpu.CompilerParams(vmem_limit_bytes=BIG),
        name="down_grad",
        cost_estimate=work(4 * rows * depth * units),
    )(act_own, act_other, *final_own, *final_other)


def up_grad_kernel(f_ref, down_ref, slope_ref, d_pre_ref, h_own_ref, h_other_ref,
                   grad_ref, sums_ref, d_scr):
    for at in range(0, f_ref.shape[0], PIECE):
        rows = slice(at, at + PIECE)
        d_scr[rows, :] = (
            dot_nt(f_ref[rows, :], down_ref[...]) * slope_ref[rows, :]
        ).astype(jnp.bfloat16)
    grad_ref[...] = (
        dot_tn(h_own_ref[...], d_pre_ref[...]) + dot_tn(h_other_ref[...], d_scr[...])
    ).astype(jnp.bfloat16)
    sums_ref[...] = column_sums(d_pre_ref[...].astype(jnp.float32)) + column_sums(
        d_scr[...].astype(jnp.float32)
    )


def up_grad(final_other, down_weight, slope_other, d_pre_own, hidden_own, hidden_other):
    rows, depth = hidden_own.shape
    units = down_weight.shape[0]
    whole = lambda shape: pl.BlockSpec(shape, lambda j: (0, 0))
    part = pl.BlockSpec((rows, UNITS), lambda j: (0, j))
    return pl.pallas_call(
        up_grad_kernel,
        grid=(units // UNITS,),
        in_specs=[
            whole((rows, depth)),
            pl.BlockSpec((UNITS, depth), lambda j: (j, 0)),
            part, part,
            whole((rows, depth)), whole((rows, depth)),
        ],
        out_specs=[
            pl.BlockSpec((depth, UNITS), lambda j: (0, j)),
            pl.BlockSpec((1, UNITS), lambda j: (0, j)),
        ],
        out_shape=[
            jax.ShapeDtypeStruct((depth, units), jnp.bfloat16),
            jax.ShapeDtypeStruct((1, units), jnp.float32),
        ],
        scratch_shapes=[pltpu.VMEM((rows, UNITS), jnp.bfloat16)],
        compiler_params=pltpu.CompilerParams(vmem_limit_bytes=BIG),
        name="up_grad",
        cost_estimate=work(6 * rows * depth * units),
    )(final_other, down_weight, slope_other, d_pre_own, hidden_own, hidden_other)


def after(value, *earlier):
    return lax.optimization_barrier((value,) + earlier)[0]


def join_halves(kept, arrived):
    return (kept.astype(jnp.float32) + arrived.astype(jnp.float32)).astype(jnp.bfloat16)


class Chain:
    def __init__(self, item, swapped=False):
        self.count = lax.axis_size("dp")
        bits = list(range(self.count.bit_length() - 1))
        if swapped:
            bits[1:3] = bits[1:3][::-1]
        self.steps = [("fold", bit) for bit in bits] + [("spread", bit) for bit in reversed(bits)]
        self.held = item.astype(jnp.bfloat16)
        self.flying = None

    def end(self, *earlier):
        if self.flying is not None:
            kind, bit, kept, arrived = self.flying
            self.flying = None
            if earlier:
                arrived = after(arrived, *earlier)
            if kind == "fold":
                self.held = join_halves(kept, arrived)
            else:
                low = (lax.axis_index("dp") >> bit) & 1 == 0
                self.held = jnp.concatenate(
                    [jnp.where(low, kept, arrived), jnp.where(low, arrived, kept)]
                )

    def push(self, *earlier):
        self.end(*earlier)
        if self.steps:
            kind, bit = self.steps.pop(0)
            perm = [(at, at ^ (1 << bit)) for at in range(self.count)]
            kept = sent = self.held
            if kind == "fold":
                rows = self.held.shape[0] // 2
                place = (lax.axis_index("dp") >> bit) & 1
                kept = lax.dynamic_slice_in_dim(self.held, place * rows, rows, 0)
                sent = lax.dynamic_slice_in_dim(self.held, (1 - place) * rows, rows, 0)
            self.flying = kind, bit, kept, lax.ppermute(sent, "dp", perm)
        return self

    def gate(self, value):
        return after(value, self.held)

    def done(self):
        return not self.steps and self.flying is None


def body_pair(
    tokens,
    doc_lengths,
    cotangent,
    query_weight,
    query_bias,
    key_weight,
    value_weight,
    value_bias,
    out_weight,
    out_bias,
    first_gain,
    first_shift,
    up_weight,
    up_bias,
    down_weight,
    down_bias,
    second_gain,
    second_shift,
):
    own_rows = tokens.shape[0]
    length = 2 * own_rows
    doc_count = doc_lengths.shape[1]
    side = lax.axis_index("mp")
    first = side == 0
    f32 = jnp.float32
    bf16 = jnp.bfloat16

    def parts(rows, count=2):
        size = rows.shape[0] // count
        return [rows[at * size : (at + 1) * size] for at in range(count)]

    row = lambda vector: vector.astype(f32).reshape(1, -1)
    whole_segment = segment_ids(doc_lengths, length)[0]
    segment_own = lax.dynamic_slice_in_dim(whole_segment, side * own_rows, own_rows, 0)
    segment_other = lax.dynamic_slice_in_dim(whole_segment, (1 - side) * own_rows, own_rows, 0)
    segment = jnp.concatenate([segment_own, segment_other])
    valid = (segment_own < doc_count - 1).astype(f32)[:, None]

    place = lax.axis_index("dp")
    count = lax.axis_size("dp")
    pack = swap(pack_weights(place.reshape(1), count, up_weight, down_weight))
    packs = lax.all_gather(pack, "dp", axis=0)
    packs = packs.reshape(count, 2, pack.shape[0] // 2, pack.shape[1])
    bias_other = swap(up_bias)

    tokens_other = swap(after(tokens, pack))
    out_other = swap(after(out_weight, tokens_other))
    project = lambda rows: (
        (matmul(rows, query_weight) + query_bias).astype(bf16),
        matmul(rows, key_weight).astype(bf16),
        (matmul(rows, value_weight) + value_bias).astype(bf16),
    )
    fills = blank(
        [
            *[((length, query_weight.shape[1]), bf16)] * 3,
            ((own_rows, tokens.shape[1]), bf16),
            ((4 * up_weight.shape[0] // count, up_bias.size), bf16),
            (up_weight.shape, f32),
            (down_weight.shape, f32),
        ]
    )
    query_own, key_own, value_own = project(tokens)
    query_other, key_other, value_other = project(tokens_other)
    key_rows = jnp.concatenate([key_own, key_other])
    values = jnp.concatenate([value_own, value_other])
    context_away, mass_other = attention_forward(
        query_other, key_rows, values, segment_other, segment
    )
    context_here = swap(context_away)
    context_own, mass_own = attention_forward(
        query_own, key_rows, values, after(segment_own, context_away, out_other), segment
    )

    hidden, hidden_own, normal_first, inverse_first = middle_norm(
        context_own, context_here, out_weight, out_other, row(out_bias), tokens,
        row(first_gain), row(first_shift),
    )
    hidden_other = swap(hidden_own)

    act_own, slope_own, base = forward_own(hidden_own, up_weight, row(up_bias), down_weight)
    earlier, final_own, second_sums = (), [], 0.0
    for at in range(2):
        *earlier, low_rows, sums = forward_other(
            hidden_own, packs, row(bias_other), base, hidden, row(down_bias), cotangent, valid,
            row(second_gain), row(second_shift), at, 2, earlier,
        )
        final_own.append(low_rows)
        second_sums = second_sums + sums
    slope_local, output, d_final = earlier
    final_other = [swap(rows) for rows in final_own]
    act_other, slope_other = gelu_rows(
        after(hidden_other, *final_own, final_other[0]), up_weight, row(up_bias)
    )
    grad_down_weight = down_grad(act_own, act_other, final_own, final_other)
    down_sum = lax.psum(grad_down_weight, "dp")

    *final_own, grad_down_weight = lax.optimization_barrier((*final_own, grad_down_weight))
    final_rows = jnp.concatenate(final_own)
    final_away = jnp.concatenate(final_other)
    queries = jnp.concatenate([query_own, query_other])
    context = jnp.concatenate([context_own, context_away])
    mass = jnp.concatenate([mass_own, mass_other], axis=1)
    gathered = jnp.concatenate([tokens, tokens_other])
    weights = (query_weight, key_weight, value_weight)
    width = query_weight.shape[1]
    once = jnp.minimum(doc_lengths[0, 0], 1)

    def entering(rows):
        return functools.reduce(jnp.add, [matmul_nt(d, w) for d, w in zip(rows, weights)])

    def run(part, start):
        return lax.while_loop(
            lambda carry: carry[0] < once,
            lambda carry: (carry[0] + 1, part(carry[1])),
            (0, start),
        )[1]

    left = []

    def backward_part(carry):
        final_rows, d_final = carry[0][3], carry[3]
        d_pre_own, d_middle, middle_own, first_sums = backward_rows(
            final_rows, slope_own, slope_local, up_weight, down_weight, packs, d_final,
            normal_first, inverse_first, row(first_gain),
        )
        d_context_away = matmul_nt(middle_own, out_other).astype(bf16)
        d_context_other = swap(d_context_away)
        d_context_own = matmul_nt(middle_own, out_weight).astype(bf16)
        grad_up_weight, grad_up_bias = up_grad(
            after(final_away, d_context_away, d_context_own), down_weight, slope_other,
            d_pre_own, hidden_own, hidden_other,
        )
        d_context = jnp.concatenate([d_context_own, d_context_other])
        up_sum = Chain(grad_up_weight).push()
        partial_away = matmul_tn(after(context_here, grad_up_weight), middle_own).astype(bf16)
        partial_here = swap(partial_away)
        up_sum.push(partial_away)
        rows, up_sum.held = lax.optimization_barrier((d_context, up_sum.held))
        d_rows = attention_backward(
            queries, key_rows, values, rows, context, mass, segment, 0, 1
        )
        up_sum.end(*d_rows)
        left[:] = [up_sum.steps]
        d_rows, up_sum.held = lax.optimization_barrier((d_rows, up_sum.held))
        grads = [matmul_tn(gathered, d).astype(bf16) for d in d_rows]
        grad_out_weight = matmul_tn(after(context_own, d_rows[0]), middle_own)
        grads.append((grad_out_weight + partial_here.astype(f32)).astype(bf16))
        away = entering([parts(d)[1] for d in d_rows]).astype(bf16)
        own = entering([parts(d)[0] for d in d_rows]) + d_middle
        biases = [jnp.sum(d_rows[at], axis=0, dtype=f32) for at in (0, 2)]
        return grads, away, up_sum.held, own, biases, grad_up_bias, first_sums

    final_rows = after(final_rows, grad_down_weight)
    grads, away, held, own, biases, grad_up_bias, first_sums = run(
        backward_part,
        (
            [*fills[:3], final_rows], fills[3], fills[4], d_final,
            [jnp.zeros((width,), f32)] * 2, jnp.zeros((1, up_bias.size), f32),
            jnp.zeros_like(second_sums),
        ),
    )
    down_sum, grads = lax.optimization_barrier((down_sum, grads))
    *qkv, out_sum = lax.psum(tuple(grads), "dp")

    short = jnp.concatenate(
        [
            first_sums[:3].reshape(-1), second_sums[:3].reshape(-1), grad_up_bias.reshape(-1),
            *biases,
        ]
    )
    sizes = [tokens.shape[1]] * 6 + [up_bias.size, width, width]

    def last_part(carry):
        held, _, _, short, own = carry
        down_total = after(down_sum, short).astype(f32)
        up_sum = Chain(held)
        up_sum.steps = list(left[0])
        up_sum.push()
        back = swap(after(away, short))
        both = 6 * tokens.shape[1]
        shared = short[:both] + swap(short[:both])
        short = jnp.concatenate([shared, short[both:]])
        up_sum.push(short, down_total)
        for step in range(count.bit_length() - 1):
            short = short + lax.ppermute(
                short, "dp", [(at, at ^ (1 << step)) for at in range(count)]
            )
            up_sum.push(short)
        total_grad = own + back.astype(f32)
        while not up_sum.done():
            up_sum.push(total_grad)
        return held, up_sum.held.astype(f32), down_total, short, total_grad

    held = after(held, grads[0])
    _, up_total, down_total, small, input_grad = run(
        last_part, (held, fills[5], fills[6], short, own)
    )
    up_total, qkv, out_sum = lax.optimization_barrier((up_total, qkv, out_sum))
    pieces, at = [], 0
    for size in sizes:
        pieces.append(small[at : at + size])
        at += size
    return (
        output,
        input_grad,
        qkv[0].astype(f32),
        pieces[7],
        qkv[1].astype(f32),
        qkv[2].astype(f32),
        pieces[8],
        out_sum.astype(f32),
        pieces[2],
        pieces[0],
        pieces[1],
        up_total,
        pieces[6],
        down_total,
        pieces[5],
        pieces[3],
        pieces[4],
    )


def solution(mesh):
    in_specs = (
        P(("dp", "mp"), None),
        P("dp", None),
        P(("dp", "mp"), None),
        P(None, "mp"),
        P("mp"),
        P(None, "mp"),
        P(None, "mp"),
        P("mp"),
        P("mp", None),
        P(),
        P(),
        P(),
        P(None, "mp"),
        P("mp"),
        P("mp", None),
        P(),
        P(),
        P(),
    )
    out_specs = (
        P(("dp", "mp"), None),
        P(("dp", "mp"), None),
        P(None, "mp"),
        P("mp"),
        P(None, "mp"),
        P(None, "mp"),
        P("mp"),
        P("mp", None),
        P(),
        P(),
        P(),
        P(None, "mp"),
        P("mp"),
        P("mp", None),
        P(),
        P(),
        P(),
    )
    dp, mp = mesh.shape["dp"], mesh.shape["mp"]
    paired = mp == 2 and dp > 1 and dp & (dp - 1) == 0
    body = body_pair if paired else body_general
    return jax.shard_map(body, mesh=mesh, in_specs=in_specs, out_specs=out_specs, check_vma=False)
```
